32 devices in a mesh: expert: 8 (over z, x), wshard: 4 (over y, core).
Axes of the slice: x: 2, y: 2, z: 4, core: 2. Of those that a mesh axis runs over, the one named last changes fastest.
Arguments:
- images: bfloat16 [12608, 512], P(('expert', 'wshard')), may hold values from -6 to 6
- attn_in: bfloat16 [2, 512, 1536], P(None, 'wshard'), may hold values from -0.25 to 0.25
- attn_out: bfloat16 [2, 512, 512], P(None, 'wshard'), may hold values from -0.75 to 0.75
- norm_gains: bfloat16 [4, 512], P(None, 'wshard'), may hold values from 0.5 to 1.5
- mlp_in: bfloat16 [512, 2048], P('wshard'), may hold values from -0.25 to 0.25
- mlp_out: bfloat16 [2048, 512], P('wshard'), may hold values from -0.1875 to 0.1875
- router: bfloat16 [512, 8], P('wshard'), may hold values from -0.1875 to 0.1875
- expert_in: bfloat16 [8, 512, 2048], P('expert'), may hold values from -0.25 to 0.25
- expert_out: bfloat16 [8, 2048, 512], P('expert'), may hold values from -0.25 to 0.25
- expert_ids: int32 [12608, 2], P(('expert', 'wshard')), may hold values from 0 to 7, all different within a row; in each aligned block of 394 rows (0 to 393, 394 to 787, ...) at most 197 rows name the same one
- cotangent: bfloat16 [12608, 512], P(('expert', 'wshard')), may hold values from -6 to 6
Outputs:
- final: bfloat16 [12608, 512], P(('expert', 'wshard'))
- images_grad: float32 [12608, 512], P(('expert', 'wshard'))
- attn_in_grad: float32 [2, 512, 1536], P(None, 'wshard')
- attn_out_grad: float32 [2, 512, 512], P(None, 'wshard')
- norm_gains_grad: float32 [4, 512], P(None, 'wshard')
- mlp_in_grad: float32 [512, 2048], P('wshard')
- mlp_out_grad: float32 [2048, 512], P('wshard')
- router_grad: float32 [512, 8], P('wshard')
- expert_in_grad: float32 [8, 512, 2048], P('expert')
- expert_out_grad: float32 [8, 2048, 512], P('expert')
The draws below stay inside these ranges and needn't reach their ends.
Inputs may be any that keep to these rules, and one draw needn't show every extreme that they name: `expert_ids`: each token names 2 different experts. The rows of one device name no expert more than 197 times, and in some device's rows one expert is named exactly 197 times.
All inputs are finite; a program needn't handle non-finite values.
Results may differ from the reference program's by a relative error of at most 0.023.
Values may be sent and summed in bfloat16 or wider, within the bound.
No kernel may reach another device: no remote copies, remote signals or barrier semaphores. Data moves between devices by JAX's collectives and lax.ppermute only.
A program may use at most 192 MiB of HBM per device.

```python
import math
import jax
import jax.numpy as jnp
import numpy as np
from jax import lax

D = 512
HEADS = 8
FF = 2048
HEAD_DIM = 64
SEQ = 197
TOP = 2
IMGS_DEV = 2
EXPERTS = 8
TOK_DEV = 394
TOKENS = 12608
CAP = 197
N_EXPERT = 8
N_WSHARD = 4


def shard_levels(own_key, extent, cuts, least, largest):
    factor_of, own = 1.0, jax.random.fold_in(own_key, 6)
    for dim, shards_of in cuts:
        heights = jnp.exp(jax.random.uniform(jax.random.fold_in(own, dim), (shards_of,), jnp.float32, least / len(cuts), largest / len(cuts)))
        factor_of = factor_of * jnp.repeat(heights, extent[dim] // shards_of).reshape([-1 if axis == dim else 1 for axis in range(len(extent))])
    return factor_of


def deal_out(key, own, number, rows, number_of, top, bound, lean):
    order = jax.random.permutation(key, number_of)
    crowded, common = shares(number_of, rows * top, bound, lean, True), shares(number_of, rows * top, bound, lean, False)
    places = jnp.arange(number_of)

    def named(tallies, rotation):
        used = int((tallies > 0).sum())
        fixed = max(1, used // 4)
        passed = fixed + (places - fixed + rotation * (used - fixed)) % max(1, number_of - fixed)
        return jnp.zeros((number_of,), jnp.int32).at[order[jnp.where(places < fixed, places, passed)]].set(jnp.asarray(tallies, jnp.int32))

    tallies = jnp.where(number % 4 == 0, named(crowded, number // 4), named(common, number - number // 4 - 1))
    mixed = jax.random.permutation(jax.random.fold_in(own, 3), number_of)
    giver, taker = mixed[0:number_of // 2 * 2:2], mixed[1:number_of // 2 * 2:2]
    margin = jnp.minimum(tallies[giver] - 1, bound - tallies[taker]) // 2
    margin = jnp.where((giver == order[0]) | (taker == order[0]) | (tallies[taker] == 0), 0, jnp.maximum(margin, 0))
    passed = jax.random.randint(jax.random.fold_in(own, 4), (number_of // 2,), 0, 1 << 20) % (margin + 1)
    tallies = tallies.at[giver].add(-passed).at[taker].add(passed)
    items = jnp.searchsorted(jnp.cumsum(tallies), jnp.arange(rows * top), side="right").astype(jnp.int32)
    listing = items.reshape(top, rows).T
    listing = listing[jax.random.permutation(jax.random.fold_in(own, 1), rows)]
    rotation = jax.random.randint(jax.random.fold_in(own, 2), (rows, 1), 0, top)
    return jnp.take_along_axis(listing, (jnp.arange(top)[None, :] + rotation) % top, axis=1)


def shares(amount, total, bound, lean, full):
    weights = [(1 << 20) // math.isqrt(standing ** lean) + 1 for standing in range(1, amount + 1)]
    largest = bound if full else min(bound, max(-(-total // amount), total * weights[0] // sum(weights)))
    least = 1 if total - largest >= amount - 1 else 0
    counts, spare = [largest] + [least] * (amount - 1), total - largest - least * (amount - 1)
    while spare > 0:
        candidates = [i for i in range(1, amount) if counts[i] < largest] or [i for i in range(1, amount) if counts[i] < bound]
        mass, budget = sum([weights[i] for i in candidates]), spare
        for i in candidates:
            addition = min(bound - counts[i], max(1, budget * weights[i] // mass), spare)
            counts[i] = counts[i] + addition
            spare = spare - addition
    return np.array(counts)


def bell_draw(own_key, dims, scale, reach, split=(), kind=jnp.bfloat16):
    result = scale * jax.random.normal(own_key, dims, jnp.float32)
    if split:
        result = result * shard_levels(own_key, dims, split, -0.22, 0.18)
    return jnp.clip(result, -reach, reach).astype(kind)


def setup_inputs(seed: int = 0) -> dict:
    splits = jax.random.split(jax.random.key(seed), 12)
    images = bell_draw(splits[0], (TOKENS, D), 1.0, 6.0, ((0, 32),))
    attn_in = bell_draw(splits[1], (2, D, 3 * D), D ** -0.5, 0.25, ((1, 4),))
    attn_out = bell_draw(splits[2], (2, D, D), (D // 8) ** -0.5, 0.75, ((1, 4),))
    norm_gains = jnp.clip(1.0 + 0.1 * jax.random.normal(splits[3], (4, D), jnp.float32), 0.5, 1.5).astype(jnp.bfloat16)
    mlp_in = bell_draw(splits[4], (D, FF), D ** -0.5, 0.25, ((0, 4),))
    mlp_out = bell_draw(splits[5], (FF, D), (FF // 2) ** -0.5, 0.1875, ((0, 4),))
    router = bell_draw(splits[6], (D, EXPERTS), (2 * D) ** -0.5, 0.1875, ((0, 4),))
    expert_in = bell_draw(splits[7], (EXPERTS, D, FF), D ** -0.5, 0.25, ((0, 8),))
    expert_out = bell_draw(splits[8], (EXPERTS, FF, D), (FF // 4) ** -0.5, 0.25, ((0, 8),))
    expert_ids_keys = jax.random.split(jax.random.fold_in(splits[9], 1), TOKENS // TOK_DEV)
    expert_ids_turns = jax.random.permutation(jax.random.fold_in(splits[9], 3), TOKENS // TOK_DEV)
    expert_ids = jax.vmap(lambda own, number: deal_out(jax.random.fold_in(splits[9], 2), own, number, TOK_DEV, EXPERTS, TOP, CAP, 2))(expert_ids_keys, expert_ids_turns).reshape((TOKENS, TOP))
    cotangent = bell_draw(splits[10], (TOKENS, D), 1.0, 6.0, ((0, 32),))
    return dict(images=images, attn_in=attn_in, attn_out=attn_out, norm_gains=norm_gains, mlp_in=mlp_in, mlp_out=mlp_out, router=router, expert_in=expert_in, expert_out=expert_out, expert_ids=expert_ids, cotangent=cotangent)


EPSILON = 1e-06
PRECISE = lax.Precision.HIGHEST

@jax.custom_vjp
def low(v):
    return lax.optimization_barrier(v.astype(jnp.bfloat16)).astype(jnp.float32)

@jax.custom_vjp
def low_back(v):
    return v

def low_keep(v):
    return (low(v), None)

def low_pass(kept, grad):
    return (grad,)

def back_keep(v):
    return (v, None)

def back_low(kept, grad):
    return (low(grad),)
low.defvjp(low_keep, low_pass)
low_back.defvjp(back_keep, back_low)

def normalize(layer_in, norm_gain):
    centred = layer_in - lax.optimization_barrier(jnp.mean(layer_in, axis=-1, keepdims=True))
    spread = lax.optimization_barrier(jnp.mean(centred * centred, axis=-1, keepdims=True))
    return centred * lax.rsqrt(spread + EPSILON) * norm_gain

def attend(layer_in, norm_gain, w_in, w_out):
    normed = low(normalize(layer_in, norm_gain))
    packed = low(low_back(jnp.dot(normed, w_in, precision=PRECISE, preferred_element_type=jnp.float32)))
    pictures = layer_in.shape[0] // SEQ
    shaped = packed.reshape(pictures, SEQ, 3, HEADS, HEAD_DIM)
    scores = low_back(jnp.einsum('gqhd,gkhd->ghqk', shaped[:, :, 0], shaped[:, :, 1], precision=PRECISE) * HEAD_DIM ** (-0.5))
    chances = low(jax.nn.softmax(scores, axis=-1))
    attended = low(low_back(jnp.einsum('ghqk,gkhd->gqhd', chances, shaped[:, :, 2], precision=PRECISE)))
    attended = attended.reshape(layer_in.shape[0], D)
    return layer_in + low_back(jnp.dot(attended, w_out, precision=PRECISE, preferred_element_type=jnp.float32))

def feed_forward(layer_in, norm_gain, w_in, w_out):
    normed = low(normalize(layer_in, norm_gain))
    hidden = low_back(jnp.dot(normed, w_in, precision=PRECISE, preferred_element_type=jnp.float32))
    active = low(jax.nn.gelu(hidden))
    return layer_in + low_back(jnp.dot(active, w_out, precision=PRECISE, preferred_element_type=jnp.float32))

def reference(images, attn_in, attn_out, norm_gains, mlp_in, mlp_out, router, expert_in, expert_out, expert_ids, cotangent):
    chosen = expert_ids.astype(jnp.int32)
    routed_ids = chosen.reshape(-1).astype(jnp.int32)
    row_total = TOKENS * TOP
    row_span = N_EXPERT * N_WSHARD * CAP
    sorted_rows = jnp.argsort(routed_ids, stable=True).astype(jnp.int32)
    matches = (routed_ids[:, None] == jnp.arange(EXPERTS, dtype=jnp.int32)[None, :]).astype(jnp.int32)
    expert_load = lax.optimization_barrier(jnp.sum(matches, axis=0)).astype(jnp.int32)
    offsets = (jnp.cumsum(expert_load) - expert_load).astype(jnp.int32)
    padded_rows = jnp.concatenate([sorted_rows, jnp.full((row_span,), row_total, jnp.int32)])
    positions = jnp.arange(row_span, dtype=jnp.int32)
    row_picks = jnp.take(padded_rows, (offsets[:, None] + positions[None, :]).astype(jnp.int32), axis=0)
    row_picks = jnp.where(positions[None, :] < expert_load[:, None], row_picks, row_total).astype(jnp.int32)

    def forward(input_rows, w_attn_in, w_attn_out, gain_rows, w_mlp_in, w_mlp_out, w_router, w_exp_in, w_exp_out):

        def front(group_rows):
            after_first = attend(group_rows, gain_rows[0], w_attn_in[0], w_attn_out[0])
            after_mlp = feed_forward(after_first, gain_rows[1], w_mlp_in, w_mlp_out)
            return attend(after_mlp, gain_rows[2], w_attn_in[1], w_attn_out[1])
        grouped = input_rows.reshape(N_EXPERT, IMGS_DEV * N_WSHARD * SEQ, D)
        after_second = lax.map(jax.checkpoint(front), grouped).reshape(TOKENS, D)
        routed_in = low(normalize(after_second, gain_rows[3]))
        logits = low_back(jnp.dot(routed_in, w_router, precision=PRECISE, preferred_element_type=jnp.float32))
        chances = jax.nn.softmax(logits, axis=-1)
        picked = jnp.take_along_axis(chances, chosen, axis=1)
        mixing = picked / lax.optimization_barrier(jnp.sum(picked, axis=1, keepdims=True))
        copies = jnp.stack([low_back(routed_in) for branch in range(TOP)], axis=1).reshape(row_total, D)
        copies = jnp.concatenate([copies, jnp.zeros((1, D), jnp.float32)], axis=0)

        def one_expert(pieces):
            picks_now, weight_in, weight_out = pieces
            gathered = jnp.take(copies, picks_now, axis=0)
            hidden = low_back(jnp.dot(gathered, weight_in, precision=PRECISE, preferred_element_type=jnp.float32))
            active = low(jax.nn.gelu(hidden))
            return low(low_back(jnp.dot(active, weight_out, precision=PRECISE, preferred_element_type=jnp.float32)))
        results = lax.map(jax.checkpoint(one_expert), (row_picks, w_exp_in, w_exp_out))
        placed = jnp.zeros((row_total + 1, D), jnp.float32).at[row_picks.reshape(-1)].add(results.reshape(-1, D))
        expert_rows = placed[:row_total].reshape(TOKENS, TOP, D)
        return after_second + lax.optimization_barrier(jnp.sum(mixing[:, :, None] * expert_rows, axis=1))
    primal = (images.astype(jnp.float32), attn_in.astype(jnp.float32), attn_out.astype(jnp.float32), norm_gains.astype(jnp.float32), mlp_in.astype(jnp.float32), mlp_out.astype(jnp.float32), router.astype(jnp.float32), expert_in.astype(jnp.float32), expert_out.astype(jnp.float32))
    final_rows, pullback = jax.vjp(forward, *primal)
    grads = pullback(cotangent.astype(jnp.float32))
    return (final_rows.astype(jnp.bfloat16), grads[0], grads[1], grads[2], grads[3], grads[4], grads[5], grads[6], grads[7], grads[8])
```

```python
import functools

import jax
import jax.numpy as jnp
from jax import lax
from jax.experimental import pallas as pl
from jax.experimental.pallas import tpu as pltpu
from jax.sharding import PartitionSpec as P

D = 512
HEADS = 8
FF = 2048
SEQ = 197
TOP = 2
HEAD_DIM = 64
PAD = 208
EXTRA = 16
CHUNK = 512
EPSILON = 1e-06
ROOT_2_PI = 0.7978845608028654
CUBIC = 0.044715

F32 = jnp.float32
BF16 = jnp.bfloat16
VMEM_LIMIT = 56 * 1024 * 1024


def dot(a, b, ca=1, cb=0):
    return lax.dot_general(a, b, (((ca,), (cb,)), ((), ())), preferred_element_type=F32)


def unit_rows(rows):
    centred = rows - jnp.mean(rows, axis=-1, keepdims=True)
    scale = lax.rsqrt(jnp.mean(centred * centred, axis=-1, keepdims=True) + EPSILON)
    return centred * scale, scale


def norm_backward(unit, scale, gain, grad):
    scaled = gain * grad
    inner = (
        scaled
        - jnp.mean(scaled, axis=-1, keepdims=True)
        - unit * jnp.mean(scaled * unit, axis=-1, keepdims=True)
    )
    return inner * scale, jnp.sum(grad * unit, axis=0, keepdims=True)


def gelu_parts(h):
    square = h * h
    t = jnp.tanh(ROOT_2_PI * h * (1.0 + CUBIC * square))
    half = 0.5 * (1.0 + t)
    slope = half + 0.5 * h * (1.0 - t * t) * (ROOT_2_PI * (1.0 + 3.0 * CUBIC * square))
    return h * half, slope


def gelu(h):
    return 0.5 * h * (1.0 + jnp.tanh(ROOT_2_PI * h * (1.0 + CUBIC * h * h)))


def start_weight(pos_ref, pieces, held, sems, first):
    copies = []
    for j, piece in enumerate(pieces):
        copy = pltpu.make_async_copy(piece, held.at[pos_ref[0] ^ j], sems.at[first + j])
        copy.start()
        copies.append(copy)
    return copies


def wait_all(copies):
    for copy in copies:
        copy.wait()


def softmax_rows(q, k):
    scores = dot(q, k, 1, 1) * (HEAD_DIM**-0.5)
    column = lax.broadcasted_iota(jnp.int32, scores.shape, 1)
    scores = jnp.where(column < SEQ, scores, -1e30)
    raised = jnp.exp(scores - jnp.max(scores, axis=-1, keepdims=True))
    return raised * (1.0 / jnp.sum(raised, axis=-1, keepdims=True))


def attend_forward_kernel(pos_ref, x_ref, gain_ref, *refs):
    wi, wo = refs[0:4], refs[4:8]
    y_ref, packed_ref, o_ref, wi_held, wo_held, sems = refs[8:]
    wi_copies = start_weight(pos_ref, wi, wi_held, sems, 0)
    wo_copies = start_weight(pos_ref, wo, wo_held, sems, 4)
    rows = x_ref[...].astype(F32)
    unit, _ = unit_rows(rows)
    normed = (unit * gain_ref[...]).astype(BF16)
    wait_all(wi_copies)
    packed_ref[...] = dot(normed, wi_held[...].reshape(D, 3 * D)).astype(BF16)
    lane = lax.broadcasted_iota(jnp.int32, (PAD, 2 * HEAD_DIM), 1)
    for image in range(x_ref.shape[0] // PAD):
        here = pl.ds(image * PAD, PAD)
        for pair in range(HEADS // 2):
            at = pair * 2 * HEAD_DIM
            q = packed_ref[here, at : at + 128]
            k = packed_ref[here, D + at : D + at + 128]
            v = packed_ref[here, 2 * D + at : 2 * D + at + 128]
            total = None
            for side in range(2):
                mine = (lane >= HEAD_DIM) == bool(side)
                chances = softmax_rows(jnp.where(mine, q, jnp.zeros_like(q)), k).astype(BF16)
                part = dot(chances, jnp.where(mine, v, jnp.zeros_like(v)))
                total = part if total is None else total + part
            o_ref[here, at : at + 128] = total.astype(BF16)
    wait_all(wo_copies)
    y_ref[...] = x_ref[...].astype(F32) + dot(o_ref[...], wo_held[...].reshape(D, D))


def attend_backward_kernel(smalls, pos_ref, x_ref, gain_ref, packed_ref, o_ref, dz_ref, *refs):
    wi, wo = refs[0:4], refs[4:8]
    extra = refs[8 : 8 + smalls]
    dx_ref, dgain_ref, send_ref, keep_ref, wi_held, wo_held, dp_ref, dout_ref, do_ref, normed_ref, sems = refs[
        8 + smalls :
    ]
    wo_copies = start_weight(pos_ref, wo, wo_held, sems, 4)
    wi_copies = start_weight(pos_ref, wi, wi_held, sems, 0)
    unit, scale = unit_rows(x_ref[...].astype(F32))
    gain = gain_ref[...]
    normed_ref[...] = (unit * gain).astype(BF16)
    dout_ref[...] = dz_ref[...].astype(BF16)
    wait_all(wo_copies)
    do_ref[...] = dot(dout_ref[...], wo_held[...].reshape(D, D), 1, 1).astype(BF16)
    lane = lax.broadcasted_iota(jnp.int32, (PAD, 2 * HEAD_DIM), 1)
    factor = HEAD_DIM**-0.5
    for image in range(x_ref.shape[0] // PAD):
        here = pl.ds(image * PAD, PAD)
        for pair in range(HEADS // 2):
            at = pair * 2 * HEAD_DIM
            q = packed_ref[here, at : at + 128]
            k = packed_ref[here, D + at : D + at + 128]
            v = packed_ref[here, 2 * D + at : 2 * D + at + 128]
            do = do_ref[here, at : at + 128]
            dq = dk = dv = None
            for side in range(2):
                mine = (lane >= HEAD_DIM) == bool(side)
                own = lambda a: jnp.where(mine, a, jnp.zeros_like(a))
                q_own, k_own, do_own = own(q), own(k), own(do)
                chances = softmax_rows(q_own, k)
                dv_part = dot(chances.astype(BF16), do_own, 0, 0)
                da = dot(do_own, v, 1, 1)
                ds = chances * (da - jnp.sum(da * chances, axis=-1, keepdims=True))
                ds = ds.astype(BF16)
                dq_part = dot(ds, k_own)
                dk_part = dot(ds, q_own, 0, 0)
                dq = dq_part if dq is None else dq + dq_part
                dk = dk_part if dk is None else dk + dk_part
                dv = dv_part if dv is None else dv + dv_part
            dp_ref[here, at : at + 128] = (dq * factor).astype(BF16)
            dp_ref[here, D + at : D + at + 128] = (dk * factor).astype(BF16)
            dp_ref[here, 2 * D + at : 2 * D + at + 128] = dv.astype(BF16)
    wait_all(wi_copies)
    dn = dot(dp_ref[...], wi_held[...].reshape(D, 3 * D), 1, 1)
    unit, scale = unit_rows(x_ref[...].astype(F32))
    dx, dgain = norm_backward(unit, scale, gain, dn)
    dx_ref[...] = dz_ref[...] + dx
    dgain_ref[...] = dgain
    for target, flip in ((send_ref, 1), (keep_ref, 0)):
        for place in range(2):
            shard = pos_ref[0] ^ (flip + 2 * (1 - place))
            columns = pl.ds(pl.multiple_of(shard * 128, 128), 128)
            target[place, 0:128, 0 : 3 * D] = dot(normed_ref[:, columns], dp_ref[...], 0, 0).astype(BF16)
            target[place, 0:128, 3 * D : 4 * D] = dot(o_ref[:, columns], dout_ref[...], 0, 0).astype(BF16)
    if smalls:
        small = jnp.concatenate([dgain] + [ref[...] for ref in extra], axis=0)
        small = jnp.concatenate([small, jnp.zeros((EXTRA - small.shape[0] % EXTRA, D), F32)], axis=0)
        for target, flip in ((send_ref, 1), (keep_ref, 0)):
            for place in range(2):
                shard = pos_ref[0] ^ (flip + 2 * (1 - place))
                piece = jnp.zeros((small.shape[0], 128), F32)
                for s in range(4):
                    piece = jnp.where(shard == s, small[:, s * 128 : (s + 1) * 128], piece)
                target[place, 128:, 0:128] = piece.astype(BF16)
                target[place, 128:, 128:] = jnp.zeros((small.shape[0], 4 * D - 128), BF16)


def feed_forward_kernel(pos_ref, x_ref, gain_ref, *refs):
    w1, w2 = refs[0:4], refs[4:8]
    y_ref, w1_held, w2_held, sems = refs[8:]
    w1_copies = start_weight(pos_ref, w1, w1_held, sems, 0)
    w2_copies = start_weight(pos_ref, w2, w2_held, sems, 4)
    unit, _ = unit_rows(x_ref[...])
    normed = (unit * gain_ref[...]).astype(BF16)
    wait_all(w1_copies)
    total = x_ref[...]
    for j in range(FF // CHUNK):
        at = slice(j * CHUNK, (j + 1) * CHUNK)
        active = gelu(dot(normed, w1_held[:, :, at].reshape(D, CHUNK))).astype(BF16)
        if j == 0:
            wait_all(w2_copies)
        total = total + dot(active, w2_held[...].reshape(FF, D)[at])
    y_ref[...] = total


def feed_backward_kernel(pos_ref, x_ref, gain_ref, dz_ref, *refs):
    w1, w2 = refs[0:4], refs[4:8]
    dx_ref, dgain_ref, send1_ref, keep1_ref, send2_ref, keep2_ref, w1_held, w2_held, g1_ref, g2_ref, sems = refs[8:]
    w1_copies = start_weight(pos_ref, w1, w1_held, sems, 0)
    w2_copies = start_weight(pos_ref, w2, w2_held, sems, 4)
    unit, scale = unit_rows(x_ref[...])
    gain = gain_ref[...]
    normed = (unit * gain).astype(BF16)
    dout = dz_ref[...].astype(BF16)
    wait_all(w1_copies)
    wait_all(w2_copies)
    dn = None
    for j in range(FF // CHUNK):
        at = slice(j * CHUNK, (j + 1) * CHUNK)
        w1_now = w1_held[:, :, at].reshape(D, CHUNK)
        w2_now = w2_held[...].reshape(FF, D)[at]
        active, slope = gelu_parts(dot(normed, w1_now))
        dh = (slope * dot(dout, w2_now, 1, 1)).astype(BF16)
        g2_ref[at] = dot(active.astype(BF16), dout, 0, 0).astype(BF16)
        g1_ref[:, at] = dot(normed, dh, 0, 0).astype(BF16)
        part = dot(dh, w1_now, 1, 1)
        dn = part if dn is None else dn + part
    dx, dgain = norm_backward(unit, scale, gain, dn)
    dx_ref[...] = dz_ref[...] + dx
    dgain_ref[...] = dgain
    for one, two, flip in ((send1_ref, send2_ref, 1), (keep1_ref, keep2_ref, 0)):
        for place in range(2):
            shard = pos_ref[0] ^ (flip + 2 * (1 - place))
            one[place] = g1_ref[pl.ds(pl.multiple_of(shard * 128, 128), 128)]
            two[place] = g2_ref[pl.ds(pl.multiple_of(shard * 512, 512), 512)]


def routing_kernel(slots, ids_ref, cot_ref, index_ref, blocks_ref):
    experts = blocks_ref.shape[0] // slots
    tokens = ids_ref.shape[1]
    expert = lax.broadcasted_iota(jnp.int32, (experts, tokens), 0)
    named = [ids_ref[k : k + 1, :] == expert for k in range(TOP)]
    matches = jnp.where(named[0] | named[1], 1.0, 0.0).astype(BF16)
    earlier = lax.broadcasted_iota(jnp.int32, (tokens, tokens), 0) < lax.broadcasted_iota(
        jnp.int32, (tokens, tokens), 1
    )
    rank = dot(matches, jnp.where(earlier, 1.0, 0.0).astype(BF16))
    index_ref[...] = jnp.full(index_ref.shape, -1, jnp.int32)
    place = lax.broadcasted_iota(jnp.int32, (blocks_ref.shape[0], tokens), 0)
    chosen = None
    for k in range(TOP):
        slot = jnp.sum(jnp.where(named[k], rank, 0.0), axis=0, keepdims=True).astype(jnp.int32)
        index = ids_ref[k : k + 1, :] * slots + slot
        index_ref[k : k + 1, :] = index
        hit = place == index
        chosen = hit if chosen is None else chosen | hit
    blocks_ref[...] = dot(jnp.where(chosen, 1.0, 0.0).astype(BF16), cot_ref[...]).astype(BF16)


def write_spare(target, block, slots, column):
    eye = lax.broadcasted_iota(jnp.int32, (slots, D), 0) == lax.broadcasted_iota(jnp.int32, (slots, D), 1)
    line = jnp.sum(jnp.where(eye, column, 0.0), axis=0, keepdims=True)
    high = line.astype(BF16).astype(F32)
    middle = (line - high).astype(BF16).astype(F32)
    low = line - high - middle
    row = lax.broadcasted_iota(jnp.int32, (8, D), 0)
    return jnp.where(row == 0, high, jnp.where(row == 1, middle, jnp.where(row == 2, low, 0.0)))


def read_spare(tile, slots):
    line = tile[0:1] + tile[1:2] + tile[2:3]
    eye = lax.broadcasted_iota(jnp.int32, (slots, D), 0) == lax.broadcasted_iota(jnp.int32, (slots, D), 1)
    return jnp.sum(jnp.where(eye, line, 0.0), axis=1, keepdims=True)


def dispatch_kernel(slots, x_ref, gain_ref, router_ref, ids_ref, index_ref, c_ref, gate_ref, blocks_ref):
    experts = blocks_ref.shape[0] // slots
    tokens = x_ref.shape[0]
    unit, _ = unit_rows(x_ref[...])
    c = (unit * gain_ref[...]).astype(BF16)
    c_ref[...] = c
    logits = dot(router_ref[...], c, 1, 1)
    expert = lax.broadcasted_iota(jnp.int32, (experts, tokens), 0)
    picked = [
        jnp.sum(jnp.where(ids_ref[k : k + 1, :] == expert, logits, 0.0), axis=0, keepdims=True) for k in range(TOP)
    ]
    gates = [0.5 + 0.5 * jnp.tanh(0.5 * (picked[k] - picked[1 - k])) for k in range(TOP)]
    gate_ref[...] = jnp.concatenate(gates + [jnp.zeros((8 - TOP, tokens), F32)], axis=0)
    for e in range(experts):
        place = lax.broadcasted_iota(jnp.int32, (slots, tokens), 0) + e * slots
        hits = [place == index_ref[k : k + 1, :] for k in range(TOP)]
        rows = dot(jnp.where(hits[0] | hits[1], 1.0, 0.0).astype(BF16), c)
        weight = sum(jnp.where(hits[k], gates[k], 0.0) for k in range(TOP))
        tile = write_spare(None, None, slots, jnp.sum(weight, axis=1, keepdims=True))
        blocks_ref[e * slots : (e + 1) * slots] = jnp.concatenate([rows[: slots - 8], tile], axis=0).astype(BF16)


def experts_kernel(c_ref, g_ref, w1_ref, w2_ref, dc_ref, z_ref, dw1_ref, dw2_ref, acc1, acc2):
    together, slots, _ = c_ref.shape
    step = pl.program_id(0)

    @pl.when(step == 0)
    def _():
        acc1[...] = jnp.zeros_like(acc1)
        acc2[...] = jnp.zeros_like(acc2)

    rows = together * slots
    gate = jnp.concatenate([read_spare(c_ref[b, slots - 8 :].astype(F32), slots) for b in range(together)], axis=0)
    c = c_ref[...].reshape(rows, D)
    g = g_ref[...].reshape(rows, D).astype(F32)
    dy = (gate * g).astype(BF16)
    y = dc = None
    for j in range(FF // CHUNK):
        at = slice(j * CHUNK, (j + 1) * CHUNK)
        active, slope = gelu_parts(dot(c, w1_ref[:, at]))
        active = active.astype(BF16)
        dh = (slope * dot(dy, w2_ref[at], 1, 1)).astype(BF16)
        y_part = dot(active, w2_ref[at])
        dc_part = dot(dh, w1_ref[:, at], 1, 1)
        y = y_part if y is None else y + y_part
        dc = dc_part if dc is None else dc + dc_part
        acc1[:, at] += dot(c, dh, 0, 0)
        acc2[at] += dot(active, dy, 0, 0)
    y = y.astype(BF16).astype(F32)
    dgate = jnp.sum(g * y, axis=1, keepdims=True)
    z_ref[...] = (gate * y).astype(BF16).reshape(together, slots, D)
    for b in range(together):
        here = slice(b * slots, (b + 1) * slots)
        tile = write_spare(None, None, slots, dgate[here])
        dc_ref[b] = jnp.concatenate([dc[here][: slots - 8], tile], axis=0).astype(BF16)

    @pl.when(step == pl.num_programs(0) - 1)
    def _():
        dw1_ref[...] = acc1[...].astype(BF16)
        dw2_ref[...] = acc2[...].astype(BF16)


def one_hot_columns(index_ref, width):
    place = lax.broadcasted_iota(jnp.int32, (index_ref.shape[0], width), 1)
    hit = (place == index_ref[:, 0:1]) | (place == index_ref[:, 1:2])
    return jnp.where(hit, 1.0, 0.0).astype(BF16)


def combine_kernel(
    slots, blocks_ref, x_ref, gain_ref, router_ref, ids_ref, index_ref, turned_ref, c_ref, gate_ref, cot_ref,
    dx_ref, dgain_ref, drouter_ref,
):
    experts = blocks_ref.shape[0] // slots
    tokens = x_ref.shape[0]
    gc = dot(one_hot_columns(turned_ref, blocks_ref.shape[0]), blocks_ref[...])
    dgates = [jnp.zeros((1, tokens), F32) for _ in range(TOP)]
    for e in range(experts):
        place = lax.broadcasted_iota(jnp.int32, (slots, tokens), 0) + e * slots
        column = read_spare(blocks_ref[(e + 1) * slots - 8 : (e + 1) * slots].astype(F32), slots)
        for k in range(TOP):
            hit = place == index_ref[k : k + 1, :]
            dgates[k] = dgates[k] + jnp.sum(jnp.where(hit, column, 0.0), axis=0, keepdims=True)
    dl = gate_ref[0:1] * gate_ref[1:2] * (dgates[0] - dgates[1])
    expert = lax.broadcasted_iota(jnp.int32, (experts, tokens), 0)
    dlogits = jnp.where(ids_ref[0:1, :] == expert, dl, 0.0) - jnp.where(ids_ref[1:2, :] == expert, dl, 0.0)
    dlogits = dlogits.astype(BF16)
    gc = gc + dot(dlogits, router_ref[...], 0, 0)
    drouter_ref[...] = dot(dlogits, c_ref[...])
    unit, scale = unit_rows(x_ref[...])
    dx, dgain = norm_backward(unit, scale, gain_ref[...], gc)
    dx_ref[...] = cot_ref[...].astype(F32) + dx
    dgain_ref[...] = dgain


def final_kernel(blocks_ref, x_ref, turned_ref, out_ref):
    out_ref[...] = (x_ref[...] + dot(one_hot_columns(turned_ref, blocks_ref.shape[0]), blocks_ref[...])).astype(BF16)


def call(kernel, outs, *args, scratch=(), specs=None, **more):
    return pl.pallas_call(
        kernel,
        out_shape=[jax.ShapeDtypeStruct(shape, kind) for shape, kind in outs],
        in_specs=specs if specs is not None else [pl.BlockSpec(memory_space=pltpu.VMEM)] * len(args),
        out_specs=[pl.BlockSpec(memory_space=pltpu.VMEM)] * len(outs),
        scratch_shapes=list(scratch),
        compiler_params=pltpu.CompilerParams(vmem_limit_bytes=VMEM_LIMIT),
        **more,
    )(*args)


WHOLE = pl.BlockSpec(memory_space=pltpu.VMEM)
SCALAR = pl.BlockSpec(memory_space=pltpu.SMEM)
AWAY = pl.BlockSpec(memory_space=pl.ANY)


def flip(array, axis, bit):
    return lax.ppermute(array, axis, [(i, i ^ bit) for i in range(lax.axis_size(axis))])


def gather_pieces(piece):
    across = flip(piece, "wshard", 2)
    return (piece, flip(piece, "wshard", 1), across, flip(across, "wshard", 1))


def sum_over_wshard(send, keep):
    half = (keep.astype(F32) + flip(send, "wshard", 1).astype(F32)).astype(BF16)
    return (half[1].astype(F32) + flip(half[0], "wshard", 2).astype(F32)).astype(BF16)


def sum_over_expert(shard):
    owners = lax.axis_size("expert")
    parts = shard.reshape(owners, -1, shard.shape[-1] if shard.shape[0] % owners == 0 else 128)
    parts = lax.all_to_all(parts, "expert", split_axis=0, concat_axis=0, tiled=True)
    own = jnp.sum(parts.astype(F32), axis=0, keepdims=True).astype(BF16)
    every = lax.all_to_all(
        jnp.broadcast_to(own, (owners,) + own.shape[1:]), "expert", split_axis=0, concat_axis=0, tiled=True
    )
    return every.reshape(shard.shape)


def expand(rows, images):
    return jnp.pad(rows.reshape(images, SEQ, -1), ((0, 0), (0, PAD - SEQ), (0, 0))).reshape(images * PAD, -1)


def contract(rows, images):
    return rows.reshape(images, PAD, -1)[:, :SEQ].reshape(images * SEQ, -1)


def local(
    images, attn_in, attn_out, norm_gains, mlp_in, mlp_out, router, expert_in, expert_out, expert_ids, cotangent
):
    owners = lax.axis_size("expert")
    experts = owners * expert_in.shape[0]
    tokens = images.shape[0]
    pictures = tokens // SEQ
    rows = pictures * PAD
    capacity = max(2, 2 * TOP * tokens // experts)
    slots = (capacity + 8 + 15) // 16 * 16
    every = experts * slots
    pos = lax.axis_index("wshard").astype(jnp.int32).reshape(1)

    small = jnp.concatenate([norm_gains, router.T], axis=0)
    small = jnp.pad(small, ((0, -small.shape[0] % 16), (0, 0)))
    small_pieces = gather_pieces(small)
    small_full = jnp.zeros((4,) + small.shape, BF16)
    for j, piece in enumerate(small_pieces):
        small_full = lax.dynamic_update_slice(small_full, piece[None], (pos[0] ^ j, 0, 0))
    small_full = small_full.transpose(1, 0, 2).reshape(small.shape[0], D)
    gains = [small_full[i : i + 1].astype(F32) for i in range(4)]
    router_full = small_full[4 : 4 + experts]

    wi = [gather_pieces(attn_in[0]), None]
    wo = [gather_pieces(attn_out[0]), None]
    w1 = gather_pieces(mlp_in)
    w2 = gather_pieces(mlp_out)
    wi[1] = gather_pieces(attn_in[1])
    wo[1] = gather_pieces(attn_out[1])

    ids = jnp.pad(expert_ids.T.reshape(TOP, pictures, SEQ), ((0, 8 - TOP), (0, 0), (0, PAD - SEQ)), constant_values=-1)
    ids = ids.reshape(8, rows)
    cot = expand(cotangent, pictures)
    x0 = expand(images, pictures)

    index, g_out = call(
        functools.partial(routing_kernel, slots), [((8, rows), jnp.int32), ((every, D), BF16)], ids, cot
    )
    turned = index.T
    trade = functools.partial(lax.all_to_all, axis_name="expert", split_axis=0, concat_axis=0, tiled=True)
    g_in = trade(g_out.reshape(experts, slots, D))

    weight_specs = [AWAY] * 8
    attn_scratch = [pltpu.VMEM((4, D // 4, 3 * D), BF16), pltpu.VMEM((4, D // 4, D), BF16)]
    mlp_scratch = [pltpu.VMEM((4, D // 4, FF), BF16), pltpu.VMEM((4, FF // 4, D), BF16)]
    sems = pltpu.SemaphoreType.DMA((8,))

    def attend(x, layer):
        return call(
            attend_forward_kernel,
            [((rows, D), F32), ((rows, 3 * D), BF16), ((rows, D), BF16)],
            pos, x, gains[2 * layer], *wi[layer], *wo[layer],
            specs=[SCALAR, WHOLE, WHOLE] + weight_specs,
            scratch=attn_scratch + [sems],
        )

    def attend_back(x, layer, packed, o, dz, extra):
        tall = 128 + (EXTRA if extra else 0) * ((sum(a.shape[0] for a in extra) + 1 + EXTRA - 1) // EXTRA)
        return call(
            functools.partial(attend_backward_kernel, len(extra)),
            [((rows, D), F32), ((1, D), F32), ((2, tall, 4 * D), BF16), ((2, tall, 4 * D), BF16)],
            pos, x, gains[2 * layer], packed, o, dz, *wi[layer], *wo[layer], *extra,
            specs=[SCALAR] + [WHOLE] * 5 + weight_specs + [WHOLE] * len(extra),
            scratch=attn_scratch
            + [pltpu.VMEM((rows, 3 * D), BF16)]
            + [pltpu.VMEM((rows, D), BF16)] * 3
            + [sems],
        )

    x1, packed1, o1 = attend(x0, 0)
    (x2,) = call(
        feed_forward_kernel, [((rows, D), F32)], pos, x1, gains[1], *w1, *w2,
        specs=[SCALAR, WHOLE, WHOLE] + weight_specs, scratch=mlp_scratch + [sems],
    )
    x3, packed2, o2 = attend(x2, 1)
    c, gate, c_out = call(
        functools.partial(dispatch_kernel, slots),
        [((rows, D), BF16), ((8, rows), F32), ((every, D), BF16)],
        x3, gains[3], router_full, ids, index,
    )
    c_in = trade(c_out.reshape(experts, slots, D))

    together = 1
    while together * 2 * slots <= 512 and experts % (together * 2) == 0:
        together *= 2
    block = pl.BlockSpec((together, slots, D), lambda i: (i, 0, 0))
    fixed1 = pl.BlockSpec((D, FF), lambda i: (0, 0))
    fixed2 = pl.BlockSpec((FF, D), lambda i: (0, 0))
    dc_out, z_out, dw1, dw2 = pl.pallas_call(
        experts_kernel,
        grid=(experts // together,),
        in_specs=[block, block, fixed1, fixed2],
        out_specs=[block, block, fixed1, fixed2],
        out_shape=[
            jax.ShapeDtypeStruct((experts, slots, D), BF16),
            jax.ShapeDtypeStruct((experts, slots, D), BF16),
            jax.ShapeDtypeStruct((D, FF), BF16),
            jax.ShapeDtypeStruct((FF, D), BF16),
        ],
        scratch_shapes=[pltpu.VMEM((D, FF), F32), pltpu.VMEM((FF, D), F32)],
        compiler_params=pltpu.CompilerParams(vmem_limit_bytes=VMEM_LIMIT),
    )(c_in, g_in, expert_in[0], expert_out[0])
    dc_in = trade(dc_out)
    z_in = trade(z_out)

    g3, gain3, drouter = call(
        functools.partial(combine_kernel, slots),
        [((rows, D), F32), ((1, D), F32), ((experts, D), F32)],
        dc_in.reshape(every, D), x3, gains[3], router_full, ids, index, turned, c, gate, cot,
    )
    g2, gain2, send, keep = attend_back(x2, 1, packed2, o2, g3, [])
    second = sum_over_expert(sum_over_wshard(send, keep))
    g1, gain1, send1, keep1, send2, keep2 = call(
        feed_backward_kernel,
        [((rows, D), F32), ((1, D), F32)]
        + [((2, D // 4, FF), BF16)] * 2
        + [((2, FF // 4, D), BF16)] * 2,
        pos, x1, gains[1], g2, *w1, *w2,
        specs=[SCALAR, WHOLE, WHOLE, WHOLE] + weight_specs,
        scratch=mlp_scratch + [pltpu.VMEM((D, FF), BF16), pltpu.VMEM((FF, D), BF16), sems],
    )
    mlp1 = sum_over_expert(sum_over_wshard(send1, keep1))
    mlp2 = sum_over_expert(sum_over_wshard(send2, keep2))
    dx, _, send, keep = attend_back(x0, 0, packed1, o1, g1, [gain1, gain2, gain3, drouter])
    first = sum_over_expert(sum_over_wshard(send, keep))
    (final,) = call(final_kernel, [((rows, D), BF16)], z_in.reshape(every, D), x3, turned)

    def sum_experts(grad):
        half = grad.shape[0] // 2
        core = pos[0] % 2
        send = lax.dynamic_slice_in_dim(grad, (1 - core) * half, half)
        keep = lax.dynamic_slice_in_dim(grad, core * half, half)
        part = (keep.astype(F32) + flip(send, "wshard", 1).astype(F32)).astype(BF16)
        part = (part.astype(F32) + flip(part, "wshard", 2).astype(F32)).astype(BF16)
        other = flip(part, "wshard", 1)
        whole = jnp.where(core == 0, jnp.concatenate([part, other]), jnp.concatenate([other, part]))
        return whole.astype(F32)[None]

    small = first[128:, 0:128].astype(F32)
    return (
        contract(final, pictures),
        contract(dx, pictures),
        jnp.stack([first[:128, : 3 * D], second[:, : 3 * D]]).astype(F32),
        jnp.stack([first[:128, 3 * D :], second[:, 3 * D :]]).astype(F32),
        small[0:4],
        mlp1.astype(F32),
        mlp2.astype(F32),
        small[4 : 4 + experts].T,
        sum_experts(dw1),
        sum_experts(dw2),
    )


def solution(mesh):
    rows = P(("expert", "wshard"), None)
    dense = (P(None, "wshard", None), P(None, "wshard", None), P(None, "wshard"))
    shards = (P("wshard", None),) * 3
    experts = (P("expert", None, None),) * 2
    return jax.shard_map(
        local,
        mesh=mesh,
        in_specs=(rows, *dense, *shards, *experts, rows, rows),
        out_specs=(rows, rows, *dense, *shards, *experts),
        check_vma=False,
    )
```

```python
import functools

import jax
import jax.numpy as jnp
from jax import lax
from jax.experimental import pallas as pl
from jax.experimental.pallas import tpu as pltpu
from jax.sharding import PartitionSpec as P

D = 512
HEADS = 8
FF = 2048
SEQ = 197
TOP = 2
HEAD_DIM = 64
PAD = 208
STRIP = 16
CHUNK = 512
EPSILON = 1e-06
ROOT_2_PI = 0.7978845608028654
CUBIC = 0.044715

F32 = jnp.float32
BF16 = jnp.bfloat16
VMEM_LIMIT = 56 * 1024 * 1024
LINKED = 8


def dot(a, b, ca=1, cb=0):
    return lax.dot_general(a, b, (((ca,), (cb,)), ((), ())), preferred_element_type=F32)


def unit_rows(rows):
    centred = rows - jnp.mean(rows, axis=-1, keepdims=True)
    scale = lax.rsqrt(jnp.mean(centred * centred, axis=-1, keepdims=True) + EPSILON)
    return centred * scale, scale


def norm_backward(unit, scale, gain, grad):
    scaled = gain * grad
    inner = (
        scaled
        - jnp.mean(scaled, axis=-1, keepdims=True)
        - unit * jnp.mean(scaled * unit, axis=-1, keepdims=True)
    )
    return inner * scale, jnp.sum(grad * unit, axis=0, keepdims=True)


def gelu_parts(h):
    square = h * h
    t = jnp.tanh(ROOT_2_PI * h * (1.0 + CUBIC * square))
    half = 0.5 * (1.0 + t)
    slope = half + 0.5 * h * (1.0 - t * t) * (ROOT_2_PI * (1.0 + 3.0 * CUBIC * square))
    return h * half, slope


def gelu(h):
    return 0.5 * h * (1.0 + jnp.tanh(ROOT_2_PI * h * (1.0 + CUBIC * h * h)))


def start_weight(pos_ref, pieces, held, sems, first):
    copies = []
    for j, piece in enumerate(pieces):
        copy = pltpu.make_async_copy(piece, held.at[pos_ref[0] ^ j], sems.at[first + j])
        copy.start()
        copies.append(copy)
    return copies


def wait_all(copies):
    for copy in copies:
        copy.wait()


def softmax_rows(q, k):
    scores = dot(q, k, 1, 1) * (HEAD_DIM**-0.5)
    column = lax.broadcasted_iota(jnp.int32, scores.shape, 1)
    scores = jnp.where(column < SEQ, scores, -1e30)
    raised = jnp.exp(scores - jnp.max(scores, axis=-1, keepdims=True))
    return raised * (1.0 / jnp.sum(raised, axis=-1, keepdims=True))


def shards_of(pos_ref, send_ref, keep_ref):
    for target, turn in ((send_ref, 1), (keep_ref, 0)):
        for place in range(2):
            yield target, place, pos_ref[0] ^ (turn + 2 * (1 - place))


def own_half(pos_ref, half):
    return 1 - ((pos_ref[1] & 1) ^ half)


def attend_forward_kernel(pos_ref, x_ref, gain_ref, *refs):
    wi, wo = refs[0:4], refs[4:8]
    y_ref, packed_ref, o_ref, wi_held, wo_held, sems = refs[8:]
    wi_copies = start_weight(pos_ref, wi, wi_held, sems, 0)
    wo_copies = start_weight(pos_ref, wo, wo_held, sems, 4)
    rows = x_ref[...].astype(F32)
    unit, _ = unit_rows(rows)
    normed = (unit * gain_ref[...]).astype(BF16)
    wait_all(wi_copies)
    packed_ref[...] = dot(normed, wi_held[...].reshape(D, 3 * D)).astype(BF16)
    lane = lax.broadcasted_iota(jnp.int32, (PAD, 2 * HEAD_DIM), 1)
    for image in range(x_ref.shape[0] // PAD):
        here = pl.ds(image * PAD, PAD)
        for pair in range(HEADS // 2):
            at = pair * 2 * HEAD_DIM
            q = packed_ref[here, at : at + 128]
            k = packed_ref[here, D + at : D + at + 128]
            v = packed_ref[here, 2 * D + at : 2 * D + at + 128]
            total = None
            for side in range(2):
                mine = (lane >= HEAD_DIM) == bool(side)
                chances = softmax_rows(jnp.where(mine, q, jnp.zeros_like(q)), k).astype(BF16)
                part = dot(chances, jnp.where(mine, v, jnp.zeros_like(v)))
                total = part if total is None else total + part
            o_ref[here, at : at + 128] = total.astype(BF16)
    wait_all(wo_copies)
    y_ref[...] = x_ref[...].astype(F32) + dot(o_ref[...], wo_held[...].reshape(D, D))


def attend_backward_kernel(smalls, pos_ref, x_ref, gain_ref, packed_ref, o_ref, dz_ref, *refs):
    wi, wo = refs[0:4], refs[4:8]
    extra = refs[8 : 8 + smalls]
    dx_ref, dgain_ref, send_ref, keep_ref, wi_held, wo_held, dp_ref, dout_ref, do_ref, normed_ref, sems = refs[
        8 + smalls :
    ]
    wo_copies = start_weight(pos_ref, wo, wo_held, sems, 4)
    wi_copies = start_weight(pos_ref, wi, wi_held, sems, 0)
    unit, scale = unit_rows(x_ref[...].astype(F32))
    gain = gain_ref[...]
    normed_ref[...] = (unit * gain).astype(BF16)
    dout_ref[...] = dz_ref[...].astype(BF16)
    wait_all(wo_copies)
    do_ref[...] = dot(dout_ref[...], wo_held[...].reshape(D, D), 1, 1).astype(BF16)
    lane = lax.broadcasted_iota(jnp.int32, (PAD, 2 * HEAD_DIM), 1)
    factor = HEAD_DIM**-0.5
    for image in range(x_ref.shape[0] // PAD):
        here = pl.ds(image * PAD, PAD)
        for pair in range(HEADS // 2):
            at = pair * 2 * HEAD_DIM
            q = packed_ref[here, at : at + 128]
            k = packed_ref[here, D + at : D + at + 128]
            v = packed_ref[here, 2 * D + at : 2 * D + at + 128]
            do = do_ref[here, at : at + 128]
            dq = dk = dv = None
            for side in range(2):
                mine = (lane >= HEAD_DIM) == bool(side)
                own = lambda a: jnp.where(mine, a, jnp.zeros_like(a))
                q_own, k_own, do_own = own(q), own(k), own(do)
                chances = softmax_rows(q_own, k)
                dv_part = dot(chances.astype(BF16), do_own, 0, 0)
                da = dot(do_own, v, 1, 1)
                ds = chances * (da - jnp.sum(da * chances, axis=-1, keepdims=True))
                ds = ds.astype(BF16)
                dq_part = dot(ds, k_own)
                dk_part = dot(ds, q_own, 0, 0)
                dq = dq_part if dq is None else dq + dq_part
                dk = dk_part if dk is None else dk + dk_part
                dv = dv_part if dv is None else dv + dv_part
            dp_ref[here, at : at + 128] = (dq * factor).astype(BF16)
            dp_ref[here, D + at : D + at + 128] = (dk * factor).astype(BF16)
            dp_ref[here, 2 * D + at : 2 * D + at + 128] = dv.astype(BF16)
    wait_all(wi_copies)
    dn = dot(dp_ref[...], wi_held[...].reshape(D, 3 * D), 1, 1)
    unit, scale = unit_rows(x_ref[...].astype(F32))
    dx, dgain = norm_backward(unit, scale, gain, dn)
    dx_ref[...] = dz_ref[...] + dx
    dgain_ref[...] = dgain
    for target, place, shard in shards_of(pos_ref, send_ref, keep_ref):
        columns = pl.ds(pl.multiple_of(shard * 128, 128), 128)
        grad_in = dot(normed_ref[:, columns], dp_ref[...], 0, 0).astype(BF16)
        grad_out = dot(o_ref[:, columns], dout_ref[...], 0, 0).astype(BF16)
        for half in range(2):
            there = own_half(pos_ref, half)
            target[place, there, :, 0 : 3 * D] = grad_in[half * 64 : half * 64 + 64]
            target[place, there, :, 3 * D : 4 * D] = grad_out[half * 64 : half * 64 + 64]
    if smalls:
        small = jnp.concatenate([dgain] + [ref[...] for ref in extra], axis=0)
        small = jnp.concatenate([small, jnp.zeros((-small.shape[0] % STRIP, D), F32)], axis=0)
        for target, place, shard in shards_of(pos_ref, send_ref, keep_ref):
            piece = jnp.zeros((small.shape[0], 128), F32)
            for s in range(4):
                piece = jnp.where(shard == s, small[:, s * 128 : (s + 1) * 128], piece)
            piece = piece.astype(BF16)
            for half in range(2):
                for strip in range(64 // STRIP):
                    for group in range(small.shape[0] // STRIP):
                        at = 4 * D + group * 128
                        target[place, half, strip * STRIP : (strip + 1) * STRIP, at : at + 128] = piece[
                            group * STRIP : (group + 1) * STRIP
                        ]


def feed_forward_kernel(pos_ref, x_ref, gain_ref, *refs):
    w1, w2 = refs[0:4], refs[4:8]
    y_ref, w1_held, w2_held, sems = refs[8:]
    w1_copies = start_weight(pos_ref, w1, w1_held, sems, 0)
    w2_copies = start_weight(pos_ref, w2, w2_held, sems, 4)
    unit, _ = unit_rows(x_ref[...])
    normed = (unit * gain_ref[...]).astype(BF16)
    wait_all(w1_copies)
    total = x_ref[...]
    for j in range(FF // CHUNK):
        at = slice(j * CHUNK, (j + 1) * CHUNK)
        active = gelu(dot(normed, w1_held[:, :, at].reshape(D, CHUNK))).astype(BF16)
        if j == 0:
            wait_all(w2_copies)
        total = total + dot(active, w2_held[...].reshape(FF, D)[at])
    y_ref[...] = total


def feed_backward_kernel(pos_ref, x_ref, gain_ref, dz_ref, *refs):
    w1, w2 = refs[0:4], refs[4:8]
    dx_ref, dgain_ref, send_ref, keep_ref, w1_held, w2_held, g1_ref, g2_ref, sems = refs[8:]
    w1_copies = start_weight(pos_ref, w1, w1_held, sems, 0)
    w2_copies = start_weight(pos_ref, w2, w2_held, sems, 4)
    unit, scale = unit_rows(x_ref[...])
    gain = gain_ref[...]
    normed = (unit * gain).astype(BF16)
    dout = dz_ref[...].astype(BF16)
    wait_all(w1_copies)
    wait_all(w2_copies)
    dn = None
    for j in range(FF // CHUNK):
        at = slice(j * CHUNK, (j + 1) * CHUNK)
        w1_now = w1_held[:, :, at].reshape(D, CHUNK)
        w2_now = w2_held[...].reshape(FF, D)[at]
        active, slope = gelu_parts(dot(normed, w1_now))
        dh = (slope * dot(dout, w2_now, 1, 1)).astype(BF16)
        g2_ref[at] = dot(active.astype(BF16), dout, 0, 0).astype(BF16)
        g1_ref[:, at] = dot(normed, dh, 0, 0).astype(BF16)
        part = dot(dh, w1_now, 1, 1)
        dn = part if dn is None else dn + part
    dx, dgain = norm_backward(unit, scale, gain, dn)
    dx_ref[...] = dz_ref[...] + dx
    dgain_ref[...] = dgain
    for target, place, shard in shards_of(pos_ref, send_ref, keep_ref):
        for half in range(2):
            there = own_half(pos_ref, half)
            target[place, there, 0:64] = g1_ref[pl.ds(pl.multiple_of(shard * 128 + half * 64, 64), 64)]
            for part in range(4):
                start = pl.multiple_of(shard * 512 + part * 128 + half * 64, 64)
                target[place, there, 64:128, part * 512 : (part + 1) * 512] = g2_ref[pl.ds(start, 64)]


def routing_kernel(slots, ids_ref, cot_ref, index_ref, blocks_ref):
    experts = blocks_ref.shape[0] // slots
    tokens = ids_ref.shape[1]
    expert = lax.broadcasted_iota(jnp.int32, (experts, tokens), 0)
    named = [ids_ref[k : k + 1, :] == expert for k in range(TOP)]
    matches = jnp.where(named[0] | named[1], 1.0, 0.0).astype(BF16)
    earlier = lax.broadcasted_iota(jnp.int32, (tokens, tokens), 0) < lax.broadcasted_iota(
        jnp.int32, (tokens, tokens), 1
    )
    rank = dot(matches, jnp.where(earlier, 1.0, 0.0).astype(BF16))
    index_ref[...] = jnp.full(index_ref.shape, -1, jnp.int32)
    place = lax.broadcasted_iota(jnp.int32, (blocks_ref.shape[0], tokens), 0)
    chosen = None
    for k in range(TOP):
        slot = jnp.sum(jnp.where(named[k], rank, 0.0), axis=0, keepdims=True).astype(jnp.int32)
        index = ids_ref[k : k + 1, :] * slots + slot
        index_ref[k : k + 1, :] = index
        hit = place == index
        chosen = hit if chosen is None else chosen | hit
    blocks_ref[...] = dot(jnp.where(chosen, 1.0, 0.0).astype(BF16), cot_ref[...]).astype(BF16)


def write_spare(slots, column):
    eye = lax.broadcasted_iota(jnp.int32, (slots, D), 0) == lax.broadcasted_iota(jnp.int32, (slots, D), 1)
    line = jnp.sum(jnp.where(eye, column, 0.0), axis=0, keepdims=True)
    high = line.astype(BF16).astype(F32)
    middle = (line - high).astype(BF16).astype(F32)
    low = line - high - middle
    row = lax.broadcasted_iota(jnp.int32, (8, D), 0)
    return jnp.where(row == 0, high, jnp.where(row == 1, middle, jnp.where(row == 2, low, 0.0)))


def read_spare(tile, slots):
    line = tile[0:1] + tile[1:2] + tile[2:3]
    eye = lax.broadcasted_iota(jnp.int32, (slots, D), 0) == lax.broadcasted_iota(jnp.int32, (slots, D), 1)
    return jnp.sum(jnp.where(eye, line, 0.0), axis=1, keepdims=True)


def small_kernel(pos_ref, *refs):
    out_ref = refs[4]
    for j in range(4):
        start = pl.multiple_of((pos_ref[0] ^ j) * 128, 128)
        out_ref[:, pl.ds(start, 128)] = refs[j][...].astype(F32)


def dispatch_kernel(slots, pos_ref, x_ref, gain_ref, router_ref, ids_ref, index_ref, c_ref, gate_ref, *blocks):
    tokens = x_ref.shape[0]
    each = blocks[0].shape[0] // slots
    experts = len(blocks) * each
    unit, _ = unit_rows(x_ref[...])
    c = (unit * gain_ref[...]).astype(BF16)
    c_ref[...] = c
    logits = dot(router_ref[...].astype(BF16), c, 1, 1)
    expert = lax.broadcasted_iota(jnp.int32, (experts, tokens), 0)
    picked = [
        jnp.sum(jnp.where(ids_ref[k : k + 1, :] == expert, logits, 0.0), axis=0, keepdims=True) for k in range(TOP)
    ]
    gates = [0.5 + 0.5 * jnp.tanh(0.5 * (picked[k] - picked[1 - k])) for k in range(TOP)]
    gate_ref[...] = jnp.concatenate(gates + [jnp.zeros((8 - TOP, tokens), F32)], axis=0)
    for k in range(experts):
        place = lax.broadcasted_iota(jnp.int32, (slots, tokens), 0) + (pos_ref[1] ^ k) * slots
        hits = [place == index_ref[k : k + 1, :] for k in range(TOP)]
        rows = dot(jnp.where(hits[0] | hits[1], 1.0, 0.0).astype(BF16), c)
        weight = sum(jnp.where(hits[k], gates[k], 0.0) for k in range(TOP))
        tile = write_spare(slots, jnp.sum(weight, axis=1, keepdims=True))
        at = k % each * slots
        blocks[k // each][at : at + slots] = jnp.concatenate([rows[: slots - 8], tile], axis=0).astype(BF16)


def experts_kernel(slots, n, each, pos_ref, w1_ref, w2_ref, *refs):
    g_refs, c_refs, refs = refs[: n * each], refs[n * each : n * each + n], refs[n * each + n :]
    dc_refs, z_refs = refs[:n], refs[n : 2 * n]
    f_ref, dh_ref, dy_ref, gate_ref, y_ref, dc_ref = refs[2 * n :]
    step = pl.program_id(0)
    blocks = [(b, slice(b * slots, (b + 1) * slots)) for b in range(n * each)]

    @pl.when(step == 0)
    def _():
        for b, here in blocks:
            end = (b % each + 1) * slots
            gate = read_spare(c_refs[b // each][end - 8 : end].astype(F32), slots)
            gate_ref[here] = jnp.broadcast_to(gate, (slots, 128))
            dy_ref[here] = (gate * g_refs[b][0].astype(F32)).astype(BF16)

    c = c_refs[0][...] if n == 1 else jnp.concatenate([ref[...] for ref in c_refs], axis=0)
    active, slope = gelu_parts(dot(c, w1_ref[...]))
    active = active.astype(BF16)
    f_ref[...] = active
    dh = (slope * dot(dy_ref[...], w2_ref[...], 1, 1)).astype(BF16)
    dh_ref[...] = dh
    y = dot(active, w2_ref[...])
    dc = dot(dh, w1_ref[...], 1, 1)

    @pl.when(step == 0)
    def _():
        y_ref[...] = y
        dc_ref[...] = dc

    @pl.when(step > 0)
    def _():
        y_ref[...] += y
        dc_ref[...] += dc

    @pl.when(step == pl.num_programs(0) - 1)
    def _():
        for b, here in blocks:
            there = slice(b % each * slots, (b % each + 1) * slots)
            rounded = y_ref[here].astype(BF16).astype(F32)
            dgate = jnp.sum(g_refs[b][0].astype(F32) * rounded, axis=1, keepdims=True)
            z_refs[b // each][there] = (gate_ref[here, 0:1] * rounded).astype(BF16)
            rows = jnp.concatenate([dc_ref[here][: slots - 8], write_spare(slots, dgate)], axis=0)
            dc_refs[b // each][there] = rows.astype(BF16)


def expert_grads_kernel(n, pos_ref, *refs):
    m = len(refs) - 2 - 3 * n
    c_refs = refs[:m]
    f_refs, dh_refs, dy_refs = refs[m : m + n], refs[m + n : m + 2 * n], refs[m + 2 * n : m + 3 * n]
    send_ref, keep_ref = refs[m + 3 * n :]
    per = m // n
    for target, half in ((send_ref, 1 - (pos_ref[0] & 1)), (keep_ref, pos_ref[0] & 1)):
        at = pl.ds(pl.multiple_of(half * 256, 256), 256)
        total1 = total2 = None
        for i in range(n):
            c = [ref[:, at] for ref in c_refs[i * per : (i + 1) * per]]
            c = c[0] if per == 1 else jnp.concatenate(c, axis=0)
            part1 = dot(c, dh_refs[i][...], 0, 0)
            part2 = dot(f_refs[i][...], dy_refs[i][:, at], 0, 0)
            total1 = part1 if total1 is None else total1 + part1
            total2 = part2 if total2 is None else total2 + part2
        target[0:256] = total1.astype(BF16)
        target[256:512, 0:256] = total2[0:256].astype(BF16)
        target[256:512, 256:512] = total2[256:512].astype(BF16)


def join_kernel(pos_ref, own_ref, other_ref, out1_ref, out2_ref):
    core = pos_ref[0] & 1
    for mine, ref in ((core, own_ref), (1 - core, other_ref)):
        at = pl.ds(pl.multiple_of(mine * 256, 256), 256)
        out1_ref[at] = ref[0:256].astype(F32)
        for block in range(FF // 256):
            out2_ref[block * 256 : (block + 1) * 256, at] = ref[256:512, block * 256 : (block + 1) * 256].astype(F32)


def arrange_kernel(pos_ref, *refs):
    for k, ref in enumerate(refs[:-1]):
        refs[-1][pos_ref[1] ^ k] = ref[...]


def one_hot_columns(index_ref, width):
    place = lax.broadcasted_iota(jnp.int32, (index_ref.shape[0], width), 1)
    hit = (place == index_ref[:, 0:1]) | (place == index_ref[:, 1:2])
    return jnp.where(hit, 1.0, 0.0).astype(BF16)


def combine_kernel(
    slots, pos_ref, x_ref, gain_ref, router_ref, ids_ref, index_ref, turned_ref, c_ref, gate_ref, cot_ref, *refs
):
    blocks, (dx_ref, dgain_ref, drouter_ref) = refs[:-3], refs[-3:]
    each = blocks[0].shape[0] // slots
    experts = len(blocks) * each
    tokens = x_ref.shape[0]
    dgates = [jnp.zeros((1, tokens), F32) for _ in range(TOP)]
    gc = None
    for k in range(experts):
        at = k % each * slots
        block = blocks[k // each][at : at + slots]
        start = (pos_ref[1] ^ k) * slots
        place = lax.broadcasted_iota(jnp.int32, (tokens, slots), 1) + start
        hit = (place == turned_ref[:, 0:1]) | (place == turned_ref[:, 1:2])
        part = dot(jnp.where(hit, 1.0, 0.0).astype(BF16), block)
        gc = part if gc is None else gc + part
        place = lax.broadcasted_iota(jnp.int32, (slots, tokens), 0) + start
        column = read_spare(block[slots - 8 :].astype(F32), slots)
        for j in range(TOP):
            hit = place == index_ref[j : j + 1, :]
            dgates[j] = dgates[j] + jnp.sum(jnp.where(hit, column, 0.0), axis=0, keepdims=True)
    dl = gate_ref[0:1] * gate_ref[1:2] * (dgates[0] - dgates[1])
    expert = lax.broadcasted_iota(jnp.int32, (experts, tokens), 0)
    dlogits = jnp.where(ids_ref[0:1, :] == expert, dl, 0.0) - jnp.where(ids_ref[1:2, :] == expert, dl, 0.0)
    dlogits = dlogits.astype(BF16)
    gc = gc + dot(dlogits, router_ref[...].astype(BF16), 0, 0)
    drouter_ref[...] = dot(dlogits, c_ref[...])
    unit, scale = unit_rows(x_ref[...])
    dx, dgain = norm_backward(unit, scale, gain_ref[...], gc)
    dx_ref[...] = cot_ref[...].astype(F32) + dx
    dgain_ref[...] = dgain


def split_square_kernel(n, packed, pos_ref, *refs):
    kept, came, outs = refs[0:n], refs[n : 2 * n], refs[2 * n :]
    for place in range(2):
        for half in range(2):
            row = 0
            for keep, new in zip(kept, came):
                tall = keep.shape[2]
                total = (keep[place, half].astype(F32) + new[place, half].astype(F32)).astype(BF16)
                if packed:
                    there = 2 * ((pos_ref[1] & 1) ^ (1 - half)) + ((pos_ref[0] >> 1) ^ (1 - place))
                    outs[0][there, row : row + tall] = total
                else:
                    outs[2 * place + half][row : row + tall] = total
                row += tall


def sum_square_kernel(a_ref, out_ref):
    total = a_ref[0].astype(F32) + a_ref[1].astype(F32) + (a_ref[2].astype(F32) + a_ref[3].astype(F32))
    total = total.astype(BF16)
    for k in range(4):
        for unit in range(a_ref.shape[1] // 64):
            start = unit * 64 + k * STRIP
            out_ref[k, unit * STRIP : (unit + 1) * STRIP] = total[start : start + STRIP]


def sum_depth_kernel(a_ref, out_ref):
    total = a_ref[0].astype(F32) + a_ref[1].astype(F32) + (a_ref[2].astype(F32) + a_ref[3].astype(F32))
    for k in range(4):
        out_ref[k] = total.astype(BF16)


def split_depth_kernel(pos_ref, a_ref, b_ref, c_ref, d_ref, out0, out1, out2, out3, total_ref):
    total_ref[...] = (
        a_ref[...].astype(F32) + b_ref[...].astype(F32) + (c_ref[...].astype(F32) + d_ref[...].astype(F32))
    )
    for k, out in enumerate((out0, out1, out2, out3)):
        for unit in range(a_ref.shape[0] // 64):
            start = pl.multiple_of(unit * 64 + ((pos_ref[1] >> 1) ^ k) * STRIP, STRIP)
            out[unit * STRIP : (unit + 1) * STRIP] = total_ref[pl.ds(start, STRIP)].astype(BF16)


def sum_kernel(*refs):
    total = refs[0][...].astype(F32)
    for ref in refs[1:-1]:
        total = total + ref[...].astype(F32)
    refs[-1][...] = total.astype(BF16)


def rows_of(pos_ref, k):
    source = pos_ref[1] ^ k
    return pl.ds(pl.multiple_of((source & 1) * 64 + (source >> 1) * STRIP, STRIP), STRIP)


def rows_at(pos_ref, k):
    return pl.ds(pl.multiple_of(((pos_ref[1] ^ k) & 1) * 64 + k // 2 * STRIP, STRIP), STRIP)


def finish_mlp_kernel(pos_ref, *refs):
    mlp1_ref, mlp2_ref = refs[2:]
    for k in range(8):
        there = rows_at(pos_ref, k)
        strips = refs[k % 2]
        mlp1_ref[there] = strips[k // 2, STRIP : 2 * STRIP].astype(F32)
        for part in range(4):
            mlp2_ref[part, there] = strips[k // 2, 2 * STRIP :, part * 512 : (part + 1) * 512].astype(F32)


def finish_attention_kernel(pos_ref, *refs):
    first, second = refs[0:8], refs[8:10]
    in_ref, out_ref, small_ref = refs[10:]
    for k in range(8):
        for layer, strip, there in (
            (0, first[k][...], rows_of(pos_ref, k)),
            (1, second[k % 2][k // 2, 0:STRIP], rows_at(pos_ref, k)),
        ):
            in_ref[layer, there] = strip[:, 0 : 3 * D].astype(F32)
            out_ref[layer, there] = strip[:, 3 * D : 4 * D].astype(F32)
    for group in range(small_ref.shape[0] // STRIP):
        at = 4 * D + group * 128
        small_ref[group * STRIP : (group + 1) * STRIP] = first[0][:, at : at + 128].astype(F32)


def final_kernel(blocks_ref, x_ref, turned_ref, out_ref):
    out_ref[...] = (x_ref[...] + dot(one_hot_columns(turned_ref, blocks_ref.shape[0]), blocks_ref[...])).astype(BF16)


def spent(us):
    return pl.CostEstimate(flops=int(us * 1.0e9), bytes_accessed=0, transcendentals=0)


def call(kernel, outs, *args, us=1.0, scratch=(), specs=None, **more):
    return list(
        pl.pallas_call(
        kernel,
        out_shape=[jax.ShapeDtypeStruct(shape, kind) for shape, kind in outs],
        in_specs=specs if specs is not None else [WHOLE] * len(args),
        out_specs=[WHOLE] * len(outs),
        scratch_shapes=list(scratch),
        cost_estimate=spent(us),
        compiler_params=pltpu.CompilerParams(vmem_limit_bytes=VMEM_LIMIT),
        **more,
        )(*args)
    )


WHOLE = pl.BlockSpec(memory_space=pltpu.VMEM)
SCALAR = pl.BlockSpec(memory_space=pltpu.SMEM)
AWAY = pl.BlockSpec(memory_space=pl.ANY)


def flip(array, axis, bit):
    return lax.ppermute(array, axis, [(i, i ^ bit) for i in range(lax.axis_size(axis))])


def flip_both(array, bit_expert, bit_wshard):
    inner = lax.axis_size("wshard")
    pairs = [
        (i, (i // inner ^ bit_expert) * inner + (i % inner ^ bit_wshard))
        for i in range(lax.axis_size("expert") * inner)
    ]
    return lax.ppermute(array, ("expert", "wshard"), pairs)


def gather_pieces(piece, across=None):
    across = flip(piece, "wshard", 2) if across is None else across
    return (piece, flip(piece, "wshard", 1), across, flip(across, "wshard", 1))


def after(array, *others):
    return lax.optimization_barrier((array, *others))[0]


def split_square(pos, bundle, packed):
    came = [flip(send, "wshard", 1) for send, _ in bundle]
    tall = sum(keep.shape[2] for _, keep in bundle)
    wide = bundle[0][0].shape[-1]
    return call(
        functools.partial(split_square_kernel, len(bundle), packed),
        [((4, tall, wide), BF16)] if packed else [((tall, wide), BF16)] * 4,
        pos,
        *[keep for _, keep in bundle],
        *came,
        specs=[SCALAR] + [WHOLE] * (2 * len(bundle)),
        us=3.0,
    )


def trade_square(blocks):
    inner = lax.axis_size("wshard")
    groups = [
        [(z * 2 + x) * inner + y * 2 + core for x in range(2) for y in range(2)]
        for z in range(lax.axis_size("expert") // 2)
        for core in range(2)
    ]
    return lax.all_to_all(blocks, ("expert", "wshard"), 0, 0, axis_index_groups=groups, tiled=True)


def trade_depth(blocks):
    groups = [[z * 2 + x for z in range(4)] for x in range(2)]
    return lax.all_to_all(blocks, "expert", 0, 0, axis_index_groups=groups, tiled=True)


def sum_square(blocks):
    _, tall, wide = blocks.shape
    return call(sum_square_kernel, [((4, tall // 4, wide), BF16)], blocks, us=2.0)[0]


def sum_depth(blocks):
    return call(sum_depth_kernel, [(blocks.shape, BF16)], blocks)[0]


def cross_square(pos, far, up, side, own):
    tall, wide = own.shape
    return call(
        split_depth_kernel,
        [((tall // 4, wide), BF16)] * 4,
        pos, own, flip(up, "wshard", 2), flip(side, "expert", 1), flip_both(far, 1, 2),
        us=2.0,
        specs=[SCALAR] + [WHOLE] * 4,
        scratch=[pltpu.VMEM((tall, wide), F32)],
    )


def cross_depth(parts):
    came = [flip(parts[k], "expert", 2 * k) for k in range(1, 4)]
    return call(sum_kernel, [(parts[0].shape, BF16)], parts[0], *came)[0]


def spread(strip):
    return [strip] + [flip(strip, "expert", k) for k in range(1, 8)]


def sum_plainly(send, keep):
    half = (keep.astype(F32) + flip(send, "wshard", 1).astype(F32)).astype(BF16)
    rows = half[1].astype(F32) + flip(half[0], "wshard", 2).astype(F32)
    return lax.psum(jnp.concatenate([rows[1], rows[0]], axis=0), "expert")


def expand(rows, images):
    return jnp.pad(rows.reshape(images, SEQ, -1), ((0, 0), (0, PAD - SEQ), (0, 0))).reshape(images * PAD, -1)


def contract(rows, images):
    return rows.reshape(images, PAD, -1)[:, :SEQ].reshape(images * SEQ, -1)


def local(
    images, attn_in, attn_out, norm_gains, mlp_in, mlp_out, router, expert_in, expert_out, expert_ids, cotangent
):
    owners = lax.axis_size("expert")
    experts = owners * expert_in.shape[0]
    tokens = images.shape[0]
    pictures = tokens // SEQ
    rows = pictures * PAD
    capacity = max(2, 2 * TOP * tokens // experts)
    slots = (capacity + 8 + 15) // 16 * 16
    every = experts * slots
    linked = owners == LINKED
    own = lax.axis_index("expert") if linked else 0
    pos = jnp.stack([lax.axis_index("wshard"), own]).astype(jnp.int32)

    small = jnp.concatenate([norm_gains, router.T], axis=0)
    small = jnp.pad(small, ((0, -small.shape[0] % 16), (0, 0)))
    (small_full,) = call(
        small_kernel, [((small.shape[0], D), F32)], pos, *gather_pieces(small), specs=[SCALAR] + [WHOLE] * 4
    )
    gains = [small_full[i : i + 1] for i in range(4)]
    router_full = small_full[4 : 4 + experts]

    wi0 = flip(attn_in[0], "wshard", 2)
    wo0 = flip(attn_out[0], "wshard", 2)
    w1_across = flip(after(mlp_in, wi0), "wshard", 2)
    w2_across = flip(after(mlp_out, wo0), "wshard", 2)
    wi1 = flip(after(attn_in[1], w1_across), "wshard", 2)
    wo1 = flip(after(attn_out[1], w1_across), "wshard", 2)
    wi = [gather_pieces(attn_in[0], wi0), None]
    wo = [gather_pieces(attn_out[0], wo0), None]

    ids = jnp.pad(expert_ids.T.reshape(TOP, pictures, SEQ), ((0, 8 - TOP), (0, 0), (0, PAD - SEQ)), constant_values=-1)
    ids = ids.reshape(8, rows)
    cot = expand(cotangent, pictures)
    x0 = expand(images, pictures)

    index, g_out = call(
        functools.partial(routing_kernel, slots), [((8, rows), jnp.int32), ((every, D), BF16)], ids, cot, us=3.4
    )
    turned = index.T
    trade = functools.partial(lax.all_to_all, axis_name="expert", split_axis=0, concat_axis=0, tiled=True)
    g_in = trade(g_out.reshape(experts, slots, D))

    weight_specs = [AWAY] * 8
    attn_scratch = [pltpu.VMEM((4, D // 4, 3 * D), BF16), pltpu.VMEM((4, D // 4, D), BF16)]
    mlp_scratch = [pltpu.VMEM((4, D // 4, FF), BF16), pltpu.VMEM((4, FF // 4, D), BF16)]
    sems = pltpu.SemaphoreType.DMA((8,))

    def attend(x, layer):
        return call(
            attend_forward_kernel,
            [((rows, D), F32), ((rows, 3 * D), BF16), ((rows, D), BF16)],
            pos, x, gains[2 * layer], *wi[layer], *wo[layer],
            specs=[SCALAR, WHOLE, WHOLE] + weight_specs,
            scratch=attn_scratch + [sems],
            us=7.0,
        )

    def attend_back(x, layer, packed, o, dz, extra):
        wide = 4 * D
        if extra:
            wide += (sum(a.shape[0] for a in extra) + 1 + STRIP - 1) // STRIP * 128
        return call(
            functools.partial(attend_backward_kernel, len(extra)),
            [((rows, D), F32), ((1, D), F32), ((2, 2, 64, wide), BF16), ((2, 2, 64, wide), BF16)],
            pos, x, gains[2 * layer], packed, o, dz, *wi[layer], *wo[layer], *extra,
            specs=[SCALAR] + [WHOLE] * 5 + weight_specs + [WHOLE] * len(extra),
            scratch=attn_scratch
            + [pltpu.VMEM((rows, 3 * D), BF16)]
            + [pltpu.VMEM((rows, D), BF16)] * 3
            + [sems],
            us=12.5,
        )

    x1, packed1, o1 = attend(x0, 0)
    w1 = gather_pieces(mlp_in, after(w1_across, x1))
    w2 = gather_pieces(mlp_out, after(w2_across, x1))
    (x2,) = call(
        feed_forward_kernel, [((rows, D), F32)], pos, x1, gains[1], *w1, *w2,
        specs=[SCALAR, WHOLE, WHOLE] + weight_specs, scratch=mlp_scratch + [sems], us=6.5,
    )
    wi[1] = gather_pieces(attn_in[1], after(wi1, x2))
    wo[1] = gather_pieces(attn_out[1], after(wo1, x2))
    x3, packed2, o2 = attend(x2, 1)
    arrays = experts if linked else max(1, experts // (2 * PAD // slots))
    each = experts // arrays
    c, gate, *c_out = call(
        functools.partial(dispatch_kernel, slots),
        [((rows, D), BF16), ((8, rows), F32)] + [((each * slots, D), BF16)] * arrays,
        pos, x3, gains[3], router_full, ids, index,
        specs=[SCALAR] + [WHOLE] * 5,
        us=4.6,
    )

    def swap(blocks, first=0):
        if linked:
            return [flip(block, "expert", k) if k else block for k, block in enumerate(blocks, first)]
        moved = trade(jnp.concatenate(blocks).reshape(experts, slots, D))
        return list(moved.reshape(arrays, each * slots, D))

    c_in = swap(c_out)
    per = 2 if linked else 1
    work = []
    dc_out, z_out, dc_in = [], [], []
    for first in range(0, arrays, per):
        given = c_in[first : first + per]
        if linked and first >= 2 * per:
            given[0], *dc_in[-2 * per : -per] = lax.optimization_barrier((given[0], *dc_in[-2 * per : -per]))
        count = list(range(first * each, (first + per) * each))
        tall = len(count) * slots
        fixed = lambda *shape: pl.BlockSpec(shape, lambda j, pos_ref: (0,) * len(shape))
        source = lambda k: pl.BlockSpec((1, slots, D), lambda j, pos_ref: (pos_ref[1] ^ k, 0, 0))
        across = lambda height: pl.BlockSpec((height, CHUNK), lambda j, pos_ref: (0, j))
        *made, f, dh, dy = pl.pallas_call(
            functools.partial(experts_kernel, slots, per, each),
            out_shape=[jax.ShapeDtypeStruct((each * slots, D), BF16)] * (2 * per)
            + [jax.ShapeDtypeStruct((tall, FF), BF16)] * 2
            + [jax.ShapeDtypeStruct((tall, D), BF16)],
            grid_spec=pltpu.PrefetchScalarGridSpec(
                num_scalar_prefetch=1,
                grid=(FF // CHUNK,),
                in_specs=[across(D), pl.BlockSpec((CHUNK, D), lambda j, pos_ref: (j, 0))]
                + [source(k) for k in count]
                + [fixed(each * slots, D)] * per,
                out_specs=[fixed(each * slots, D)] * (2 * per) + [across(tall)] * 2 + [fixed(tall, D)],
                scratch_shapes=[pltpu.VMEM((tall, 128), F32), pltpu.VMEM((tall, D), F32), pltpu.VMEM((tall, D), F32)],
            ),
            cost_estimate=spent(8.0),
            compiler_params=pltpu.CompilerParams(vmem_limit_bytes=VMEM_LIMIT),
        )(pos, expert_in[0], expert_out[0], *[g_in] * len(count), *given)
        dc_out += made[:per]
        z_out += made[per:]
        if linked:
            dc_in += swap(made[:per], first)
        work.append((f, dh, dy))
    if not linked:
        dc_in = swap(dc_out)
    if linked:
        (z_block,) = call(
            arrange_kernel, [((experts, slots, D), BF16)], pos, *z_out, specs=[SCALAR] + [WHOLE] * experts, us=2.0
        )
    else:
        z_block = jnp.concatenate(z_out).reshape(experts, slots, D)
    n = len(work)
    whole_rows = lambda a: pl.BlockSpec(a.shape, lambda j: (0, 0))
    chunk = lambda a: pl.BlockSpec((a.shape[0], CHUNK), lambda j: (0, j))
    fs, dhs, dys = ([w[i] for w in work] for i in range(3))
    if linked:
        dys[0], *dc_in[per : 2 * per] = lax.optimization_barrier((dys[0], *dc_in[per : 2 * per]))
    grad_send, grad_keep = pl.pallas_call(
        functools.partial(expert_grads_kernel, n),
        grid=(FF // CHUNK,),
        in_specs=[SCALAR]
        + [whole_rows(a) for a in c_in]
        + [chunk(a) for a in fs + dhs]
        + [whole_rows(a) for a in dys],
        out_specs=[pl.BlockSpec((512, CHUNK), lambda j: (0, j))] * 2,
        out_shape=[jax.ShapeDtypeStruct((512, FF), BF16)] * 2,
        cost_estimate=spent(10.0),
        compiler_params=pltpu.CompilerParams(vmem_limit_bytes=VMEM_LIMIT),
    )(pos, *c_in, *fs, *dhs, *dys)
    add = lambda a, b: (a.astype(F32) + b.astype(F32)).astype(BF16)

    x3_late, z_block, grad_send, grad_keep = lax.optimization_barrier((x3, z_block, grad_send, grad_keep))
    g3, gain3, drouter = call(
        functools.partial(combine_kernel, slots),
        [((rows, D), F32), ((1, D), F32), ((experts, D), F32)],
        pos, x3_late, gains[3], router_full, ids, index, turned, c, gate, cot, *dc_in,
        specs=[SCALAR] + [WHOLE] * (9 + arrays),
        us=5.5,
    )
    g3, z_block, grad_send = lax.optimization_barrier((g3, z_block, grad_send))
    z_in = trade(z_block)
    grads = add(grad_keep, flip(grad_send, "wshard", 1))
    g3, grads = lax.optimization_barrier((g3, grads))
    crossed = [flip(grads[at], "wshard", 2) for at in (slice(0, 160), slice(160, 352), slice(352, 512))]
    g2, gain2, *second = attend_back(x2, 1, packed2, o2, g3, [])
    g2, crossed[0] = lax.optimization_barrier((g2, crossed[0]))
    g1, gain1, *mlp = call(
        feed_backward_kernel,
        [((rows, D), F32), ((1, D), F32)] + [((2, 2, 128, FF), BF16)] * 2,
        pos, x1, gains[1], g2, *w1, *w2,
        specs=[SCALAR, WHOLE, WHOLE, WHOLE] + weight_specs,
        scratch=mlp_scratch + [pltpu.VMEM((D, FF), BF16), pltpu.VMEM((FF, D), BF16), sems],
        us=12.5,
    )
    *second, mlp[0], mlp[1], crossed[1] = lax.optimization_barrier((*second, mlp[0], mlp[1], crossed[1]))
    if linked:
        square = split_square(pos, [second, mlp], True)
        g1, z_in, crossed[2], *square = lax.optimization_barrier((g1, z_in, crossed[2], *square))
        square = trade_square(square[0])
    dx, _, *first = attend_back(x0, 0, packed1, o1, g1, [gain1, gain2, gain3, drouter])
    (final,) = call(final_kernel, [((rows, D), BF16)], z_in.reshape(every, D), x3, turned, us=3.5)

    grads = add(grads, jnp.concatenate(crossed))
    expert1, expert2 = call(
        join_kernel,
        [((D, FF), F32), ((FF, D), F32)],
        pos, grads, flip(grads, "wshard", 1),
        specs=[SCALAR] + [WHOLE] * 2,
        us=4.0,
    )

    wide = first[0].shape[-1]
    if linked:
        tail = split_square(pos, [first], False)
        square, *tail = lax.optimization_barrier((square, *tail))
        bulk = trade_depth(sum_square(square))
        tail = cross_square(pos, *tail)
        bulk, *tail = lax.optimization_barrier((bulk, *tail))
        bulk = sum_depth(bulk)
        tail = cross_depth(tail)
        bulk, tail = lax.optimization_barrier((bulk, tail))
        bulk = trade_depth(bulk)
        tail = spread(tail)
        bulk = [bulk, flip(bulk, "expert", 1)]
        mlp1, mlp2 = call(
            finish_mlp_kernel,
            [((D // 4, FF), F32), ((4, 128, D), F32)],
            pos, *bulk, specs=[SCALAR] + [WHOLE] * 2, us=2.0,
        )
        grad_in, grad_out, smalls = call(
            finish_attention_kernel,
            [((2, D // 4, 3 * D), F32), ((2, D // 4, D), F32), (((wide - 4 * D) // 128 * STRIP, 128), F32)],
            pos, *tail, *bulk, specs=[SCALAR] + [WHOLE] * 10, us=2.0,
        )
        mlp2 = mlp2.reshape(FF // 4, D)
    else:
        first, second, mlp = sum_plainly(*first), sum_plainly(*second), sum_plainly(*mlp)
        grad_in = jnp.stack([first[:, : 3 * D], second[:, : 3 * D]])
        grad_out = jnp.stack([first[:, 3 * D : 4 * D], second[:, 3 * D :]])
        smalls = first[:STRIP, 4 * D :].reshape(STRIP, -1, 128).transpose(1, 0, 2).reshape(-1, 128)
        mlp1 = jnp.concatenate([mlp[0:64], mlp[128:192]], axis=0)
        mlp2 = jnp.stack([mlp[64:128], mlp[192:256]]).reshape(2, 64, 4, D).transpose(2, 0, 1, 3).reshape(FF // 4, D)

    return (
        contract(final, pictures),
        contract(dx, pictures),
        grad_in,
        grad_out,
        smalls[0:4],
        mlp1,
        mlp2,
        smalls[4 : 4 + experts].T,
        expert1[None],
        expert2[None],
    )


def solution(mesh):
    rows = P(("expert", "wshard"), None)
    dense = (P(None, "wshard", None), P(None, "wshard", None), P(None, "wshard"))
    shards = (P("wshard", None),) * 3
    experts = (P("expert", None, None),) * 2
    return jax.shard_map(
        local,
        mesh=mesh,
        in_specs=(rows, *dense, *shards, *experts, rows, rows),
        out_specs=(rows, rows, *dense, *shards, *experts),
        check_vma=False,
    )
```

```python
import functools

import jax
import jax.numpy as jnp
from jax import lax
from jax.experimental import pallas as pl
from jax.experimental.pallas import tpu as pltpu
from jax.sharding import PartitionSpec as P

D = 512
HEADS = 8
FF = 2048
SEQ = 197
TOP = 2
HEAD_DIM = 64
PAD = 208
STRIP = 32
CHUNK = 512
EPSILON = 1e-06
ROOT_2_PI = 0.7978845608028654
CUBIC = 0.044715

F32 = jnp.float32
BF16 = jnp.bfloat16
VMEM_LIMIT = 40 * 1024 * 1024
LINKED = 8


def dot(a, b, ca=1, cb=0):
    return lax.dot_general(a, b, (((ca,), (cb,)), ((), ())), preferred_element_type=F32)


def unit_rows(rows):
    centred = rows - jnp.mean(rows, axis=-1, keepdims=True)
    scale = lax.rsqrt(jnp.mean(centred * centred, axis=-1, keepdims=True) + EPSILON)
    return centred * scale, scale


def norm_backward(unit, scale, gain, grad):
    scaled = gain * grad
    inner = (
        scaled
        - jnp.mean(scaled, axis=-1, keepdims=True)
        - unit * jnp.mean(scaled * unit, axis=-1, keepdims=True)
    )
    return inner * scale, jnp.sum(grad * unit, axis=0, keepdims=True)


def gelu_parts(h):
    square = h * h
    t = jnp.tanh(ROOT_2_PI * h * (1.0 + CUBIC * square))
    half = 0.5 * (1.0 + t)
    slope = half + 0.5 * h * (1.0 - t * t) * (ROOT_2_PI * (1.0 + 3.0 * CUBIC * square))
    return h * half, slope


def gelu(h):
    return 0.5 * h * (1.0 + jnp.tanh(ROOT_2_PI * h * (1.0 + CUBIC * h * h)))


def start_weight(pos_ref, pieces, held, sems, first):
    copies = []
    for j, piece in enumerate(pieces):
        copy = pltpu.make_async_copy(piece, held.at[pos_ref[0] ^ j], sems.at[first + j])
        copy.start()
        copies.append(copy)
    return copies


def wait_all(copies):
    for copy in copies:
        copy.wait()


def softmax_rows(q, k):
    scores = dot(q, k, 1, 1) * (HEAD_DIM**-0.5)
    column = lax.broadcasted_iota(jnp.int32, scores.shape, 1)
    scores = jnp.where(column < SEQ, scores, -1e30)
    raised = jnp.exp(scores - jnp.max(scores, axis=-1, keepdims=True))
    return raised * (1.0 / jnp.sum(raised, axis=-1, keepdims=True))


def shards_of(pos_ref, send_ref, keep_ref):
    for target, turn in ((send_ref, 1), (keep_ref, 0)):
        for place in range(2):
            yield target, place, pos_ref[0] ^ (turn + 2 * (1 - place))


def own_half(pos_ref, half):
    return 1 - ((pos_ref[1] & 1) ^ half)


def attend_forward_kernel(pos_ref, x_ref, gain_ref, *refs):
    wi, wo = refs[0:4], refs[4:8]
    y_ref, packed_ref, o_ref, wi_held, wo_held, sems = refs[8:]
    wi_copies = start_weight(pos_ref, wi, wi_held, sems, 0)
    wo_copies = start_weight(pos_ref, wo, wo_held, sems, 4)
    rows = x_ref[...].astype(F32)
    unit, _ = unit_rows(rows)
    normed = (unit * gain_ref[...]).astype(BF16)
    wait_all(wi_copies)
    packed_ref[...] = dot(normed, wi_held[...].reshape(D, 3 * D)).astype(BF16)
    lane = lax.broadcasted_iota(jnp.int32, (PAD, 2 * HEAD_DIM), 1)
    for image in range(x_ref.shape[0] // PAD):
        here = pl.ds(image * PAD, PAD)
        for pair in range(HEADS // 2):
            at = pair * 2 * HEAD_DIM
            q = packed_ref[here, at : at + 128]
            k = packed_ref[here, D + at : D + at + 128]
            v = packed_ref[here, 2 * D + at : 2 * D + at + 128]
            total = None
            for side in range(2):
                mine = (lane >= HEAD_DIM) == bool(side)
                chances = softmax_rows(jnp.where(mine, q, jnp.zeros_like(q)), k).astype(BF16)
                part = dot(chances, jnp.where(mine, v, jnp.zeros_like(v)))
                total = part if total is None else total + part
            o_ref[here, at : at + 128] = total.astype(BF16)
    wait_all(wo_copies)
    y_ref[...] = x_ref[...].astype(F32) + dot(o_ref[...], wo_held[...].reshape(D, D))


def attend_backward_kernel(smalls, pos_ref, x_ref, gain_ref, packed_ref, o_ref, dz_ref, *refs):
    wi, wo = refs[0:4], refs[4:8]
    extra = refs[8 : 8 + smalls]
    dx_ref, dgain_ref, send_ref, keep_ref, wi_held, wo_held, dp_ref, dout_ref, do_ref, normed_ref, sems = refs[
        8 + smalls :
    ]
    wo_copies = start_weight(pos_ref, wo, wo_held, sems, 4)
    wi_copies = start_weight(pos_ref, wi, wi_held, sems, 0)
    unit, scale = unit_rows(x_ref[...].astype(F32))
    gain = gain_ref[...]
    normed_ref[...] = (unit * gain).astype(BF16)
    dout_ref[...] = dz_ref[...].astype(BF16)
    wait_all(wo_copies)
    do_ref[...] = dot(dout_ref[...], wo_held[...].reshape(D, D), 1, 1).astype(BF16)
    lane = lax.broadcasted_iota(jnp.int32, (PAD, 2 * HEAD_DIM), 1)
    factor = HEAD_DIM**-0.5
    for image in range(x_ref.shape[0] // PAD):
        here = pl.ds(image * PAD, PAD)
        for pair in range(HEADS // 2):
            at = pair * 2 * HEAD_DIM
            q = packed_ref[here, at : at + 128]
            k = packed_ref[here, D + at : D + at + 128]
            v = packed_ref[here, 2 * D + at : 2 * D + at + 128]
            do = do_ref[here, at : at + 128]
            dq = dk = dv = None
            for side in range(2):
                mine = (lane >= HEAD_DIM) == bool(side)
                own = lambda a: jnp.where(mine, a, jnp.zeros_like(a))
                q_own, k_own, do_own = own(q), own(k), own(do)
                chances = softmax_rows(q_own, k)
                dv_part = dot(chances.astype(BF16), do_own, 0, 0)
                da = dot(do_own, v, 1, 1)
                ds = chances * (da - jnp.sum(da * chances, axis=-1, keepdims=True))
                ds = ds.astype(BF16)
                dq_part = dot(ds, k_own)
                dk_part = dot(ds, q_own, 0, 0)
                dq = dq_part if dq is None else dq + dq_part
                dk = dk_part if dk is None else dk + dk_part
                dv = dv_part if dv is None else dv + dv_part
            dp_ref[here, at : at + 128] = (dq * factor).astype(BF16)
            dp_ref[here, D + at : D + at + 128] = (dk * factor).astype(BF16)
            dp_ref[here, 2 * D + at : 2 * D + at + 128] = dv.astype(BF16)
    wait_all(wi_copies)
    dn = dot(dp_ref[...], wi_held[...].reshape(D, 3 * D), 1, 1)
    unit, scale = unit_rows(x_ref[...].astype(F32))
    dx, dgain = norm_backward(unit, scale, gain, dn)
    dx_ref[...] = dz_ref[...] + dx
    dgain_ref[...] = dgain
    for target, place, shard in shards_of(pos_ref, send_ref, keep_ref):
        columns = pl.ds(pl.multiple_of(shard * 128, 128), 128)
        grad_in = dot(normed_ref[:, columns], dp_ref[...], 0, 0).astype(BF16)
        grad_out = dot(o_ref[:, columns], dout_ref[...], 0, 0).astype(BF16)
        for half in range(2):
            there = own_half(pos_ref, half)
            target[place, there, :, 0 : 3 * D] = grad_in[half * 64 : half * 64 + 64]
            target[place, there, :, 3 * D : 4 * D] = grad_out[half * 64 : half * 64 + 64]
    if smalls:
        small = jnp.concatenate([dgain] + [ref[...] for ref in extra], axis=0)
        small = jnp.concatenate([small, jnp.zeros((-small.shape[0] % STRIP, D), F32)], axis=0)
        for target, place, shard in shards_of(pos_ref, send_ref, keep_ref):
            piece = jnp.zeros((small.shape[0], 128), F32)
            for s in range(4):
                piece = jnp.where(shard == s, small[:, s * 128 : (s + 1) * 128], piece)
            piece = piece.astype(BF16)
            for half in range(2):
                for strip in range(64 // STRIP):
                    for group in range(small.shape[0] // STRIP):
                        at = 4 * D + group * 128
                        target[place, half, strip * STRIP : (strip + 1) * STRIP, at : at + 128] = piece[
                            group * STRIP : (group + 1) * STRIP
                        ]


def feed_forward_kernel(pos_ref, x_ref, gain_ref, *refs):
    w1, w2 = refs[0:4], refs[4:8]
    y_ref, w1_held, w2_held, sems = refs[8:]
    w1_copies = start_weight(pos_ref, w1, w1_held, sems, 0)
    w2_copies = start_weight(pos_ref, w2, w2_held, sems, 4)
    unit, _ = unit_rows(x_ref[...])
    normed = (unit * gain_ref[...]).astype(BF16)
    wait_all(w1_copies)
    total = x_ref[...]
    for j in range(FF // CHUNK):
        at = slice(j * CHUNK, (j + 1) * CHUNK)
        active = gelu(dot(normed, w1_held[:, :, at].reshape(D, CHUNK))).astype(BF16)
        if j == 0:
            wait_all(w2_copies)
        total = total + dot(active, w2_held[...].reshape(FF, D)[at])
    y_ref[...] = total


def feed_backward_kernel(pos_ref, x_ref, gain_ref, dz_ref, *refs):
    w1, w2 = refs[0:4], refs[4:8]
    dx_ref, dgain_ref, send_ref, keep_ref, w1_held, w2_held, g1_ref, g2_ref, sems = refs[8:]
    w1_copies = start_weight(pos_ref, w1, w1_held, sems, 0)
    w2_copies = start_weight(pos_ref, w2, w2_held, sems, 4)
    unit, scale = unit_rows(x_ref[...])
    gain = gain_ref[...]
    normed = (unit * gain).astype(BF16)
    dout = dz_ref[...].astype(BF16)
    wait_all(w1_copies)
    wait_all(w2_copies)
    dn = None
    for j in range(FF // CHUNK):
        at = slice(j * CHUNK, (j + 1) * CHUNK)
        w1_now = w1_held[:, :, at].reshape(D, CHUNK)
        w2_now = w2_held[...].reshape(FF, D)[at]
        active, slope = gelu_parts(dot(normed, w1_now))
        dh = (slope * dot(dout, w2_now, 1, 1)).astype(BF16)
        g2_ref[at] = dot(active.astype(BF16), dout, 0, 0).astype(BF16)
        g1_ref[:, at] = dot(normed, dh, 0, 0).astype(BF16)
        part = dot(dh, w1_now, 1, 1)
        dn = part if dn is None else dn + part
    dx, dgain = norm_backward(unit, scale, gain, dn)
    dx_ref[...] = dz_ref[...] + dx
    dgain_ref[...] = dgain
    for target, place, shard in shards_of(pos_ref, send_ref, keep_ref):
        for half in range(2):
            there = own_half(pos_ref, half)
            target[place, there, 0:64] = g1_ref[pl.ds(pl.multiple_of(shard * 128 + half * 64, 64), 64)]
            for part in range(4):
                start = pl.multiple_of(shard * 512 + part * 128 + half * 64, 64)
                target[place, there, 64:128, part * 512 : (part + 1) * 512] = g2_ref[pl.ds(start, 64)]


def routing_kernel(slots, ids_ref, cot_ref, index_ref, blocks_ref):
    experts = blocks_ref.shape[0] // slots
    tokens = ids_ref.shape[1]
    expert = lax.broadcasted_iota(jnp.int32, (experts, tokens), 0)
    named = [ids_ref[k : k + 1, :] == expert for k in range(TOP)]
    matches = jnp.where(named[0] | named[1], 1.0, 0.0).astype(BF16)
    earlier = lax.broadcasted_iota(jnp.int32, (tokens, tokens), 0) < lax.broadcasted_iota(
        jnp.int32, (tokens, tokens), 1
    )
    rank = dot(matches, jnp.where(earlier, 1.0, 0.0).astype(BF16))
    index_ref[...] = jnp.full(index_ref.shape, -1, jnp.int32)
    place = lax.broadcasted_iota(jnp.int32, (blocks_ref.shape[0], tokens), 0)
    chosen = None
    for k in range(TOP):
        slot = jnp.sum(jnp.where(named[k], rank, 0.0), axis=0, keepdims=True).astype(jnp.int32)
        index = ids_ref[k : k + 1, :] * slots + slot
        index_ref[k : k + 1, :] = index
        hit = place == index
        chosen = hit if chosen is None else chosen | hit
    blocks_ref[...] = dot(jnp.where(chosen, 1.0, 0.0).astype(BF16), cot_ref[...]).astype(BF16)


def write_spare(slots, column):
    eye = lax.broadcasted_iota(jnp.int32, (slots, D), 0) == lax.broadcasted_iota(jnp.int32, (slots, D), 1)
    line = jnp.sum(jnp.where(eye, column, 0.0), axis=0, keepdims=True)
    high = line.astype(BF16).astype(F32)
    middle = (line - high).astype(BF16).astype(F32)
    low = line - high - middle
    row = lax.broadcasted_iota(jnp.int32, (8, D), 0)
    return jnp.where(row == 0, high, jnp.where(row == 1, middle, jnp.where(row == 2, low, 0.0)))


def read_spare(tile, slots):
    line = tile[0:1] + tile[1:2] + tile[2:3]
    eye = lax.broadcasted_iota(jnp.int32, (slots, D), 0) == lax.broadcasted_iota(jnp.int32, (slots, D), 1)
    return jnp.sum(jnp.where(eye, line, 0.0), axis=1, keepdims=True)


def small_kernel(pos_ref, *refs):
    out_ref = refs[4]
    for j in range(4):
        start = pl.multiple_of((pos_ref[0] ^ j) * 128, 128)
        out_ref[:, pl.ds(start, 128)] = refs[j][...].astype(F32)


def dispatch_kernel(slots, pos_ref, x_ref, gain_ref, router_ref, ids_ref, index_ref, c_ref, gate_ref, *blocks):
    tokens = x_ref.shape[0]
    each = blocks[0].shape[0] // slots
    experts = len(blocks) * each
    unit, _ = unit_rows(x_ref[...])
    c = (unit * gain_ref[...]).astype(BF16)
    c_ref[...] = c
    logits = dot(router_ref[...].astype(BF16), c, 1, 1)
    expert = lax.broadcasted_iota(jnp.int32, (experts, tokens), 0)
    picked = [
        jnp.sum(jnp.where(ids_ref[k : k + 1, :] == expert, logits, 0.0), axis=0, keepdims=True) for k in range(TOP)
    ]
    gates = [0.5 + 0.5 * jnp.tanh(0.5 * (picked[k] - picked[1 - k])) for k in range(TOP)]
    gate_ref[...] = jnp.concatenate(gates + [jnp.zeros((8 - TOP, tokens), F32)], axis=0)
    for k in range(experts):
        place = lax.broadcasted_iota(jnp.int32, (slots, tokens), 0) + (pos_ref[1] ^ k) * slots
        hits = [place == index_ref[k : k + 1, :] for k in range(TOP)]
        rows = dot(jnp.where(hits[0] | hits[1], 1.0, 0.0).astype(BF16), c)
        weight = sum(jnp.where(hits[k], gates[k], 0.0) for k in range(TOP))
        tile = write_spare(slots, jnp.sum(weight, axis=1, keepdims=True))
        at = k % each * slots
        blocks[k // each][at : at + slots] = jnp.concatenate([rows[: slots - 8], tile], axis=0).astype(BF16)


def experts_kernel(slots, n, each, pos_ref, w1_ref, w2_ref, *refs):
    g_refs, c_refs, refs = refs[: n * each], refs[n * each : n * each + n], refs[n * each + n :]
    dc_refs, z_refs = refs[:n], refs[n : 2 * n]
    f_ref, dh_ref, dy_ref, gate_ref, y_ref, dc_ref = refs[2 * n :]
    step = pl.program_id(0)
    blocks = [(b, slice(b * slots, (b + 1) * slots)) for b in range(n * each)]

    @pl.when(step == 0)
    def _():
        for b, here in blocks:
            end = (b % each + 1) * slots
            gate = read_spare(c_refs[b // each][end - 8 : end].astype(F32), slots)
            gate_ref[here] = jnp.broadcast_to(gate, (slots, 128))
            dy_ref[here] = (gate * g_refs[b][0].astype(F32)).astype(BF16)

    c = c_refs[0][...] if n == 1 else jnp.concatenate([ref[...] for ref in c_refs], axis=0)
    active, slope = gelu_parts(dot(c, w1_ref[...]))
    active = active.astype(BF16)
    f_ref[...] = active
    dh = (slope * dot(dy_ref[...], w2_ref[...], 1, 1)).astype(BF16)
    dh_ref[...] = dh
    y = dot(active, w2_ref[...])
    dc = dot(dh, w1_ref[...], 1, 1)

    @pl.when(step == 0)
    def _():
        y_ref[...] = y
        dc_ref[...] = dc

    @pl.when(step > 0)
    def _():
        y_ref[...] += y
        dc_ref[...] += dc

    @pl.when(step == pl.num_programs(0) - 1)
    def _():
        for b, here in blocks:
            there = slice(b % each * slots, (b % each + 1) * slots)
            rounded = y_ref[here].astype(BF16).astype(F32)
            dgate = jnp.sum(g_refs[b][0].astype(F32) * rounded, axis=1, keepdims=True)
            z_refs[b // each][there] = (gate_ref[here, 0:1] * rounded).astype(BF16)
            rows = jnp.concatenate([dc_ref[here][: slots - 8], write_spare(slots, dgate)], axis=0)
            dc_refs[b // each][there] = rows.astype(BF16)


def expert_grads_kernel(n, pos_ref, *refs):
    m = len(refs) - 2 - 3 * n
    c_refs = refs[:m]
    f_refs, dh_refs, dy_refs = refs[m : m + n], refs[m + n : m + 2 * n], refs[m + 2 * n : m + 3 * n]
    send_ref, keep_ref = refs[m + 3 * n :]
    per = m // n
    for target, half in ((send_ref, 1 - (pos_ref[0] & 1)), (keep_ref, pos_ref[0] & 1)):
        at = pl.ds(pl.multiple_of(half * 256, 256), 256)
        total1 = total2 = None
        for i in range(n):
            c = [ref[:, at] for ref in c_refs[i * per : (i + 1) * per]]
            c = c[0] if per == 1 else jnp.concatenate(c, axis=0)
            part1 = dot(c, dh_refs[i][...], 0, 0)
            part2 = dot(f_refs[i][...], dy_refs[i][:, at], 0, 0)
            total1 = part1 if total1 is None else total1 + part1
            total2 = part2 if total2 is None else total2 + part2
        target[0:256] = total1.astype(BF16)
        target[256:512, 0:256] = total2[0:256].astype(BF16)
        target[256:512, 256:512] = total2[256:512].astype(BF16)


def join_kernel(pos_ref, own_ref, other_ref, out1_ref, out2_ref):
    core = pos_ref[0] & 1
    for mine, ref in ((core, own_ref), (1 - core, other_ref)):
        at = pl.ds(pl.multiple_of(mine * 256, 256), 256)
        out1_ref[at] = ref[0:256].astype(F32)
        for block in range(FF // 256):
            out2_ref[block * 256 : (block + 1) * 256, at] = ref[256:512, block * 256 : (block + 1) * 256].astype(F32)


def arrange_kernel(pos_ref, *refs):
    for k, ref in enumerate(refs[:-1]):
        refs[-1][pos_ref[1] ^ k] = ref[...]


def one_hot_columns(index_ref, width):
    place = lax.broadcasted_iota(jnp.int32, (index_ref.shape[0], width), 1)
    hit = (place == index_ref[:, 0:1]) | (place == index_ref[:, 1:2])
    return jnp.where(hit, 1.0, 0.0).astype(BF16)


def combine_kernel(
    slots, pos_ref, x_ref, gain_ref, router_ref, ids_ref, index_ref, turned_ref, c_ref, gate_ref, cot_ref, *refs
):
    blocks, (dx_ref, dgain_ref, drouter_ref) = refs[:-3], refs[-3:]
    each = blocks[0].shape[0] // slots
    experts = len(blocks) * each
    tokens = x_ref.shape[0]
    dgates = [jnp.zeros((1, tokens), F32) for _ in range(TOP)]
    gc = None
    for k in range(experts):
        at = k % each * slots
        block = blocks[k // each][at : at + slots]
        start = (pos_ref[1] ^ k) * slots
        place = lax.broadcasted_iota(jnp.int32, (tokens, slots), 1) + start
        hit = (place == turned_ref[:, 0:1]) | (place == turned_ref[:, 1:2])
        part = dot(jnp.where(hit, 1.0, 0.0).astype(BF16), block)
        gc = part if gc is None else gc + part
        place = lax.broadcasted_iota(jnp.int32, (slots, tokens), 0) + start
        column = read_spare(block[slots - 8 :].astype(F32), slots)
        for j in range(TOP):
            hit = place == index_ref[j : j + 1, :]
            dgates[j] = dgates[j] + jnp.sum(jnp.where(hit, column, 0.0), axis=0, keepdims=True)
    dl = gate_ref[0:1] * gate_ref[1:2] * (dgates[0] - dgates[1])
    expert = lax.broadcasted_iota(jnp.int32, (experts, tokens), 0)
    dlogits = jnp.where(ids_ref[0:1, :] == expert, dl, 0.0) - jnp.where(ids_ref[1:2, :] == expert, dl, 0.0)
    dlogits = dlogits.astype(BF16)
    gc = gc + dot(dlogits, router_ref[...].astype(BF16), 0, 0)
    drouter_ref[...] = dot(dlogits, c_ref[...])
    unit, scale = unit_rows(x_ref[...])
    dx, dgain = norm_backward(unit, scale, gain_ref[...], gc)
    dx_ref[...] = cot_ref[...].astype(F32) + dx
    dgain_ref[...] = dgain


def split_cube_kernel(n, pos_ref, *refs):
    kept, came, out_ref = refs[0:n], refs[n : 2 * n], refs[2 * n]
    for place in range(2):
        for half in range(2):
            x = (pos_ref[1] & 1) ^ (1 - half)
            y = (pos_ref[0] >> 1) ^ (1 - place)
            row = 0
            for keep, new in zip(kept, came):
                total = (keep[place, half].astype(F32) + new[place, half].astype(F32)).astype(BF16)
                for start in range(0, keep.shape[2], 64):
                    for depth in range(2):
                        at = start + depth * STRIP
                        out_ref[depth * 4 + x * 2 + y, row : row + STRIP] = total[at : at + STRIP]
                    row += STRIP


def sum_cube_kernel(a_ref, out_ref):
    total = a_ref[0].astype(F32)
    for k in range(1, a_ref.shape[0]):
        total = total + a_ref[k].astype(F32)
    out_ref[...] = total.astype(BF16)


def sum_kernel(*refs):
    total = refs[0][...].astype(F32)
    for ref in refs[1:-1]:
        total = total + ref[...].astype(F32)
    refs[-1][...] = total.astype(BF16)


def rows_of(pos_ref, k):
    source = pos_ref[1] ^ k
    return pl.ds(pl.multiple_of((source & 1) * 64 + (source >> 1 & 1) * STRIP, STRIP), STRIP)


def finish_mlp_kernel(pos_ref, *refs):
    mlp1_ref, mlp2_ref = refs[4:]
    for k in range(4):
        there = rows_of(pos_ref, k)
        mlp1_ref[there] = refs[k][STRIP : 2 * STRIP].astype(F32)
        for part in range(4):
            mlp2_ref[part, there] = refs[k][2 * STRIP :, part * 512 : (part + 1) * 512].astype(F32)


def finish_attention_kernel(pos_ref, *refs):
    in_ref, out_ref, small_ref = refs[8:]
    for k in range(4):
        there = rows_of(pos_ref, k)
        for layer, ref in ((0, refs[k]), (1, refs[4 + k])):
            in_ref[layer, there] = ref[0:STRIP, 0 : 3 * D].astype(F32)
            out_ref[layer, there] = ref[0:STRIP, 3 * D : 4 * D].astype(F32)
    for group in range(small_ref.shape[0] // STRIP):
        at = 4 * D + group * 128
        small_ref[group * STRIP : (group + 1) * STRIP] = refs[0][:, at : at + 128].astype(F32)


def final_kernel(blocks_ref, x_ref, turned_ref, out_ref):
    out_ref[...] = (x_ref[...] + dot(one_hot_columns(turned_ref, blocks_ref.shape[0]), blocks_ref[...])).astype(BF16)


def spent(us):
    return pl.CostEstimate(flops=int(us * 1.0e9), bytes_accessed=0, transcendentals=0)


def call(kernel, outs, *args, us=1.0, scratch=(), specs=None, **more):
    return list(
        pl.pallas_call(
        kernel,
        out_shape=[jax.ShapeDtypeStruct(shape, kind) for shape, kind in outs],
        in_specs=specs if specs is not None else [WHOLE] * len(args),
        out_specs=[WHOLE] * len(outs),
        scratch_shapes=list(scratch),
        cost_estimate=spent(us),
        compiler_params=pltpu.CompilerParams(vmem_limit_bytes=VMEM_LIMIT),
        **more,
        )(*args)
    )


WHOLE = pl.BlockSpec(memory_space=pltpu.VMEM)
SCALAR = pl.BlockSpec(memory_space=pltpu.SMEM)
AWAY = pl.BlockSpec(memory_space=pl.ANY)


def flip(array, axis, bit):
    return lax.ppermute(array, axis, [(i, i ^ bit) for i in range(lax.axis_size(axis))])


def gather_pieces(piece, across=None):
    across = flip(piece, "wshard", 2) if across is None else across
    return (piece, flip(piece, "wshard", 1), across, flip(across, "wshard", 1))


def after(array, *others):
    return lax.optimization_barrier((array, *others))[0]


def split_cube(pos, bundle):
    came = [flip(send, "wshard", 1) for send, _ in bundle]
    tall = sum(keep.shape[2] for _, keep in bundle)
    wide = bundle[0][0].shape[-1]
    return call(
        functools.partial(split_cube_kernel, len(bundle)),
        [((8, tall // 2, wide), BF16)],
        pos,
        *[keep for _, keep in bundle],
        *came,
        specs=[SCALAR] + [WHOLE] * (2 * len(bundle)),
        us=3.0,
    )[0]


def trade_cube(blocks):
    inner = lax.axis_size("wshard")
    groups = [
        [((2 * z + depth) * 2 + x) * inner + y * 2 + core for depth in range(2) for x in range(2) for y in range(2)]
        for z in range(lax.axis_size("expert") // 4)
        for core in range(2)
    ]
    return lax.all_to_all(blocks, ("expert", "wshard"), 0, 0, axis_index_groups=groups, tiled=True)


def sum_cube(blocks):
    return call(sum_cube_kernel, [(blocks.shape[1:], BF16)], blocks, us=2.0)[0]


def sum_two(strip, other):
    return call(sum_kernel, [(strip.shape, BF16)], strip, other)[0]


def spread(strip):
    return [strip] + [flip(strip, "expert", k) for k in range(1, 4)]


def sum_plainly(send, keep):
    half = (keep.astype(F32) + flip(send, "wshard", 1).astype(F32)).astype(BF16)
    rows = half[1].astype(F32) + flip(half[0], "wshard", 2).astype(F32)
    return lax.psum(jnp.concatenate([rows[1], rows[0]], axis=0), "expert")


def expand(rows, images):
    return jnp.pad(rows.reshape(images, SEQ, -1), ((0, 0), (0, PAD - SEQ), (0, 0))).reshape(images * PAD, -1)


def contract(rows, images):
    return rows.reshape(images, PAD, -1)[:, :SEQ].reshape(images * SEQ, -1)


def local(
    images, attn_in, attn_out, norm_gains, mlp_in, mlp_out, router, expert_in, expert_out, expert_ids, cotangent
):
    owners = lax.axis_size("expert")
    experts = owners * expert_in.shape[0]
    tokens = images.shape[0]
    pictures = tokens // SEQ
    rows = pictures * PAD
    capacity = max(2, 2 * TOP * tokens // experts)
    slots = (capacity + 8 + 15) // 16 * 16
    every = experts * slots
    linked = owners == LINKED
    own = lax.axis_index("expert") if linked else 0
    pos = jnp.stack([lax.axis_index("wshard"), own]).astype(jnp.int32)

    small = jnp.concatenate([norm_gains, router.T], axis=0)
    small = jnp.pad(small, ((0, -small.shape[0] % 16), (0, 0)))
    (small_full,) = call(
        small_kernel, [((small.shape[0], D), F32)], pos, *gather_pieces(small), specs=[SCALAR] + [WHOLE] * 4
    )
    gains = [small_full[i : i + 1] for i in range(4)]
    router_full = small_full[4 : 4 + experts]

    wi0 = flip(attn_in[0], "wshard", 2)
    wo0 = flip(attn_out[0], "wshard", 2)
    w1_across = flip(after(mlp_in, wi0), "wshard", 2)
    w2_across = flip(after(mlp_out, wo0), "wshard", 2)
    wi1 = flip(after(attn_in[1], w1_across), "wshard", 2)
    wo1 = flip(after(attn_out[1], w1_across), "wshard", 2)
    wi = [gather_pieces(attn_in[0], wi0), None]
    wo = [gather_pieces(attn_out[0], wo0), None]

    ids = jnp.pad(expert_ids.T.reshape(TOP, pictures, SEQ), ((0, 8 - TOP), (0, 0), (0, PAD - SEQ)), constant_values=-1)
    ids = ids.reshape(8, rows)
    cot = expand(cotangent, pictures)
    x0 = expand(images, pictures)

    index, g_out = call(
        functools.partial(routing_kernel, slots), [((8, rows), jnp.int32), ((every, D), BF16)], ids, cot, us=3.4
    )
    turned = index.T
    trade = functools.partial(lax.all_to_all, axis_name="expert", split_axis=0, concat_axis=0, tiled=True)
    g_in = trade(g_out.reshape(experts, slots, D))

    weight_specs = [AWAY] * 8
    attn_scratch = [pltpu.VMEM((4, D // 4, 3 * D), BF16), pltpu.VMEM((4, D // 4, D), BF16)]
    mlp_scratch = [pltpu.VMEM((4, D // 4, FF), BF16), pltpu.VMEM((4, FF // 4, D), BF16)]
    sems = pltpu.SemaphoreType.DMA((8,))

    def attend(x, layer):
        return call(
            attend_forward_kernel,
            [((rows, D), F32), ((rows, 3 * D), BF16), ((rows, D), BF16)],
            pos, x, gains[2 * layer], *wi[layer], *wo[layer],
            specs=[SCALAR, WHOLE, WHOLE] + weight_specs,
            scratch=attn_scratch + [sems],
            us=7.0,
        )

    def attend_back(x, layer, packed, o, dz, extra):
        wide = 4 * D
        if extra:
            wide += (sum(a.shape[0] for a in extra) + 1 + STRIP - 1) // STRIP * 128
        return call(
            functools.partial(attend_backward_kernel, len(extra)),
            [((rows, D), F32), ((1, D), F32), ((2, 2, 64, wide), BF16), ((2, 2, 64, wide), BF16)],
            pos, x, gains[2 * layer], packed, o, dz, *wi[layer], *wo[layer], *extra,
            specs=[SCALAR] + [WHOLE] * 5 + weight_specs + [WHOLE] * len(extra),
            scratch=attn_scratch
            + [pltpu.VMEM((rows, 3 * D), BF16)]
            + [pltpu.VMEM((rows, D), BF16)] * 3
            + [sems],
            us=12.5,
        )

    x1, packed1, o1 = attend(x0, 0)
    w1 = gather_pieces(mlp_in, after(w1_across, x1))
    w2 = gather_pieces(mlp_out, after(w2_across, x1))
    (x2,) = call(
        feed_forward_kernel, [((rows, D), F32)], pos, x1, gains[1], *w1, *w2,
        specs=[SCALAR, WHOLE, WHOLE] + weight_specs, scratch=mlp_scratch + [sems], us=6.5,
    )
    wi[1] = gather_pieces(attn_in[1], after(wi1, x2))
    wo[1] = gather_pieces(attn_out[1], after(wo1, x2))
    x3, packed2, o2 = attend(x2, 1)
    arrays = experts if linked else max(1, experts // (2 * PAD // slots))
    each = experts // arrays
    c, gate, *c_out = call(
        functools.partial(dispatch_kernel, slots),
        [((rows, D), BF16), ((8, rows), F32)] + [((each * slots, D), BF16)] * arrays,
        pos, x3, gains[3], router_full, ids, index,
        specs=[SCALAR] + [WHOLE] * 5,
        us=4.6,
    )

    def swap(blocks, first=0):
        if linked:
            return [flip(block, "expert", k) if k else block for k, block in enumerate(blocks, first)]
        moved = trade(jnp.concatenate(blocks).reshape(experts, slots, D))
        return list(moved.reshape(arrays, each * slots, D))

    c_in = swap(c_out)
    per = 2 if linked else 1
    work = []
    dc_out, z_out, dc_in = [], [], []
    for first in range(0, arrays, per):
        given = c_in[first : first + per]
        if linked and first >= 2 * per:
            given[0], *dc_in[-2 * per : -per] = lax.optimization_barrier((given[0], *dc_in[-2 * per : -per]))
        count = list(range(first * each, (first + per) * each))
        tall = len(count) * slots
        fixed = lambda *shape: pl.BlockSpec(shape, lambda j, pos_ref: (0,) * len(shape))
        source = lambda k: pl.BlockSpec((1, slots, D), lambda j, pos_ref: (pos_ref[1] ^ k, 0, 0))
        across = lambda height: pl.BlockSpec((height, CHUNK), lambda j, pos_ref: (0, j))
        *made, f, dh, dy = pl.pallas_call(
            functools.partial(experts_kernel, slots, per, each),
            out_shape=[jax.ShapeDtypeStruct((each * slots, D), BF16)] * (2 * per)
            + [jax.ShapeDtypeStruct((tall, FF), BF16)] * 2
            + [jax.ShapeDtypeStruct((tall, D), BF16)],
            grid_spec=pltpu.PrefetchScalarGridSpec(
                num_scalar_prefetch=1,
                grid=(FF // CHUNK,),
                in_specs=[across(D), pl.BlockSpec((CHUNK, D), lambda j, pos_ref: (j, 0))]
                + [source(k) for k in count]
                + [fixed(each * slots, D)] * per,
                out_specs=[fixed(each * slots, D)] * (2 * per) + [across(tall)] * 2 + [fixed(tall, D)],
                scratch_shapes=[pltpu.VMEM((tall, 128), F32), pltpu.VMEM((tall, D), F32), pltpu.VMEM((tall, D), F32)],
            ),
            cost_estimate=spent(8.0),
            compiler_params=pltpu.CompilerParams(vmem_limit_bytes=VMEM_LIMIT),
        )(pos, expert_in[0], expert_out[0], *[g_in] * len(count), *given)
        dc_out += made[:per]
        z_out += made[per:]
        if linked:
            dc_in += swap(made[:per], first)
        work.append((f, dh, dy))
    if not linked:
        dc_in = swap(dc_out)
    if linked:
        (z_block,) = call(
            arrange_kernel, [((experts, slots, D), BF16)], pos, *z_out, specs=[SCALAR] + [WHOLE] * experts, us=2.0
        )
    else:
        z_block = jnp.concatenate(z_out).reshape(experts, slots, D)
    n = len(work)
    whole_rows = lambda a: pl.BlockSpec(a.shape, lambda j: (0, 0))
    chunk = lambda a: pl.BlockSpec((a.shape[0], CHUNK), lambda j: (0, j))
    fs, dhs, dys = ([w[i] for w in work] for i in range(3))
    if linked:
        dys[0], *dc_in[per : 2 * per] = lax.optimization_barrier((dys[0], *dc_in[per : 2 * per]))
    grad_send, grad_keep = pl.pallas_call(
        functools.partial(expert_grads_kernel, n),
        grid=(FF // CHUNK,),
        in_specs=[SCALAR]
        + [whole_rows(a) for a in c_in]
        + [chunk(a) for a in fs + dhs]
        + [whole_rows(a) for a in dys],
        out_specs=[pl.BlockSpec((512, CHUNK), lambda j: (0, j))] * 2,
        out_shape=[jax.ShapeDtypeStruct((512, FF), BF16)] * 2,
        cost_estimate=spent(10.0),
        compiler_params=pltpu.CompilerParams(vmem_limit_bytes=VMEM_LIMIT),
    )(pos, *c_in, *fs, *dhs, *dys)
    add = lambda a, b: (a.astype(F32) + b.astype(F32)).astype(BF16)

    x3_late, z_block, grad_send, grad_keep = lax.optimization_barrier((x3, z_block, grad_send, grad_keep))
    g3, gain3, drouter = call(
        functools.partial(combine_kernel, slots),
        [((rows, D), F32), ((1, D), F32), ((experts, D), F32)],
        pos, x3_late, gains[3], router_full, ids, index, turned, c, gate, cot, *dc_in,
        specs=[SCALAR] + [WHOLE] * (9 + arrays),
        us=5.5,
    )
    g3, z_block, grad_send = lax.optimization_barrier((g3, z_block, grad_send))
    z_in = trade(z_block)
    grads = add(grad_keep, flip(grad_send, "wshard", 1))
    g3, grads = lax.optimization_barrier((g3, grads))
    crossed = [flip(grads[at], "wshard", 2) for at in (slice(0, 176), slice(176, 352), slice(352, 512))]
    g2, gain2, *second = attend_back(x2, 1, packed2, o2, g3, [])
    g1, gain1, *mlp = call(
        feed_backward_kernel,
        [((rows, D), F32), ((1, D), F32)] + [((2, 2, 128, FF), BF16)] * 2,
        pos, x1, gains[1], g2, *w1, *w2,
        specs=[SCALAR, WHOLE, WHOLE, WHOLE] + weight_specs,
        scratch=mlp_scratch + [pltpu.VMEM((D, FF), BF16), pltpu.VMEM((FF, D), BF16), sems],
        us=12.5,
    )
    *second, mlp[0], mlp[1], crossed[0], crossed[1] = lax.optimization_barrier(
        (*second, mlp[0], mlp[1], crossed[0], crossed[1])
    )
    if linked:
        bulk = split_cube(pos, [second, mlp])
        g1 = after(g1, z_in, bulk, crossed[2])
        bulk = trade_cube(after(bulk, crossed[2]))
    dx, _, *first = attend_back(x0, 0, packed1, o1, g1, [gain1, gain2, gain3, drouter])
    (final,) = call(final_kernel, [((rows, D), BF16)], z_in.reshape(every, D), x3, turned, us=3.5)

    wide = first[0].shape[-1]
    grads = add(after(grads, dx), jnp.concatenate(crossed))
    expert1, expert2 = call(
        join_kernel,
        [((D, FF), F32), ((FF, D), F32)],
        pos, grads, flip(grads, "wshard", 1),
        specs=[SCALAR] + [WHOLE] * 2,
        us=4.0,
    )

    if linked:
        tail = split_cube(pos, [(first[0], after(first[1], final))])
        final_rows, input_grad = contract(final, pictures), contract(dx, pictures)
        bulk = sum_cube(after(bulk, tail, final_rows, input_grad, expert1))
        deep = flip(bulk, "expert", 4)
        tail = sum_cube(after(trade_cube(after(tail, bulk)), deep))
        bulk = spread(sum_two(bulk, deep))
        tail = spread(sum_two(tail, flip(tail, "expert", 4)))
        mlp1, mlp2 = call(
            finish_mlp_kernel,
            [((D // 4, FF), F32), ((4, 128, D), F32)],
            pos, *bulk, specs=[SCALAR] + [WHOLE] * 4, us=2.0,
        )
        grad_in, grad_out, smalls = call(
            finish_attention_kernel,
            [((2, D // 4, 3 * D), F32), ((2, D // 4, D), F32), (((wide - 4 * D) // 128 * STRIP, 128), F32)],
            pos, *tail, *bulk, specs=[SCALAR] + [WHOLE] * 8, us=2.0,
        )
        mlp2 = mlp2.reshape(FF // 4, D)
    else:
        first, second, mlp = sum_plainly(*first), sum_plainly(*second), sum_plainly(*mlp)
        grad_in = jnp.stack([first[:, : 3 * D], second[:, : 3 * D]])
        grad_out = jnp.stack([first[:, 3 * D : 4 * D], second[:, 3 * D :]])
        smalls = first[:STRIP, 4 * D :].reshape(STRIP, -1, 128).transpose(1, 0, 2).reshape(-1, 128)
        mlp1 = jnp.concatenate([mlp[0:64], mlp[128:192]], axis=0)
        final_rows, input_grad = contract(final, pictures), contract(dx, pictures)
        mlp2 = jnp.stack([mlp[64:128], mlp[192:256]]).reshape(2, 64, 4, D).transpose(2, 0, 1, 3).reshape(FF // 4, D)

    return (
        final_rows,
        input_grad,
        grad_in,
        grad_out,
        smalls[0:4],
        mlp1,
        mlp2,
        smalls[4 : 4 + experts].T,
        expert1[None],
        expert2[None],
    )


def solution(mesh):
    rows = P(("expert", "wshard"), None)
    dense = (P(None, "wshard", None), P(None, "wshard", None), P(None, "wshard"))
    shards = (P("wshard", None),) * 3
    experts = (P("expert", None, None),) * 2
    return jax.shard_map(
        local,
        mesh=mesh,
        in_specs=(rows, *dense, *shards, *experts, rows, rows),
        out_specs=(rows, rows, *dense, *shards, *experts),
        check_vma=False,
    )
```

```python
import functools

import jax
import jax.numpy as jnp
from jax import lax
from jax.experimental import pallas as pl
from jax.experimental.pallas import tpu as pltpu
from jax.sharding import PartitionSpec as P

D = 512
HEADS = 8
FF = 2048
SEQ = 197
TOP = 2
HEAD_DIM = 64
PAD = 208
STRIP = 32
CHUNK = 512
EPSILON = 1e-06
ROOT_2_PI = 0.7978845608028654
CUBIC = 0.044715

F32 = jnp.float32
BF16 = jnp.bfloat16
VMEM_LIMIT = 40 * 1024 * 1024
LINKED = 8


def dot(a, b, ca=1, cb=0):
    return lax.dot_general(a, b, (((ca,), (cb,)), ((), ())), preferred_element_type=F32)


def unit_rows(rows):
    centred = rows - jnp.mean(rows, axis=-1, keepdims=True)
    scale = lax.rsqrt(jnp.mean(centred * centred, axis=-1, keepdims=True) + EPSILON)
    return centred * scale, scale


def norm_backward(unit, scale, gain, grad):
    scaled = gain * grad
    inner = (
        scaled
        - jnp.mean(scaled, axis=-1, keepdims=True)
        - unit * jnp.mean(scaled * unit, axis=-1, keepdims=True)
    )
    return inner * scale, jnp.sum(grad * unit, axis=0, keepdims=True)


def gelu_parts(h):
    square = h * h
    t = jnp.tanh(ROOT_2_PI * h * (1.0 + CUBIC * square))
    half = 0.5 * (1.0 + t)
    slope = half + 0.5 * h * (1.0 - t * t) * (ROOT_2_PI * (1.0 + 3.0 * CUBIC * square))
    return h * half, slope


def gelu(h):
    return 0.5 * h * (1.0 + jnp.tanh(ROOT_2_PI * h * (1.0 + CUBIC * h * h)))


def start_weight(pos_ref, pieces, held, sems, first):
    copies = []
    for j, piece in enumerate(pieces):
        copy = pltpu.make_async_copy(piece, held.at[pos_ref[0] ^ j], sems.at[first + j])
        copy.start()
        copies.append(copy)
    return copies


def wait_all(copies):
    for copy in copies:
        copy.wait()


def softmax_rows(q, k):
    scores = dot(q, k, 1, 1) * (HEAD_DIM**-0.5)
    column = lax.broadcasted_iota(jnp.int32, scores.shape, 1)
    scores = jnp.where(column < SEQ, scores, -1e30)
    raised = jnp.exp(scores - jnp.max(scores, axis=-1, keepdims=True))
    return raised * (1.0 / jnp.sum(raised, axis=-1, keepdims=True))


def shards_of(pos_ref, send_ref, keep_ref):
    for target, turn in ((send_ref, 1), (keep_ref, 0)):
        for place in range(2):
            yield target, place, pos_ref[0] ^ (turn + 2 * (1 - place))


def own_half(pos_ref, half):
    return 1 - ((pos_ref[1] & 1) ^ half)


def attend_forward_kernel(pos_ref, x_ref, gain_ref, *refs):
    wi, wo = refs[0:4], refs[4:8]
    y_ref, packed_ref, o_ref, wi_held, wo_held, sems = refs[8:]
    wi_copies = start_weight(pos_ref, wi, wi_held, sems, 0)
    wo_copies = start_weight(pos_ref, wo, wo_held, sems, 4)
    rows = x_ref[...].astype(F32)
    unit, _ = unit_rows(rows)
    normed = (unit * gain_ref[...]).astype(BF16)
    wait_all(wi_copies)
    packed_ref[...] = dot(normed, wi_held[...].reshape(D, 3 * D)).astype(BF16)
    lane = lax.broadcasted_iota(jnp.int32, (PAD, 2 * HEAD_DIM), 1)
    for image in range(x_ref.shape[0] // PAD):
        here = pl.ds(image * PAD, PAD)
        for pair in range(HEADS // 2):
            at = pair * 2 * HEAD_DIM
            q = packed_ref[here, at : at + 128]
            k = packed_ref[here, D + at : D + at + 128]
            v = packed_ref[here, 2 * D + at : 2 * D + at + 128]
            total = None
            for side in range(2):
                mine = (lane >= HEAD_DIM) == bool(side)
                chances = softmax_rows(jnp.where(mine, q, jnp.zeros_like(q)), k).astype(BF16)
                part = dot(chances, jnp.where(mine, v, jnp.zeros_like(v)))
                total = part if total is None else total + part
            o_ref[here, at : at + 128] = total.astype(BF16)
    wait_all(wo_copies)
    y_ref[...] = x_ref[...].astype(F32) + dot(o_ref[...], wo_held[...].reshape(D, D))


def attend_backward_kernel(smalls, pos_ref, x_ref, gain_ref, packed_ref, o_ref, dz_ref, *refs):
    wi, wo = refs[0:4], refs[4:8]
    extra = refs[8 : 8 + smalls]
    dx_ref, dgain_ref, send_ref, keep_ref, wi_held, wo_held, dp_ref, dout_ref, do_ref, normed_ref, sems = refs[
        8 + smalls :
    ]
    wo_copies = start_weight(pos_ref, wo, wo_held, sems, 4)
    wi_copies = start_weight(pos_ref, wi, wi_held, sems, 0)
    unit, scale = unit_rows(x_ref[...].astype(F32))
    gain = gain_ref[...]
    normed_ref[...] = (unit * gain).astype(BF16)
    dout_ref[...] = dz_ref[...].astype(BF16)
    wait_all(wo_copies)
    do_ref[...] = dot(dout_ref[...], wo_held[...].reshape(D, D), 1, 1).astype(BF16)
    lane = lax.broadcasted_iota(jnp.int32, (PAD, 2 * HEAD_DIM), 1)
    factor = HEAD_DIM**-0.5
    for image in range(x_ref.shape[0] // PAD):
        here = pl.ds(image * PAD, PAD)
        for pair in range(HEADS // 2):
            at = pair * 2 * HEAD_DIM
            q = packed_ref[here, at : at + 128]
            k = packed_ref[here, D + at : D + at + 128]
            v = packed_ref[here, 2 * D + at : 2 * D + at + 128]
            do = do_ref[here, at : at + 128]
            dq = dk = dv = None
            for side in range(2):
                mine = (lane >= HEAD_DIM) == bool(side)
                own = lambda a: jnp.where(mine, a, jnp.zeros_like(a))
                q_own, k_own, do_own = own(q), own(k), own(do)
                chances = softmax_rows(q_own, k)
                dv_part = dot(chances.astype(BF16), do_own, 0, 0)
                da = dot(do_own, v, 1, 1)
                ds = chances * (da - jnp.sum(da * chances, axis=-1, keepdims=True))
                ds = ds.astype(BF16)
                dq_part = dot(ds, k_own)
                dk_part = dot(ds, q_own, 0, 0)
                dq = dq_part if dq is None else dq + dq_part
                dk = dk_part if dk is None else dk + dk_part
                dv = dv_part if dv is None else dv + dv_part
            dp_ref[here, at : at + 128] = (dq * factor).astype(BF16)
            dp_ref[here, D + at : D + at + 128] = (dk * factor).astype(BF16)
            dp_ref[here, 2 * D + at : 2 * D + at + 128] = dv.astype(BF16)
    wait_all(wi_copies)
    dn = dot(dp_ref[...], wi_held[...].reshape(D, 3 * D), 1, 1)
    unit, scale = unit_rows(x_ref[...].astype(F32))
    dx, dgain = norm_backward(unit, scale, gain, dn)
    dx_ref[...] = dz_ref[...] + dx
    dgain_ref[...] = dgain
    for target, place, shard in shards_of(pos_ref, send_ref, keep_ref):
        columns = pl.ds(pl.multiple_of(shard * 128, 128), 128)
        grad_in = dot(normed_ref[:, columns], dp_ref[...], 0, 0).astype(BF16)
        grad_out = dot(o_ref[:, columns], dout_ref[...], 0, 0).astype(BF16)
        for half in range(2):
            there = own_half(pos_ref, half)
            target[place, there, :, 0 : 3 * D] = grad_in[half * 64 : half * 64 + 64]
            target[place, there, :, 3 * D : 4 * D] = grad_out[half * 64 : half * 64 + 64]
    if smalls:
        small = jnp.concatenate([dgain] + [ref[...] for ref in extra], axis=0)
        small = jnp.concatenate([small, jnp.zeros((-small.shape[0] % STRIP, D), F32)], axis=0)
        for target, place, shard in shards_of(pos_ref, send_ref, keep_ref):
            piece = jnp.zeros((small.shape[0], 128), F32)
            for s in range(4):
                piece = jnp.where(shard == s, small[:, s * 128 : (s + 1) * 128], piece)
            piece = piece.astype(BF16)
            for half in range(2):
                for strip in range(64 // STRIP):
                    for group in range(small.shape[0] // STRIP):
                        at = 4 * D + group * 128
                        target[place, half, strip * STRIP : (strip + 1) * STRIP, at : at + 128] = piece[
                            group * STRIP : (group + 1) * STRIP
                        ]


def feed_forward_kernel(pos_ref, x_ref, gain_ref, *refs):
    w1, w2 = refs[0:4], refs[4:8]
    y_ref, w1_held, w2_held, sems = refs[8:]
    w1_copies = start_weight(pos_ref, w1, w1_held, sems, 0)
    w2_copies = start_weight(pos_ref, w2, w2_held, sems, 4)
    unit, _ = unit_rows(x_ref[...])
    normed = (unit * gain_ref[...]).astype(BF16)
    wait_all(w1_copies)
    total = x_ref[...]
    for j in range(FF // CHUNK):
        at = slice(j * CHUNK, (j + 1) * CHUNK)
        active = gelu(dot(normed, w1_held[:, :, at].reshape(D, CHUNK))).astype(BF16)
        if j == 0:
            wait_all(w2_copies)
        total = total + dot(active, w2_held[...].reshape(FF, D)[at])
    y_ref[...] = total


def feed_backward_kernel(pos_ref, x_ref, gain_ref, dz_ref, *refs):
    w1, w2 = refs[0:4], refs[4:8]
    dx_ref, dgain_ref, send_ref, keep_ref, w1_held, w2_held, g1_ref, g2_ref, sems = refs[8:]
    w1_copies = start_weight(pos_ref, w1, w1_held, sems, 0)
    w2_copies = start_weight(pos_ref, w2, w2_held, sems, 4)
    unit, scale = unit_rows(x_ref[...])
    gain = gain_ref[...]
    normed = (unit * gain).astype(BF16)
    dout = dz_ref[...].astype(BF16)
    wait_all(w1_copies)
    wait_all(w2_copies)
    dn = None
    for j in range(FF // CHUNK):
        at = slice(j * CHUNK, (j + 1) * CHUNK)
        w1_now = w1_held[:, :, at].reshape(D, CHUNK)
        w2_now = w2_held[...].reshape(FF, D)[at]
        active, slope = gelu_parts(dot(normed, w1_now))
        dh = (slope * dot(dout, w2_now, 1, 1)).astype(BF16)
        g2_ref[at] = dot(active.astype(BF16), dout, 0, 0).astype(BF16)
        g1_ref[:, at] = dot(normed, dh, 0, 0).astype(BF16)
        part = dot(dh, w1_now, 1, 1)
        dn = part if dn is None else dn + part
    dx, dgain = norm_backward(unit, scale, gain, dn)
    dx_ref[...] = dz_ref[...] + dx
    dgain_ref[...] = dgain
    for target, place, shard in shards_of(pos_ref, send_ref, keep_ref):
        for half in range(2):
            there = own_half(pos_ref, half)
            target[place, there, 0:64] = g1_ref[pl.ds(pl.multiple_of(shard * 128 + half * 64, 64), 64)]
            for part in range(4):
                start = pl.multiple_of(shard * 512 + part * 128 + half * 64, 64)
                target[place, there, 64:128, part * 512 : (part + 1) * 512] = g2_ref[pl.ds(start, 64)]


def routing_kernel(slots, ids_ref, cot_ref, index_ref, blocks_ref):
    experts = blocks_ref.shape[0] // slots
    tokens = ids_ref.shape[1]
    expert = lax.broadcasted_iota(jnp.int32, (experts, tokens), 0)
    named = [ids_ref[k : k + 1, :] == expert for k in range(TOP)]
    matches = jnp.where(named[0] | named[1], 1.0, 0.0).astype(BF16)
    earlier = lax.broadcasted_iota(jnp.int32, (tokens, tokens), 0) < lax.broadcasted_iota(
        jnp.int32, (tokens, tokens), 1
    )
    rank = dot(matches, jnp.where(earlier, 1.0, 0.0).astype(BF16))
    index_ref[...] = jnp.full(index_ref.shape, -1, jnp.int32)
    place = lax.broadcasted_iota(jnp.int32, (blocks_ref.shape[0], tokens), 0)
    chosen = None
    for k in range(TOP):
        slot = jnp.sum(jnp.where(named[k], rank, 0.0), axis=0, keepdims=True).astype(jnp.int32)
        index = ids_ref[k : k + 1, :] * slots + slot
        index_ref[k : k + 1, :] = index
        hit = place == index
        chosen = hit if chosen is None else chosen | hit
    blocks_ref[...] = dot(jnp.where(chosen, 1.0, 0.0).astype(BF16), cot_ref[...]).astype(BF16)


def write_spare(slots, column):
    eye = lax.broadcasted_iota(jnp.int32, (slots, D), 0) == lax.broadcasted_iota(jnp.int32, (slots, D), 1)
    line = jnp.sum(jnp.where(eye, column, 0.0), axis=0, keepdims=True)
    high = line.astype(BF16).astype(F32)
    middle = (line - high).astype(BF16).astype(F32)
    low = line - high - middle
    row = lax.broadcasted_iota(jnp.int32, (8, D), 0)
    return jnp.where(row == 0, high, jnp.where(row == 1, middle, jnp.where(row == 2, low, 0.0)))


def read_spare(tile, slots):
    line = tile[0:1] + tile[1:2] + tile[2:3]
    eye = lax.broadcasted_iota(jnp.int32, (slots, D), 0) == lax.broadcasted_iota(jnp.int32, (slots, D), 1)
    return jnp.sum(jnp.where(eye, line, 0.0), axis=1, keepdims=True)


def small_kernel(pos_ref, *refs):
    out_ref = refs[4]
    for j in range(4):
        start = pl.multiple_of((pos_ref[0] ^ j) * 128, 128)
        out_ref[:, pl.ds(start, 128)] = refs[j][...].astype(F32)


def dispatch_kernel(slots, pos_ref, x_ref, gain_ref, router_ref, ids_ref, index_ref, c_ref, gate_ref, *blocks):
    tokens = x_ref.shape[0]
    each = blocks[0].shape[0] // slots
    experts = len(blocks) * each
    unit, _ = unit_rows(x_ref[...])
    c = (unit * gain_ref[...]).astype(BF16)
    c_ref[...] = c
    logits = dot(router_ref[...].astype(BF16), c, 1, 1)
    expert = lax.broadcasted_iota(jnp.int32, (experts, tokens), 0)
    picked = [
        jnp.sum(jnp.where(ids_ref[k : k + 1, :] == expert, logits, 0.0), axis=0, keepdims=True) for k in range(TOP)
    ]
    gates = [0.5 + 0.5 * jnp.tanh(0.5 * (picked[k] - picked[1 - k])) for k in range(TOP)]
    gate_ref[...] = jnp.concatenate(gates + [jnp.zeros((8 - TOP, tokens), F32)], axis=0)
    for k in range(experts):
        place = lax.broadcasted_iota(jnp.int32, (slots, tokens), 0) + (pos_ref[1] ^ k) * slots
        hits = [place == index_ref[k : k + 1, :] for k in range(TOP)]
        rows = dot(jnp.where(hits[0] | hits[1], 1.0, 0.0).astype(BF16), c)
        weight = sum(jnp.where(hits[k], gates[k], 0.0) for k in range(TOP))
        tile = write_spare(slots, jnp.sum(weight, axis=1, keepdims=True))
        at = k % each * slots
        blocks[k // each][at : at + slots] = jnp.concatenate([rows[: slots - 8], tile], axis=0).astype(BF16)


def experts_kernel(slots, n, each, pos_ref, w1_ref, w2_ref, *refs):
    g_refs, c_refs, refs = refs[: n * each], refs[n * each : n * each + n], refs[n * each + n :]
    dc_refs, z_refs = refs[:n], refs[n : 2 * n]
    f_ref, dh_ref, dy_ref, gate_ref, y_ref, dc_ref = refs[2 * n :]
    step = pl.program_id(0)
    blocks = [(b, slice(b * slots, (b + 1) * slots)) for b in range(n * each)]

    @pl.when(step == 0)
    def _():
        for b, here in blocks:
            end = (b % each + 1) * slots
            gate = read_spare(c_refs[b // each][end - 8 : end].astype(F32), slots)
            gate_ref[here] = jnp.broadcast_to(gate, (slots, 128))
            dy_ref[here] = (gate * g_refs[b][0].astype(F32)).astype(BF16)

    c = c_refs[0][...] if n == 1 else jnp.concatenate([ref[...] for ref in c_refs], axis=0)
    active, slope = gelu_parts(dot(c, w1_ref[...]))
    active = active.astype(BF16)
    f_ref[...] = active
    dh = (slope * dot(dy_ref[...], w2_ref[...], 1, 1)).astype(BF16)
    dh_ref[...] = dh
    y = dot(active, w2_ref[...])
    dc = dot(dh, w1_ref[...], 1, 1)

    @pl.when(step == 0)
    def _():
        y_ref[...] = y
        dc_ref[...] = dc

    @pl.when(step > 0)
    def _():
        y_ref[...] += y
        dc_ref[...] += dc

    @pl.when(step == pl.num_programs(0) - 1)
    def _():
        for b, here in blocks:
            there = slice(b % each * slots, (b % each + 1) * slots)
            rounded = y_ref[here].astype(BF16).astype(F32)
            dgate = jnp.sum(g_refs[b][0].astype(F32) * rounded, axis=1, keepdims=True)
            z_refs[b // each][there] = (gate_ref[here, 0:1] * rounded).astype(BF16)
            rows = jnp.concatenate([dc_ref[here][: slots - 8], write_spare(slots, dgate)], axis=0)
            dc_refs[b // each][there] = rows.astype(BF16)


def expert_grads_kernel(n, pos_ref, *refs):
    m = len(refs) - 2 - 3 * n
    c_refs = refs[:m]
    f_refs, dh_refs, dy_refs = refs[m : m + n], refs[m + n : m + 2 * n], refs[m + 2 * n : m + 3 * n]
    send_ref, keep_ref = refs[m + 3 * n :]
    per = m // n
    for target, half in ((send_ref, 1 - (pos_ref[0] & 1)), (keep_ref, pos_ref[0] & 1)):
        at = pl.ds(pl.multiple_of(half * 256, 256), 256)
        total1 = total2 = None
        for i in range(n):
            c = [ref[:, at] for ref in c_refs[i * per : (i + 1) * per]]
            c = c[0] if per == 1 else jnp.concatenate(c, axis=0)
            part1 = dot(c, dh_refs[i][...], 0, 0)
            part2 = dot(f_refs[i][...], dy_refs[i][:, at], 0, 0)
            total1 = part1 if total1 is None else total1 + part1
            total2 = part2 if total2 is None else total2 + part2
        target[0:256] = total1.astype(BF16)
        target[256:512, 0:256] = total2[0:256].astype(BF16)
        target[256:512, 256:512] = total2[256:512].astype(BF16)


def cut_kernel(a_ref, b_ref, *outs):
    row = 0
    for out in outs:
        rows = slice(row, row + out.shape[0])
        out[...] = (a_ref[rows].astype(F32) + b_ref[rows].astype(F32)).astype(BF16)
        row += out.shape[0]


def glue_kernel(*refs):
    n, row = (len(refs) - 1) // 2, 0
    for a_ref, b_ref in zip(refs[:n], refs[n : 2 * n]):
        refs[-1][row : row + a_ref.shape[0]] = (a_ref[...].astype(F32) + b_ref[...].astype(F32)).astype(BF16)
        row += a_ref.shape[0]


def join_kernel(pos_ref, own_ref, other_ref, out1_ref, out2_ref):
    core = pos_ref[0] & 1
    for mine, ref in ((core, own_ref), (1 - core, other_ref)):
        at = pl.ds(pl.multiple_of(mine * 256, 256), 256)
        out1_ref[at] = ref[0:256].astype(F32)
        for block in range(FF // 256):
            out2_ref[block * 256 : (block + 1) * 256, at] = ref[256:512, block * 256 : (block + 1) * 256].astype(F32)


def arrange_kernel(pos_ref, *refs):
    for k, ref in enumerate(refs[:-1]):
        refs[-1][pos_ref[1] ^ k] = ref[...]


def one_hot_columns(index_ref, width):
    place = lax.broadcasted_iota(jnp.int32, (index_ref.shape[0], width), 1)
    hit = (place == index_ref[:, 0:1]) | (place == index_ref[:, 1:2])
    return jnp.where(hit, 1.0, 0.0).astype(BF16)


def combine_kernel(
    slots, pos_ref, x_ref, gain_ref, router_ref, ids_ref, index_ref, turned_ref, c_ref, gate_ref, cot_ref, *refs
):
    blocks, (dx_ref, dgain_ref, drouter_ref) = refs[:-3], refs[-3:]
    each = blocks[0].shape[0] // slots
    experts = len(blocks) * each
    tokens = x_ref.shape[0]
    dgates = [jnp.zeros((1, tokens), F32) for _ in range(TOP)]
    gc = None
    for k in range(experts):
        at = k % each * slots
        block = blocks[k // each][at : at + slots]
        start = (pos_ref[1] ^ k) * slots
        place = lax.broadcasted_iota(jnp.int32, (tokens, slots), 1) + start
        hit = (place == turned_ref[:, 0:1]) | (place == turned_ref[:, 1:2])
        part = dot(jnp.where(hit, 1.0, 0.0).astype(BF16), block)
        gc = part if gc is None else gc + part
        place = lax.broadcasted_iota(jnp.int32, (slots, tokens), 0) + start
        column = read_spare(block[slots - 8 :].astype(F32), slots)
        for j in range(TOP):
            hit = place == index_ref[j : j + 1, :]
            dgates[j] = dgates[j] + jnp.sum(jnp.where(hit, column, 0.0), axis=0, keepdims=True)
    dl = gate_ref[0:1] * gate_ref[1:2] * (dgates[0] - dgates[1])
    expert = lax.broadcasted_iota(jnp.int32, (experts, tokens), 0)
    dlogits = jnp.where(ids_ref[0:1, :] == expert, dl, 0.0) - jnp.where(ids_ref[1:2, :] == expert, dl, 0.0)
    dlogits = dlogits.astype(BF16)
    gc = gc + dot(dlogits, router_ref[...].astype(BF16), 0, 0)
    drouter_ref[...] = dot(dlogits, c_ref[...])
    unit, scale = unit_rows(x_ref[...])
    dx, dgain = norm_backward(unit, scale, gain_ref[...], gc)
    dx_ref[...] = cot_ref[...].astype(F32) + dx
    dgain_ref[...] = dgain


def split_cube_kernel(n, pos_ref, *refs):
    kept, came, out_ref = refs[0:n], refs[n : 2 * n], refs[2 * n]
    for place in range(2):
        for half in range(2):
            x = (pos_ref[1] & 1) ^ (1 - half)
            y = (pos_ref[0] >> 1) ^ (1 - place)
            row = 0
            for keep, new in zip(kept, came):
                total = (keep[place, half].astype(F32) + new[place, half].astype(F32)).astype(BF16)
                for start in range(0, keep.shape[2], 64):
                    for depth in range(2):
                        at = start + depth * STRIP
                        out_ref[depth * 4 + x * 2 + y, row : row + STRIP] = total[at : at + STRIP]
                    row += STRIP


def sum_cube_kernel(a_ref, out_ref):
    total = a_ref[0].astype(F32)
    for k in range(1, a_ref.shape[0]):
        total = total + a_ref[k].astype(F32)
    out_ref[...] = total.astype(BF16)


def sum_kernel(*refs):
    total = refs[0][...].astype(F32)
    for ref in refs[1:-1]:
        total = total + ref[...].astype(F32)
    refs[-1][...] = total.astype(BF16)


def rows_of(pos_ref, k):
    source = pos_ref[1] ^ k
    return pl.ds(pl.multiple_of((source & 1) * 64 + (source >> 1 & 1) * STRIP, STRIP), STRIP)


def finish_mlp_kernel(pos_ref, *refs):
    mlp1_ref, mlp2_ref = refs[4:]
    for k in range(4):
        there = rows_of(pos_ref, k)
        mlp1_ref[there] = refs[k][STRIP : 2 * STRIP].astype(F32)
        for part in range(4):
            mlp2_ref[part, there] = refs[k][2 * STRIP :, part * 512 : (part + 1) * 512].astype(F32)


def finish_attention_kernel(pos_ref, *refs):
    in_ref, out_ref, small_ref = refs[8:]
    for k in range(4):
        there = rows_of(pos_ref, k)
        for layer, ref in ((0, refs[k]), (1, refs[4 + k])):
            in_ref[layer, there] = ref[0:STRIP, 0 : 3 * D].astype(F32)
            out_ref[layer, there] = ref[0:STRIP, 3 * D : 4 * D].astype(F32)
    for group in range(small_ref.shape[0] // STRIP):
        at = 4 * D + group * 128
        small_ref[group * STRIP : (group + 1) * STRIP] = refs[0][:, at : at + 128].astype(F32)


def final_kernel(blocks_ref, x_ref, turned_ref, out_ref):
    out_ref[...] = (x_ref[...] + dot(one_hot_columns(turned_ref, blocks_ref.shape[0]), blocks_ref[...])).astype(BF16)


def spent(us):
    return pl.CostEstimate(flops=int(us * 1.0e9), bytes_accessed=0, transcendentals=0)


def call(kernel, outs, *args, us=1.0, scratch=(), specs=None, room=40, **more):
    return list(
        pl.pallas_call(
        kernel,
        out_shape=[(pltpu.HBM if rest else jax.ShapeDtypeStruct)(shape, kind) for shape, kind, *rest in outs],
        in_specs=specs if specs is not None else [WHOLE] * len(args),
        out_specs=[WHOLE] * len(outs),
        scratch_shapes=list(scratch),
        cost_estimate=spent(us),
        compiler_params=pltpu.CompilerParams(vmem_limit_bytes=room * 1024 * 1024),
        **more,
        )(*args)
    )


WHOLE = pl.BlockSpec(memory_space=pltpu.VMEM)
SCALAR = pl.BlockSpec(memory_space=pltpu.SMEM)
AWAY = pl.BlockSpec(memory_space=pltpu.HBM)


def flip(array, axis, bit):
    return lax.ppermute(array, axis, [(i, i ^ bit) for i in range(lax.axis_size(axis))])


def gather_pieces(piece, across=None):
    across = flip(piece, "wshard", 2) if across is None else across
    return (piece, flip(piece, "wshard", 1), across, flip(across, "wshard", 1))


def after(array, *others):
    return lax.optimization_barrier((array, *others))[0]


def split_cube(pos, bundle):
    came = [flip(send, "wshard", 1) for send, _ in bundle]
    tall = sum(keep.shape[2] for _, keep in bundle)
    wide = bundle[0][0].shape[-1]
    return call(
        functools.partial(split_cube_kernel, len(bundle)),
        [((8, tall // 2, wide), BF16, AWAY)],
        pos,
        *[keep for _, keep in bundle],
        *came,
        specs=[SCALAR] + [WHOLE] * (2 * len(bundle)),
        us=3.0,
    )[0]


def trade_cube(blocks):
    inner = lax.axis_size("wshard")
    groups = [
        [((2 * z + depth) * 2 + x) * inner + y * 2 + core for depth in range(2) for x in range(2) for y in range(2)]
        for z in range(lax.axis_size("expert") // 4)
        for core in range(2)
    ]
    return lax.all_to_all(blocks, ("expert", "wshard"), 0, 0, axis_index_groups=groups, tiled=True)


def sum_cube(blocks):
    return call(sum_cube_kernel, [(blocks.shape[1:], BF16, AWAY)], blocks, us=2.0)[0]


def sum_two(strip, other):
    return call(sum_kernel, [(strip.shape, BF16, AWAY)], strip, other)[0]


def spread(strip):
    return [strip] + [flip(strip, "expert", k) for k in range(1, 4)]


def sum_plainly(send, keep):
    half = (keep.astype(F32) + flip(send, "wshard", 1).astype(F32)).astype(BF16)
    rows = half[1].astype(F32) + flip(half[0], "wshard", 2).astype(F32)
    return lax.psum(jnp.concatenate([rows[1], rows[0]], axis=0), "expert")


def expand(rows, images):
    return jnp.pad(rows.reshape(images, SEQ, -1), ((0, 0), (0, PAD - SEQ), (0, 0))).reshape(images * PAD, -1)


def contract(rows, images):
    return rows.reshape(images, PAD, -1)[:, :SEQ].reshape(images * SEQ, -1)


def local(
    images, attn_in, attn_out, norm_gains, mlp_in, mlp_out, router, expert_in, expert_out, expert_ids, cotangent
):
    owners = lax.axis_size("expert")
    experts = owners * expert_in.shape[0]
    tokens = images.shape[0]
    pictures = tokens // SEQ
    rows = pictures * PAD
    capacity = max(2, 2 * TOP * tokens // experts)
    slots = (capacity + 8 + 15) // 16 * 16
    every = experts * slots
    linked = owners == LINKED
    own = lax.axis_index("expert") if linked else 0
    pos = jnp.stack([lax.axis_index("wshard"), own]).astype(jnp.int32)

    small = jnp.concatenate([norm_gains, router.T], axis=0)
    small = jnp.pad(small, ((0, -small.shape[0] % 16), (0, 0)))
    (small_full,) = call(
        small_kernel, [((small.shape[0], D), F32)], pos, *gather_pieces(small), specs=[SCALAR] + [WHOLE] * 4
    )
    gains = [small_full[i : i + 1] for i in range(4)]
    router_full = small_full[4 : 4 + experts]

    wi0 = flip(attn_in[0], "wshard", 2)
    wo0 = flip(attn_out[0], "wshard", 2)
    w1_across = flip(after(mlp_in, wi0), "wshard", 2)
    w2_across = flip(after(mlp_out, wi0), "wshard", 2)
    wi1 = flip(after(attn_in[1], w1_across), "wshard", 2)
    wo1 = flip(after(attn_out[1], w1_across), "wshard", 2)
    wi = [gather_pieces(attn_in[0], wi0), None]
    wo = [gather_pieces(attn_out[0], wo0), None]
    x0 = expand(images, pictures)

    weight_specs = [AWAY] * 8
    attn_scratch = [pltpu.VMEM((4, D // 4, 3 * D), BF16), pltpu.VMEM((4, D // 4, D), BF16)]
    mlp_scratch = [pltpu.VMEM((4, D // 4, FF), BF16), pltpu.VMEM((4, FF // 4, D), BF16)]
    sems = pltpu.SemaphoreType.DMA((8,))

    def attend(x, layer):
        return call(
            attend_forward_kernel,
            [((rows, D), F32), ((rows, 3 * D), BF16), ((rows, D), BF16)],
            pos, x, gains[2 * layer], *wi[layer], *wo[layer],
            specs=[SCALAR, WHOLE, WHOLE] + weight_specs,
            scratch=attn_scratch + [sems],
            us=7.0,
        )

    def attend_back(x, layer, packed, o, dz, extra):
        wide = 4 * D
        if extra:
            wide += (sum(a.shape[0] for a in extra) + 1 + STRIP - 1) // STRIP * 128
        return call(
            functools.partial(attend_backward_kernel, len(extra)),
            [((rows, D), F32), ((1, D), F32), ((2, 2, 64, wide), BF16, AWAY), ((2, 2, 64, wide), BF16, AWAY)],
            pos, x, gains[2 * layer], packed, o, dz, *wi[layer], *wo[layer], *extra,
            specs=[SCALAR] + [WHOLE] * 5 + weight_specs + [WHOLE] * len(extra),
            scratch=attn_scratch
            + [pltpu.VMEM((rows, 3 * D), BF16)]
            + [pltpu.VMEM((rows, D), BF16)] * 3
            + [sems],
            us=12.5,
            room=58,
        )

    x1, packed1, o1 = attend(x0, 0)
    ids = jnp.pad(after(expert_ids, x1).T.reshape(TOP, pictures, SEQ), ((0, 8 - TOP), (0, 0), (0, PAD - SEQ)), constant_values=-1)
    ids = ids.reshape(8, rows)
    cot = expand(after(cotangent, x1), pictures)

    index, g_out = call(
        functools.partial(routing_kernel, slots), [((8, rows), jnp.int32), ((every, D), BF16)], ids, cot, us=3.4
    )
    turned = index.T
    trade = functools.partial(lax.all_to_all, axis_name="expert", split_axis=0, concat_axis=0, tiled=True)
    g_in = trade(g_out.reshape(experts, slots, D))

    w1 = gather_pieces(mlp_in, after(w1_across, x1))
    w2 = gather_pieces(mlp_out, after(w2_across, x1))
    (x2,) = call(
        feed_forward_kernel, [((rows, D), F32)], pos, x1, gains[1], *w1, *w2,
        specs=[SCALAR, WHOLE, WHOLE] + weight_specs, scratch=mlp_scratch + [sems], us=6.5,
    )
    wi[1] = gather_pieces(attn_in[1], after(wi1, x2))
    wo[1] = gather_pieces(attn_out[1], after(wo1, x2))
    x3, packed2, o2 = attend(x2, 1)
    arrays = experts if linked else max(1, experts // (2 * PAD // slots))
    each = experts // arrays
    c, gate, *c_out = call(
        functools.partial(dispatch_kernel, slots),
        [((rows, D), BF16), ((8, rows), F32)] + [((each * slots, D), BF16, AWAY)] * arrays,
        pos, x3, gains[3], router_full, ids, index,
        specs=[SCALAR] + [WHOLE] * 5,
        us=4.6,
    )

    def swap(blocks, first=0):
        if linked:
            return [flip(block, "expert", k) if k else block for k, block in enumerate(blocks, first)]
        moved = trade(jnp.concatenate(blocks).reshape(experts, slots, D))
        return list(moved.reshape(arrays, each * slots, D))

    c_in = swap(c_out)
    per = 2 if linked else 1
    work = []
    dc_out, z_out, dc_in = [], [], []
    for first in range(0, arrays, per):
        given = c_in[first : first + per]
        if linked and first >= 2 * per:
            given[0], *dc_in[-2 * per : -per] = lax.optimization_barrier((given[0], *dc_in[-2 * per : -per]))
        count = list(range(first * each, (first + per) * each))
        tall = len(count) * slots
        fixed = lambda *shape: pl.BlockSpec(shape, lambda j, pos_ref: (0,) * len(shape))
        source = lambda k: pl.BlockSpec((1, slots, D), lambda j, pos_ref: (pos_ref[1] ^ k, 0, 0))
        across = lambda height: pl.BlockSpec((height, CHUNK), lambda j, pos_ref: (0, j))
        *made, f, dh, dy = pl.pallas_call(
            functools.partial(experts_kernel, slots, per, each),
            out_shape=[pltpu.HBM((each * slots, D), BF16)] * (2 * per)
            + [pltpu.HBM((tall, FF), BF16)] * 2
            + [pltpu.HBM((tall, D), BF16)],
            grid_spec=pltpu.PrefetchScalarGridSpec(
                num_scalar_prefetch=1,
                grid=(FF // CHUNK,),
                in_specs=[across(D), pl.BlockSpec((CHUNK, D), lambda j, pos_ref: (j, 0))]
                + [source(k) for k in count]
                + [fixed(each * slots, D)] * per,
                out_specs=[fixed(each * slots, D)] * (2 * per) + [across(tall)] * 2 + [fixed(tall, D)],
                scratch_shapes=[pltpu.VMEM((tall, 128), F32), pltpu.VMEM((tall, D), F32), pltpu.VMEM((tall, D), F32)],
            ),
            cost_estimate=spent(8.0),
            compiler_params=pltpu.CompilerParams(vmem_limit_bytes=VMEM_LIMIT),
        )(pos, expert_in[0], expert_out[0], *[g_in] * len(count), *given)
        dc_out += made[:per]
        z_out += made[per:]
        if linked:
            dc_in += swap(made[:per], first)
        work.append((f, dh, dy))
    if not linked:
        dc_in = swap(dc_out)
    if linked:
        (z_block,) = call(
            arrange_kernel, [((experts, slots, D), BF16, AWAY)], pos, *z_out, specs=[SCALAR] + [WHOLE] * experts, us=2.0
        )
    else:
        z_block = jnp.concatenate(z_out).reshape(experts, slots, D)
    n = len(work)
    whole_rows = lambda a: pl.BlockSpec(a.shape, lambda j: (0, 0))
    chunk = lambda a: pl.BlockSpec((a.shape[0], CHUNK), lambda j: (0, j))
    fs, dhs, dys = ([w[i] for w in work] for i in range(3))
    if linked:
        dys[0], *dc_in[per : 2 * per] = lax.optimization_barrier((dys[0], *dc_in[per : 2 * per]))
    grad_send, grad_keep = pl.pallas_call(
        functools.partial(expert_grads_kernel, n),
        grid=(FF // CHUNK,),
        in_specs=[SCALAR]
        + [whole_rows(a) for a in c_in]
        + [chunk(a) for a in fs + dhs]
        + [whole_rows(a) for a in dys],
        out_specs=[pl.BlockSpec((512, CHUNK), lambda j: (0, j))] * 2,
        out_shape=[pltpu.HBM((512, FF), BF16)] * 2,
        cost_estimate=spent(10.0),
        compiler_params=pltpu.CompilerParams(vmem_limit_bytes=VMEM_LIMIT),
    )(pos, *c_in, *fs, *dhs, *dys)
    x3_late, z_block, grad_send, grad_keep = lax.optimization_barrier((x3, z_block, grad_send, grad_keep))
    g3, gain3, drouter = call(
        functools.partial(combine_kernel, slots),
        [((rows, D), F32), ((1, D), F32), ((experts, D), F32)],
        pos, x3_late, gains[3], router_full, ids, index, turned, c, gate, cot, *dc_in,
        specs=[SCALAR] + [WHOLE] * (9 + arrays),
        us=5.5,
    )
    g3, z_block, grad_send = lax.optimization_barrier((g3, z_block, grad_send))
    z_in = trade(z_block)
    grads = call(
        cut_kernel,
        [((tall, FF), BF16, AWAY) for tall in (128, 128, 256)],
        grad_keep, flip(grad_send, "wshard", 1),
        us=2.0,
    )
    g3 = after(g3, *grads)
    crossed = [flip(piece, "wshard", 2) for piece in grads[:2]]
    g2, gain2, *second = attend_back(x2, 1, packed2, o2, g3, [])
    g1, gain1, *mlp = call(
        feed_backward_kernel,
        [((rows, D), F32), ((1, D), F32)] + [((2, 2, 128, FF), BF16, AWAY)] * 2,
        pos, x1, gains[1], g2, *w1, *w2,
        specs=[SCALAR, WHOLE, WHOLE, WHOLE] + weight_specs,
        scratch=mlp_scratch + [pltpu.VMEM((D, FF), BF16), pltpu.VMEM((FF, D), BF16), sems],
        us=12.5,
        room=58,
    )
    *second, mlp[0], mlp[1], crossed[0], crossed[1] = lax.optimization_barrier(
        (*second, mlp[0], mlp[1], crossed[0], crossed[1])
    )
    if linked:
        bulk = split_cube(pos, [second, mlp])
        g1 = after(g1, z_in, bulk)
        bulk = trade_cube(bulk)
    dx, _, *first = attend_back(x0, 0, packed1, o1, g1, [gain1, gain2, gain3, drouter])
    (final,) = call(final_kernel, [((rows, D), BF16)], z_in.reshape(every, D), x3, turned, us=3.5)

    wide = first[0].shape[-1]
    if linked:
        tail = split_cube(pos, [(first[0], after(first[1], final))])
        final_rows, input_grad = contract(final, pictures), contract(dx, pictures)
        bulk = sum_cube(after(bulk, tail, final_rows, input_grad))
        deep = flip(bulk, "expert", 4)
        tail = sum_cube(after(trade_cube(after(tail, bulk)), deep))
        last = flip(after(grads[2], tail), "wshard", 2)
        bulk = spread(sum_two(bulk, deep))
        tail = sum_two(tail, flip(tail, "expert", 4))
        crossed.append(after(last, tail, *bulk))
        tail = spread(tail)
        mlp1, mlp2 = call(
            finish_mlp_kernel,
            [((D // 4, FF), F32), ((4, 128, D), F32)],
            pos, *bulk, specs=[SCALAR] + [WHOLE] * 4, us=2.0,
        )
        grad_in, grad_out, smalls = call(
            finish_attention_kernel,
            [((2, D // 4, 3 * D), F32), ((2, D // 4, D), F32), (((wide - 4 * D) // 128 * STRIP, 128), F32)],
            pos, *tail, *bulk, specs=[SCALAR] + [WHOLE] * 8, us=2.0,
        )
        mlp2 = mlp2.reshape(FF // 4, D)
    else:
        first, second, mlp = sum_plainly(*first), sum_plainly(*second), sum_plainly(*mlp)
        grad_in = jnp.stack([first[:, : 3 * D], second[:, : 3 * D]])
        grad_out = jnp.stack([first[:, 3 * D : 4 * D], second[:, 3 * D :]])
        smalls = first[:STRIP, 4 * D :].reshape(STRIP, -1, 128).transpose(1, 0, 2).reshape(-1, 128)
        mlp1 = jnp.concatenate([mlp[0:64], mlp[128:192]], axis=0)
        final_rows, input_grad = contract(final, pictures), contract(dx, pictures)
        mlp2 = jnp.stack([mlp[64:128], mlp[192:256]]).reshape(2, 64, 4, D).transpose(2, 0, 1, 3).reshape(FF // 4, D)

    if not linked:
        crossed.append(flip(grads[2], "wshard", 2))
    (joined,) = call(glue_kernel, [((512, FF), BF16, AWAY)], *grads, *crossed, us=2.0)
    expert1, expert2 = call(
        join_kernel,
        [((D, FF), F32), ((FF, D), F32)],
        pos, joined, flip(joined, "wshard", 1),
        specs=[SCALAR] + [WHOLE] * 2,
        us=4.0,
    )

    return (
        final_rows,
        input_grad,
        grad_in,
        grad_out,
        smalls[0:4],
        mlp1,
        mlp2,
        smalls[4 : 4 + experts].T,
        expert1[None],
        expert2[None],
    )


def solution(mesh):
    rows = P(("expert", "wshard"), None)
    dense = (P(None, "wshard", None), P(None, "wshard", None), P(None, "wshard"))
    shards = (P("wshard", None),) * 3
    experts = (P("expert", None, None),) * 2
    return jax.shard_map(
        local,
        mesh=mesh,
        in_specs=(rows, *dense, *shards, *experts, rows, rows),
        out_specs=(rows, rows, *dense, *shards, *experts),
        check_vma=False,
    )
```

```python
import functools

import jax
import jax.numpy as jnp
from jax import lax
from jax.experimental import pallas as pl
from jax.experimental.pallas import tpu as pltpu
from jax.sharding import PartitionSpec as P

D = 512
HEADS = 8
FF = 2048
SEQ = 197
TOP = 2
HEAD_DIM = 64
PAD = 208
STRIP = 32
CHUNK = 512
EPSILON = 1e-06
ROOT_2_PI = 0.7978845608028654
CUBIC = 0.044715

F32 = jnp.float32
BF16 = jnp.bfloat16
VMEM_LIMIT = 40 * 1024 * 1024
LINKED = 8


def dot(a, b, ca=1, cb=0):
    return lax.dot_general(a, b, (((ca,), (cb,)), ((), ())), preferred_element_type=F32)


def unit_rows(rows):
    centred = rows - jnp.mean(rows, axis=-1, keepdims=True)
    scale = lax.rsqrt(jnp.mean(centred * centred, axis=-1, keepdims=True) + EPSILON)
    return centred * scale, scale


def norm_backward(unit, scale, gain, grad):
    scaled = gain * grad
    inner = (
        scaled
        - jnp.mean(scaled, axis=-1, keepdims=True)
        - unit * jnp.mean(scaled * unit, axis=-1, keepdims=True)
    )
    return inner * scale, jnp.sum(grad * unit, axis=0, keepdims=True)


def gelu_parts(h):
    square = h * h
    t = jnp.tanh(ROOT_2_PI * h * (1.0 + CUBIC * square))
    half = 0.5 * (1.0 + t)
    slope = half + 0.5 * h * (1.0 - t * t) * (ROOT_2_PI * (1.0 + 3.0 * CUBIC * square))
    return h * half, slope


def gelu(h):
    return 0.5 * h * (1.0 + jnp.tanh(ROOT_2_PI * h * (1.0 + CUBIC * h * h)))


def start_weight(pos_ref, pieces, held, sems, first):
    copies = []
    for j, piece in enumerate(pieces):
        copy = pltpu.make_async_copy(piece, held.at[pos_ref[0] ^ j], sems.at[first + j])
        copy.start()
        copies.append(copy)
    return copies


def wait_all(copies):
    for copy in copies:
        copy.wait()


def softmax_rows(q, k):
    scores = dot(q, k, 1, 1) * (HEAD_DIM**-0.5)
    column = lax.broadcasted_iota(jnp.int32, scores.shape, 1)
    scores = jnp.where(column < SEQ, scores, -1e30)
    raised = jnp.exp(scores - jnp.max(scores, axis=-1, keepdims=True))
    return raised * (1.0 / jnp.sum(raised, axis=-1, keepdims=True))


def shards_of(pos_ref, send_ref, keep_ref):
    for target, turn in ((send_ref, 1), (keep_ref, 0)):
        for place in range(2):
            yield target, place, pos_ref[0] ^ (turn + 2 * (1 - place))


def own_half(pos_ref, half):
    return 1 - ((pos_ref[1] & 1) ^ half)


def attend_forward_kernel(pos_ref, x_ref, gain_ref, *refs):
    wi, wo = refs[0:4], refs[4:8]
    y_ref, packed_ref, o_ref, wi_held, wo_held, sems = refs[8:]
    wi_copies = start_weight(pos_ref, wi, wi_held, sems, 0)
    wo_copies = start_weight(pos_ref, wo, wo_held, sems, 4)
    rows = x_ref[...].astype(F32)
    unit, _ = unit_rows(rows)
    normed = (unit * gain_ref[...]).astype(BF16)
    wait_all(wi_copies)
    packed_ref[...] = dot(normed, wi_held[...].reshape(D, 3 * D)).astype(BF16)
    lane = lax.broadcasted_iota(jnp.int32, (PAD, 2 * HEAD_DIM), 1)
    for image in range(x_ref.shape[0] // PAD):
        here = pl.ds(image * PAD, PAD)
        for pair in range(HEADS // 2):
            at = pair * 2 * HEAD_DIM
            q = packed_ref[here, at : at + 128]
            k = packed_ref[here, D + at : D + at + 128]
            v = packed_ref[here, 2 * D + at : 2 * D + at + 128]
            total = None
            for side in range(2):
                mine = (lane >= HEAD_DIM) == bool(side)
                chances = softmax_rows(jnp.where(mine, q, jnp.zeros_like(q)), k).astype(BF16)
                part = dot(chances, jnp.where(mine, v, jnp.zeros_like(v)))
                total = part if total is None else total + part
            o_ref[here, at : at + 128] = total.astype(BF16)
    wait_all(wo_copies)
    y_ref[...] = x_ref[...].astype(F32) + dot(o_ref[...], wo_held[...].reshape(D, D))


def attend_backward_kernel(smalls, pos_ref, x_ref, gain_ref, packed_ref, o_ref, dz_ref, *refs):
    wi, wo = refs[0:4], refs[4:8]
    extra = refs[8 : 8 + smalls]
    dx_ref, dgain_ref, send_ref, keep_ref, wi_held, wo_held, dp_ref, dout_ref, do_ref, normed_ref, sems = refs[
        8 + smalls :
    ]
    wo_copies = start_weight(pos_ref, wo, wo_held, sems, 4)
    wi_copies = start_weight(pos_ref, wi, wi_held, sems, 0)
    unit, scale = unit_rows(x_ref[...].astype(F32))
    gain = gain_ref[...]
    normed_ref[...] = (unit * gain).astype(BF16)
    dout_ref[...] = dz_ref[...].astype(BF16)
    wait_all(wo_copies)
    do_ref[...] = dot(dout_ref[...], wo_held[...].reshape(D, D), 1, 1).astype(BF16)
    lane = lax.broadcasted_iota(jnp.int32, (PAD, 2 * HEAD_DIM), 1)
    factor = HEAD_DIM**-0.5
    for image in range(x_ref.shape[0] // PAD):
        here = pl.ds(image * PAD, PAD)
        for pair in range(HEADS // 2):
            at = pair * 2 * HEAD_DIM
            q = packed_ref[here, at : at + 128]
            k = packed_ref[here, D + at : D + at + 128]
            v = packed_ref[here, 2 * D + at : 2 * D + at + 128]
            do = do_ref[here, at : at + 128]
            dq = dk = dv = None
            for side in range(2):
                mine = (lane >= HEAD_DIM) == bool(side)
                own = lambda a: jnp.where(mine, a, jnp.zeros_like(a))
                q_own, k_own, do_own = own(q), own(k), own(do)
                chances = softmax_rows(q_own, k)
                dv_part = dot(chances.astype(BF16), do_own, 0, 0)
                da = dot(do_own, v, 1, 1)
                ds = chances * (da - jnp.sum(da * chances, axis=-1, keepdims=True))
                ds = ds.astype(BF16)
                dq_part = dot(ds, k_own)
                dk_part = dot(ds, q_own, 0, 0)
                dq = dq_part if dq is None else dq + dq_part
                dk = dk_part if dk is None else dk + dk_part
                dv = dv_part if dv is None else dv + dv_part
            dp_ref[here, at : at + 128] = (dq * factor).astype(BF16)
            dp_ref[here, D + at : D + at + 128] = (dk * factor).astype(BF16)
            dp_ref[here, 2 * D + at : 2 * D + at + 128] = dv.astype(BF16)
    wait_all(wi_copies)
    dn = dot(dp_ref[...], wi_held[...].reshape(D, 3 * D), 1, 1)
    unit, scale = unit_rows(x_ref[...].astype(F32))
    dx, dgain = norm_backward(unit, scale, gain, dn)
    dx_ref[...] = dz_ref[...] + dx
    dgain_ref[...] = dgain
    for target, place, shard in shards_of(pos_ref, send_ref, keep_ref):
        columns = pl.ds(pl.multiple_of(shard * 128, 128), 128)
        grad_in = dot(normed_ref[:, columns], dp_ref[...], 0, 0).astype(BF16)
        grad_out = dot(o_ref[:, columns], dout_ref[...], 0, 0).astype(BF16)
        for half in range(2):
            there = own_half(pos_ref, half)
            target[place, there, :, 0 : 3 * D] = grad_in[half * 64 : half * 64 + 64]
            target[place, there, :, 3 * D : 4 * D] = grad_out[half * 64 : half * 64 + 64]
    if smalls:
        small = jnp.concatenate([dgain] + [ref[...] for ref in extra], axis=0)
        small = jnp.concatenate([small, jnp.zeros((-small.shape[0] % STRIP, D), F32)], axis=0)
        for target, place, shard in shards_of(pos_ref, send_ref, keep_ref):
            piece = jnp.zeros((small.shape[0], 128), F32)
            for s in range(4):
                piece = jnp.where(shard == s, small[:, s * 128 : (s + 1) * 128], piece)
            piece = piece.astype(BF16)
            for half in range(2):
                for strip in range(64 // STRIP):
                    for group in range(small.shape[0] // STRIP):
                        at = 4 * D + group * 128
                        target[place, half, strip * STRIP : (strip + 1) * STRIP, at : at + 128] = piece[
                            group * STRIP : (group + 1) * STRIP
                        ]


def feed_forward_kernel(pos_ref, x_ref, gain_ref, *refs):
    w1, w2 = refs[0:4], refs[4:8]
    y_ref, w1_held, w2_held, sems = refs[8:]
    w1_copies = start_weight(pos_ref, w1, w1_held, sems, 0)
    w2_copies = start_weight(pos_ref, w2, w2_held, sems, 4)
    unit, _ = unit_rows(x_ref[...])
    normed = (unit * gain_ref[...]).astype(BF16)
    wait_all(w1_copies)
    total = x_ref[...]
    for j in range(FF // 1024):
        at = slice(j * 1024, (j + 1) * 1024)
        active = gelu(dot(normed, w1_held[:, :, at].reshape(D, 1024))).astype(BF16)
        if j == 0:
            wait_all(w2_copies)
        total = total + dot(active, w2_held[...].reshape(FF, D)[at])
    y_ref[...] = total


def feed_backward_kernel(pos_ref, x_ref, gain_ref, dz_ref, *refs):
    w1, w2 = refs[0:4], refs[4:8]
    dx_ref, dgain_ref, send_ref, keep_ref, w1_held, w2_held, g1_ref, g2_ref, sems = refs[8:]
    w1_copies = start_weight(pos_ref, w1, w1_held, sems, 0)
    w2_copies = start_weight(pos_ref, w2, w2_held, sems, 4)
    unit, scale = unit_rows(x_ref[...])
    gain = gain_ref[...]
    normed = (unit * gain).astype(BF16)
    dout = dz_ref[...].astype(BF16)
    wait_all(w1_copies)
    wait_all(w2_copies)
    dn = None
    for j in range(FF // 1024):
        at = slice(j * 1024, (j + 1) * 1024)
        w1_now = w1_held[:, :, at].reshape(D, 1024)
        w2_now = w2_held[...].reshape(FF, D)[at]
        active, slope = gelu_parts(dot(normed, w1_now))
        dh = (slope * dot(dout, w2_now, 1, 1)).astype(BF16)
        g2_ref[at] = dot(active.astype(BF16), dout, 0, 0).astype(BF16)
        g1_ref[:, at] = dot(normed, dh, 0, 0).astype(BF16)
        part = dot(dh, w1_now, 1, 1)
        dn = part if dn is None else dn + part
    dx, dgain = norm_backward(unit, scale, gain, dn)
    dx_ref[...] = dz_ref[...] + dx
    dgain_ref[...] = dgain
    for target, place, shard in shards_of(pos_ref, send_ref, keep_ref):
        for half in range(2):
            there = own_half(pos_ref, half)
            target[place, there, 0:64] = g1_ref[pl.ds(pl.multiple_of(shard * 128 + half * 64, 64), 64)]
            for part in range(4):
                start = pl.multiple_of(shard * 512 + part * 128 + half * 64, 64)
                target[place, there, 64:128, part * 512 : (part + 1) * 512] = g2_ref[pl.ds(start, 64)]


def routing_kernel(slots, ids_ref, cot_ref, index_ref, blocks_ref):
    experts = blocks_ref.shape[0] // slots
    tokens = ids_ref.shape[1]
    expert = lax.broadcasted_iota(jnp.int32, (experts, tokens), 0)
    named = [ids_ref[k : k + 1, :] == expert for k in range(TOP)]
    matches = jnp.where(named[0] | named[1], 1.0, 0.0).astype(BF16)
    earlier = lax.broadcasted_iota(jnp.int32, (tokens, tokens), 0) < lax.broadcasted_iota(
        jnp.int32, (tokens, tokens), 1
    )
    rank = dot(matches, jnp.where(earlier, 1.0, 0.0).astype(BF16))
    index_ref[...] = jnp.full(index_ref.shape, -1, jnp.int32)
    place = lax.broadcasted_iota(jnp.int32, (blocks_ref.shape[0], tokens), 0)
    chosen = None
    for k in range(TOP):
        slot = jnp.sum(jnp.where(named[k], rank, 0.0), axis=0, keepdims=True).astype(jnp.int32)
        index = ids_ref[k : k + 1, :] * slots + slot
        index_ref[k : k + 1, :] = index
        hit = place == index
        chosen = hit if chosen is None else chosen | hit
    blocks_ref[...] = dot(jnp.where(chosen, 1.0, 0.0).astype(BF16), cot_ref[...]).astype(BF16)


def write_spare(slots, column):
    eye = lax.broadcasted_iota(jnp.int32, (slots, D), 0) == lax.broadcasted_iota(jnp.int32, (slots, D), 1)
    line = jnp.sum(jnp.where(eye, column, 0.0), axis=0, keepdims=True)
    high = line.astype(BF16).astype(F32)
    middle = (line - high).astype(BF16).astype(F32)
    low = line - high - middle
    row = lax.broadcasted_iota(jnp.int32, (8, D), 0)
    return jnp.where(row == 0, high, jnp.where(row == 1, middle, jnp.where(row == 2, low, 0.0)))


def read_spare(tile, slots):
    line = tile[0:1] + tile[1:2] + tile[2:3]
    eye = lax.broadcasted_iota(jnp.int32, (slots, D), 0) == lax.broadcasted_iota(jnp.int32, (slots, D), 1)
    return jnp.sum(jnp.where(eye, line, 0.0), axis=1, keepdims=True)


def small_kernel(pos_ref, *refs):
    out_ref = refs[4]
    for j in range(4):
        start = pl.multiple_of((pos_ref[0] ^ j) * 128, 128)
        out_ref[:, pl.ds(start, 128)] = refs[j][...].astype(F32)


def dispatch_kernel(slots, pos_ref, x_ref, gain_ref, router_ref, ids_ref, index_ref, c_ref, gate_ref, *blocks):
    tokens = x_ref.shape[0]
    each = blocks[0].shape[0] // slots
    experts = len(blocks) * each
    unit, _ = unit_rows(x_ref[...])
    c = (unit * gain_ref[...]).astype(BF16)
    c_ref[...] = c
    logits = dot(router_ref[...].astype(BF16), c, 1, 1)
    expert = lax.broadcasted_iota(jnp.int32, (experts, tokens), 0)
    picked = [
        jnp.sum(jnp.where(ids_ref[k : k + 1, :] == expert, logits, 0.0), axis=0, keepdims=True) for k in range(TOP)
    ]
    gates = [0.5 + 0.5 * jnp.tanh(0.5 * (picked[k] - picked[1 - k])) for k in range(TOP)]
    gate_ref[...] = jnp.concatenate(gates + [jnp.zeros((8 - TOP, tokens), F32)], axis=0)
    for k in range(experts):
        place = lax.broadcasted_iota(jnp.int32, (slots, tokens), 0) + (pos_ref[1] ^ k) * slots
        hits = [place == index_ref[k : k + 1, :] for k in range(TOP)]
        rows = dot(jnp.where(hits[0] | hits[1], 1.0, 0.0).astype(BF16), c)
        weight = sum(jnp.where(hits[k], gates[k], 0.0) for k in range(TOP))
        tile = write_spare(slots, jnp.sum(weight, axis=1, keepdims=True))
        at = k % each * slots
        blocks[k // each][at : at + slots] = jnp.concatenate([rows[: slots - 8], tile], axis=0).astype(BF16)


def experts_kernel(slots, n, each, pos_ref, w1_ref, w2_ref, *refs):
    g_refs, c_refs, refs = refs[: n * each], refs[n * each : n * each + n], refs[n * each + n :]
    dc_refs, z_refs = refs[:n], refs[n : 2 * n]
    f_ref, dh_ref, dy_ref, gate_ref, y_ref, dc_ref = refs[2 * n :]
    step = pl.program_id(0)
    blocks = [(b, slice(b * slots, (b + 1) * slots)) for b in range(n * each)]

    @pl.when(step == 0)
    def _():
        for b, here in blocks:
            end = (b % each + 1) * slots
            gate = read_spare(c_refs[b // each][end - 8 : end].astype(F32), slots)
            gate_ref[here] = jnp.broadcast_to(gate, (slots, 128))
            dy_ref[here] = (gate * g_refs[b][0].astype(F32)).astype(BF16)

    c = c_refs[0][...] if n == 1 else jnp.concatenate([ref[...] for ref in c_refs], axis=0)
    active, slope = gelu_parts(dot(c, w1_ref[...]))
    active = active.astype(BF16)
    f_ref[...] = active
    dh = (slope * dot(dy_ref[...], w2_ref[...], 1, 1)).astype(BF16)
    dh_ref[...] = dh
    y = dot(active, w2_ref[...])
    dc = dot(dh, w1_ref[...], 1, 1)

    @pl.when(step == 0)
    def _():
        y_ref[...] = y
        dc_ref[...] = dc

    @pl.when(step > 0)
    def _():
        y_ref[...] += y
        dc_ref[...] += dc

    @pl.when(step == pl.num_programs(0) - 1)
    def _():
        for b, here in blocks:
            there = slice(b % each * slots, (b % each + 1) * slots)
            rounded = y_ref[here].astype(BF16).astype(F32)
            dgate = jnp.sum(g_refs[b][0].astype(F32) * rounded, axis=1, keepdims=True)
            z_refs[b // each][there] = (gate_ref[here, 0:1] * rounded).astype(BF16)
            rows = jnp.concatenate([dc_ref[here][: slots - 8], write_spare(slots, dgate)], axis=0)
            dc_refs[b // each][there] = rows.astype(BF16)


def expert_grads_kernel(n, pos_ref, *refs):
    m = len(refs) - 2 - 3 * n
    c_refs = refs[:m]
    f_refs, dh_refs, dy_refs = refs[m : m + n], refs[m + n : m + 2 * n], refs[m + 2 * n : m + 3 * n]
    send_ref, keep_ref = refs[m + 3 * n :]
    per = m // n
    for target, half in ((send_ref, 1 - (pos_ref[0] & 1)), (keep_ref, pos_ref[0] & 1)):
        at = pl.ds(pl.multiple_of(half * 256, 256), 256)
        total1 = total2 = None
        for i in range(n):
            c = [ref[:, at] for ref in c_refs[i * per : (i + 1) * per]]
            c = c[0] if per == 1 else jnp.concatenate(c, axis=0)
            part1 = dot(c, dh_refs[i][...], 0, 0)
            part2 = dot(f_refs[i][...], dy_refs[i][:, at], 0, 0)
            total1 = part1 if total1 is None else total1 + part1
            total2 = part2 if total2 is None else total2 + part2
        target[0:256] = total1.astype(BF16)
        for block in range(total2.shape[0] // 256):
            rows = slice(block * 256, (block + 1) * 256)
            target[256:512, rows] = total2[rows].astype(BF16)


def cut_kernel(a_ref, b_ref, *outs):
    row = 0
    for out in outs:
        rows = slice(row, row + out.shape[0])
        out[...] = (a_ref[rows].astype(F32) + b_ref[rows].astype(F32)).astype(BF16)
        row += out.shape[0]


def glue_kernel(*refs):
    n, row = (len(refs) - 1) // 2, 0
    for a_ref, b_ref in zip(refs[:n], refs[n : 2 * n]):
        refs[-1][row : row + a_ref.shape[0]] = (a_ref[...].astype(F32) + b_ref[...].astype(F32)).astype(BF16)
        row += a_ref.shape[0]


def join_rows_kernel(pos_ref, own_ref, other_ref, out_ref):
    core = pos_ref[0] & 1
    for mine, ref in ((core, own_ref), (1 - core, other_ref)):
        out_ref[pl.ds(pl.multiple_of(mine * 256, 256), 256)] = ref[...].astype(F32)


def join_columns_kernel(pos_ref, own_ref, other_ref, out_ref):
    core = pos_ref[0] & 1
    for mine, ref in ((core, own_ref), (1 - core, other_ref)):
        at = pl.ds(pl.multiple_of(mine * 256, 256), 256)
        for block in range(FF // 256):
            rows = slice(block * 256, (block + 1) * 256)
            out_ref[rows, at] = ref[:, rows].astype(F32)


def arrange_kernel(pos_ref, *refs):
    for k, ref in enumerate(refs[:-1]):
        refs[-1][pos_ref[1] ^ k] = ref[...]


def one_hot_columns(index_ref, width):
    place = lax.broadcasted_iota(jnp.int32, (index_ref.shape[0], width), 1)
    hit = (place == index_ref[:, 0:1]) | (place == index_ref[:, 1:2])
    return jnp.where(hit, 1.0, 0.0).astype(BF16)


def combine_kernel(
    slots, pos_ref, x_ref, gain_ref, router_ref, ids_ref, index_ref, turned_ref, c_ref, gate_ref, cot_ref, *refs
):
    blocks, (dx_ref, dgain_ref, drouter_ref) = refs[:-3], refs[-3:]
    each = blocks[0].shape[0] // slots
    experts = len(blocks) * each
    tokens = x_ref.shape[0]
    dgates = [jnp.zeros((1, tokens), F32) for _ in range(TOP)]
    gc = None
    for k in range(experts):
        at = k % each * slots
        block = blocks[k // each][at : at + slots]
        start = (pos_ref[1] ^ k) * slots
        place = lax.broadcasted_iota(jnp.int32, (tokens, slots), 1) + start
        hit = (place == turned_ref[:, 0:1]) | (place == turned_ref[:, 1:2])
        part = dot(jnp.where(hit, 1.0, 0.0).astype(BF16), block)
        gc = part if gc is None else gc + part
        place = lax.broadcasted_iota(jnp.int32, (slots, tokens), 0) + start
        column = read_spare(block[slots - 8 :].astype(F32), slots)
        for j in range(TOP):
            hit = place == index_ref[j : j + 1, :]
            dgates[j] = dgates[j] + jnp.sum(jnp.where(hit, column, 0.0), axis=0, keepdims=True)
    dl = gate_ref[0:1] * gate_ref[1:2] * (dgates[0] - dgates[1])
    expert = lax.broadcasted_iota(jnp.int32, (experts, tokens), 0)
    dlogits = jnp.where(ids_ref[0:1, :] == expert, dl, 0.0) - jnp.where(ids_ref[1:2, :] == expert, dl, 0.0)
    dlogits = dlogits.astype(BF16)
    gc = gc + dot(dlogits, router_ref[...].astype(BF16), 0, 0)
    drouter_ref[...] = dot(dlogits, c_ref[...])
    unit, scale = unit_rows(x_ref[...])
    dx, dgain = norm_backward(unit, scale, gain_ref[...], gc)
    dx_ref[...] = cot_ref[...].astype(F32) + dx
    dgain_ref[...] = dgain


def split_cube_kernel(n, pos_ref, *refs):
    kept, came, out_ref = refs[0:n], refs[n : 2 * n], refs[2 * n]
    for place in range(2):
        for half in range(2):
            x = (pos_ref[1] & 1) ^ (1 - half)
            y = (pos_ref[0] >> 1) ^ (1 - place)
            row = 0
            for keep, new in zip(kept, came):
                total = (keep[place, half].astype(F32) + new[place, half].astype(F32)).astype(BF16)
                for start in range(0, keep.shape[2], 64):
                    for depth in range(2):
                        at = start + depth * STRIP
                        out_ref[depth * 4 + x * 2 + y, row : row + STRIP] = total[at : at + STRIP]
                    row += STRIP


def sum_cube_kernel(a_ref, out_ref):
    total = a_ref[0].astype(F32)
    for k in range(1, a_ref.shape[0]):
        total = total + a_ref[k].astype(F32)
    out_ref[...] = total.astype(BF16)


def sum_kernel(*refs):
    total = refs[0][...].astype(F32)
    for ref in refs[1:-1]:
        total = total + ref[...].astype(F32)
    refs[-1][...] = total.astype(BF16)


def rows_of(pos_ref, k):
    source = pos_ref[1] ^ k
    return pl.ds(pl.multiple_of((source & 1) * 64 + (source >> 1 & 1) * STRIP, STRIP), STRIP)


def finish_mlp_kernel(pos_ref, *refs):
    mlp1_ref, mlp2_ref = refs[4:]
    for k in range(4):
        there = rows_of(pos_ref, k)
        mlp1_ref[there] = refs[k][STRIP : 2 * STRIP].astype(F32)
        for part in range(4):
            mlp2_ref[part, there] = refs[k][2 * STRIP :, part * 512 : (part + 1) * 512].astype(F32)


def finish_attention_kernel(pos_ref, *refs):
    in_ref, out_ref, small_ref = refs[8:]
    for k in range(4):
        there = rows_of(pos_ref, k)
        for layer, ref in ((0, refs[k]), (1, refs[4 + k])):
            in_ref[layer, there] = ref[0:STRIP, 0 : 3 * D].astype(F32)
            out_ref[layer, there] = ref[0:STRIP, 3 * D : 4 * D].astype(F32)
    for group in range(small_ref.shape[0] // STRIP):
        at = 4 * D + group * 128
        small_ref[group * STRIP : (group + 1) * STRIP] = refs[0][:, at : at + 128].astype(F32)


def final_kernel(blocks_ref, x_ref, turned_ref, out_ref):
    out_ref[...] = (x_ref[...] + dot(one_hot_columns(turned_ref, blocks_ref.shape[0]), blocks_ref[...])).astype(BF16)


def spent(us):
    return pl.CostEstimate(flops=int(us * 1.0e9), bytes_accessed=0, transcendentals=0)


def call(kernel, outs, *args, us=1.0, scratch=(), specs=None, room=40, **more):
    return list(
        pl.pallas_call(
        kernel,
        out_shape=[(pltpu.HBM if rest else jax.ShapeDtypeStruct)(shape, kind) for shape, kind, *rest in outs],
        in_specs=specs if specs is not None else [WHOLE] * len(args),
        out_specs=[WHOLE] * len(outs),
        scratch_shapes=list(scratch),
        cost_estimate=spent(us),
        compiler_params=pltpu.CompilerParams(vmem_limit_bytes=room * 1024 * 1024),
        **more,
        )(*args)
    )


WHOLE = pl.BlockSpec(memory_space=pltpu.VMEM)
SCALAR = pl.BlockSpec(memory_space=pltpu.SMEM)
AWAY = pl.BlockSpec(memory_space=pltpu.HBM)


def flip(array, axis, bit):
    return lax.ppermute(array, axis, [(i, i ^ bit) for i in range(lax.axis_size(axis))])


def gather_pieces(piece, across=None):
    across = flip(piece, "wshard", 2) if across is None else across
    return (piece, flip(piece, "wshard", 1), across, flip(across, "wshard", 1))


def after(array, *others):
    return lax.optimization_barrier((array, *others))[0]


def split_cube(pos, bundle):
    came = [flip(send, "wshard", 1) for send, _ in bundle]
    tall = sum(keep.shape[2] for _, keep in bundle)
    wide = bundle[0][0].shape[-1]
    return call(
        functools.partial(split_cube_kernel, len(bundle)),
        [((8, tall // 2, wide), BF16, AWAY)],
        pos,
        *[keep for _, keep in bundle],
        *came,
        specs=[SCALAR] + [WHOLE] * (2 * len(bundle)),
        us=3.0,
    )[0]


def trade_cube(blocks):
    inner = lax.axis_size("wshard")
    groups = [
        [((2 * z + depth) * 2 + x) * inner + y * 2 + core for depth in range(2) for x in range(2) for y in range(2)]
        for z in range(lax.axis_size("expert") // 4)
        for core in range(2)
    ]
    return lax.all_to_all(blocks, ("expert", "wshard"), 0, 0, axis_index_groups=groups, tiled=True)


def sum_cube(blocks):
    return call(sum_cube_kernel, [(blocks.shape[1:], BF16, AWAY)], blocks, us=2.0)[0]


def sum_two(strip, other):
    return call(sum_kernel, [(strip.shape, BF16, AWAY)], strip, other)[0]


def spread(strip):
    return [strip] + [flip(strip, "expert", k) for k in range(1, 4)]


def sum_plainly(send, keep):
    half = (keep.astype(F32) + flip(send, "wshard", 1).astype(F32)).astype(BF16)
    rows = half[1].astype(F32) + flip(half[0], "wshard", 2).astype(F32)
    return lax.psum(jnp.concatenate([rows[1], rows[0]], axis=0), "expert")


def expand(rows, images):
    return jnp.pad(rows.reshape(images, SEQ, -1), ((0, 0), (0, PAD - SEQ), (0, 0))).reshape(images * PAD, -1)


def contract(rows, images):
    return rows.reshape(images, PAD, -1)[:, :SEQ].reshape(images * SEQ, -1)


def local(
    images, attn_in, attn_out, norm_gains, mlp_in, mlp_out, router, expert_in, expert_out, expert_ids, cotangent
):
    owners = lax.axis_size("expert")
    experts = owners * expert_in.shape[0]
    tokens = images.shape[0]
    pictures = tokens // SEQ
    rows = pictures * PAD
    capacity = max(2, 2 * TOP * tokens // experts)
    slots = (capacity + 8 + 15) // 16 * 16
    every = experts * slots
    linked = owners == LINKED
    own = lax.axis_index("expert") if linked else 0
    pos = jnp.stack([lax.axis_index("wshard"), own]).astype(jnp.int32)

    small = jnp.concatenate([norm_gains, router.T], axis=0)
    small = jnp.pad(small, ((0, -small.shape[0] % 16), (0, 0)))
    (small_full,) = call(
        small_kernel, [((small.shape[0], D), F32)], pos, *gather_pieces(small), specs=[SCALAR] + [WHOLE] * 4
    )
    gains = [small_full[i : i + 1] for i in range(4)]
    router_full = small_full[4 : 4 + experts]

    wi0 = flip(attn_in[0], "wshard", 2)
    wo0 = flip(attn_out[0], "wshard", 2)
    w1_across = flip(after(mlp_in, wi0), "wshard", 2)
    w2_across = flip(after(mlp_out, wi0), "wshard", 2)
    wi1 = flip(after(attn_in[1], w1_across), "wshard", 2)
    wo1 = flip(after(attn_out[1], w1_across), "wshard", 2)
    wi = [gather_pieces(attn_in[0], wi0), None]
    wo = [gather_pieces(attn_out[0], wo0), None]
    x0 = expand(images, pictures)

    weight_specs = [AWAY] * 8
    attn_scratch = [pltpu.VMEM((4, D // 4, 3 * D), BF16), pltpu.VMEM((4, D // 4, D), BF16)]
    mlp_scratch = [pltpu.VMEM((4, D // 4, FF), BF16), pltpu.VMEM((4, FF // 4, D), BF16)]
    sems = pltpu.SemaphoreType.DMA((8,))

    def attend(x, layer):
        return call(
            attend_forward_kernel,
            [((rows, D), F32), ((rows, 3 * D), BF16), ((rows, D), BF16)],
            pos, x, gains[2 * layer], *wi[layer], *wo[layer],
            specs=[SCALAR, WHOLE, WHOLE] + weight_specs,
            scratch=attn_scratch + [sems],
            us=7.0,
        )

    def attend_back(x, layer, packed, o, dz, extra):
        wide = 4 * D
        if extra:
            wide += (sum(a.shape[0] for a in extra) + 1 + STRIP - 1) // STRIP * 128
        return call(
            functools.partial(attend_backward_kernel, len(extra)),
            [((rows, D), F32), ((1, D), F32), ((2, 2, 64, wide), BF16, AWAY), ((2, 2, 64, wide), BF16, AWAY)],
            pos, x, gains[2 * layer], packed, o, dz, *wi[layer], *wo[layer], *extra,
            specs=[SCALAR] + [WHOLE] * 5 + weight_specs + [WHOLE] * len(extra),
            scratch=attn_scratch
            + [pltpu.VMEM((rows, 3 * D), BF16)]
            + [pltpu.VMEM((rows, D), BF16)] * 3
            + [sems],
            us=12.5,
            room=58,
        )

    x1, packed1, o1 = attend(x0, 0)
    ids = jnp.pad(after(expert_ids, x1).T.reshape(TOP, pictures, SEQ), ((0, 8 - TOP), (0, 0), (0, PAD - SEQ)), constant_values=-1)
    ids = ids.reshape(8, rows)
    cot = expand(after(cotangent, x1), pictures)

    index, g_out = call(
        functools.partial(routing_kernel, slots), [((8, rows), jnp.int32), ((every, D), BF16)], ids, cot, us=3.4
    )
    turned = index.T
    trade = functools.partial(lax.all_to_all, axis_name="expert", split_axis=0, concat_axis=0, tiled=True)
    g_in = trade(g_out.reshape(experts, slots, D))

    w1 = gather_pieces(mlp_in, after(w1_across, x1))
    w2 = gather_pieces(mlp_out, after(w2_across, x1))
    (x2,) = call(
        feed_forward_kernel, [((rows, D), F32)], pos, x1, gains[1], *w1, *w2,
        specs=[SCALAR, WHOLE, WHOLE] + weight_specs, scratch=mlp_scratch + [sems], us=6.5,
    )
    wi[1] = gather_pieces(attn_in[1], after(wi1, x2))
    wo[1] = gather_pieces(attn_out[1], after(wo1, x2))
    x3, packed2, o2 = attend(x2, 1)
    arrays = experts if linked else max(1, experts // (2 * PAD // slots))
    each = experts // arrays
    c, gate, *c_out = call(
        functools.partial(dispatch_kernel, slots),
        [((rows, D), BF16), ((8, rows), F32)] + [((each * slots, D), BF16, AWAY)] * arrays,
        pos, x3, gains[3], router_full, ids, index,
        specs=[SCALAR] + [WHOLE] * 5,
        us=4.6,
    )

    def swap(blocks, first=0):
        if linked:
            return [flip(block, "expert", k) if k else block for k, block in enumerate(blocks, first)]
        moved = trade(jnp.concatenate(blocks).reshape(experts, slots, D))
        return list(moved.reshape(arrays, each * slots, D))

    c_in = swap(c_out)
    per = 2 if linked else 1
    work = []
    dc_out, z_out, dc_in = [], [], []
    for first in range(0, arrays, per):
        given = c_in[first : first + per]
        if linked and first >= 2 * per:
            given[0], *dc_in[-2 * per : -per] = lax.optimization_barrier((given[0], *dc_in[-2 * per : -per]))
        count = list(range(first * each, (first + per) * each))
        tall = len(count) * slots
        fixed = lambda *shape: pl.BlockSpec(shape, lambda j, pos_ref: (0,) * len(shape))
        source = lambda k: pl.BlockSpec((1, slots, D), lambda j, pos_ref: (pos_ref[1] ^ k, 0, 0))
        across = lambda height: pl.BlockSpec((height, 1024), lambda j, pos_ref: (0, j))
        *made, f, dh, dy = pl.pallas_call(
            functools.partial(experts_kernel, slots, per, each),
            out_shape=[pltpu.HBM((each * slots, D), BF16)] * (2 * per)
            + [pltpu.HBM((tall, FF), BF16)] * 2
            + [pltpu.HBM((tall, D), BF16)],
            grid_spec=pltpu.PrefetchScalarGridSpec(
                num_scalar_prefetch=1,
                grid=(FF // 1024,),
                in_specs=[across(D), pl.BlockSpec((1024, D), lambda j, pos_ref: (j, 0))]
                + [source(k) for k in count]
                + [fixed(each * slots, D)] * per,
                out_specs=[fixed(each * slots, D)] * (2 * per) + [across(tall)] * 2 + [fixed(tall, D)],
                scratch_shapes=[pltpu.VMEM((tall, 128), F32), pltpu.VMEM((tall, D), F32), pltpu.VMEM((tall, D), F32)],
            ),
            cost_estimate=spent(8.0),
            compiler_params=pltpu.CompilerParams(vmem_limit_bytes=VMEM_LIMIT),
        )(pos, expert_in[0], expert_out[0], *[g_in] * len(count), *given)
        dc_out += made[:per]
        z_out += made[per:]
        if linked:
            dc_in += swap(made[:per], first)
        work.append((f, dh, dy))
    if not linked:
        dc_in = swap(dc_out)
    if linked:
        (z_block,) = call(
            arrange_kernel, [((experts, slots, D), BF16, AWAY)], pos, *z_out, specs=[SCALAR] + [WHOLE] * experts, us=2.0
        )
    else:
        z_block = jnp.concatenate(z_out).reshape(experts, slots, D)
    n = len(work)
    whole_rows = lambda a: pl.BlockSpec(a.shape, lambda j: (0, 0))
    chunk = lambda a: pl.BlockSpec((a.shape[0], 1024), lambda j: (0, j))
    fs, dhs, dys = ([w[i] for w in work] for i in range(3))
    if linked:
        dys[0], *dc_in[per : 2 * per] = lax.optimization_barrier((dys[0], *dc_in[per : 2 * per]))
    grad_send, grad_keep = pl.pallas_call(
        functools.partial(expert_grads_kernel, n),
        grid=(FF // 1024,),
        in_specs=[SCALAR]
        + [whole_rows(a) for a in c_in]
        + [chunk(a) for a in fs + dhs]
        + [whole_rows(a) for a in dys],
        out_specs=[pl.BlockSpec((512, 1024), lambda j: (0, j))] * 2,
        out_shape=[pltpu.HBM((512, FF), BF16)] * 2,
        cost_estimate=spent(10.0),
        compiler_params=pltpu.CompilerParams(vmem_limit_bytes=VMEM_LIMIT),
    )(pos, *c_in, *fs, *dhs, *dys)
    x3_late, z_block, grad_send, grad_keep = lax.optimization_barrier((x3, z_block, grad_send, grad_keep))
    g3, gain3, drouter = call(
        functools.partial(combine_kernel, slots),
        [((rows, D), F32), ((1, D), F32), ((experts, D), F32)],
        pos, x3_late, gains[3], router_full, ids, index, turned, c, gate, cot, *dc_in,
        specs=[SCALAR] + [WHOLE] * (9 + arrays),
        us=5.5,
    )
    g3, z_block, grad_send = lax.optimization_barrier((g3, z_block, grad_send))
    z_in = trade(z_block)
    grads = call(
        cut_kernel,
        [((tall, FF), BF16, AWAY) for tall in (128, 128, 256)],
        grad_keep, flip(grad_send, "wshard", 1),
        us=2.0,
    )
    g3 = after(g3, *grads)
    crossed = [flip(piece, "wshard", 2) for piece in grads[:2]]
    g2, gain2, *second = attend_back(x2, 1, packed2, o2, g3, [])
    g1, gain1, *mlp = call(
        feed_backward_kernel,
        [((rows, D), F32), ((1, D), F32)] + [((2, 2, 128, FF), BF16, AWAY)] * 2,
        pos, x1, gains[1], g2, *w1, *w2,
        specs=[SCALAR, WHOLE, WHOLE, WHOLE] + weight_specs,
        scratch=mlp_scratch + [pltpu.VMEM((D, FF), BF16), pltpu.VMEM((FF, D), BF16), sems],
        us=12.5,
        room=58,
    )
    *second, mlp[0], mlp[1], crossed[0], crossed[1] = lax.optimization_barrier(
        (*second, mlp[0], mlp[1], crossed[0], crossed[1])
    )
    if linked:
        bulk = split_cube(pos, [second, mlp])
        g1 = after(g1, z_in, bulk)
        bulk = trade_cube(bulk)
    dx, _, *first = attend_back(x0, 0, packed1, o1, g1, [gain1, gain2, gain3, drouter])
    (final,) = call(final_kernel, [((rows, D), BF16)], z_in.reshape(every, D), x3, turned, us=3.5)

    wide = first[0].shape[-1]

    def join(kernel, shape, pieces, came):
        (half,) = call(glue_kernel, [((256, FF), BF16, AWAY)], *pieces, *came)
        return call(
            kernel, [(shape, F32)], pos, half, flip(half, "wshard", 1), specs=[SCALAR] + [WHOLE] * 2, us=2.0
        )[0]

    expert1 = join(join_rows_kernel, (D, FF), [after(grads[0], dx), grads[1]], crossed)
    if linked:
        tail = split_cube(pos, [(first[0], after(first[1], final))])
        final_rows, input_grad = contract(final, pictures), contract(dx, pictures)
        bulk = sum_cube(after(bulk, tail, final_rows, input_grad))
        deep = flip(bulk, "expert", 4)
        tail = sum_cube(after(trade_cube(after(tail, bulk)), deep, expert1))
        last = flip(after(grads[2], tail), "wshard", 2)
        bulk = spread(sum_two(bulk, deep))
        tail = sum_two(tail, flip(tail, "expert", 4))
        last = after(last, tail, *bulk)
        tail = spread(tail)
        mlp1, mlp2 = call(
            finish_mlp_kernel,
            [((D // 4, FF), F32), ((4, 128, D), F32)],
            pos, *bulk, specs=[SCALAR] + [WHOLE] * 4, us=2.0,
        )
        grad_in, grad_out, smalls = call(
            finish_attention_kernel,
            [((2, D // 4, 3 * D), F32), ((2, D // 4, D), F32), (((wide - 4 * D) // 128 * STRIP, 128), F32)],
            pos, *tail, *bulk, specs=[SCALAR] + [WHOLE] * 8, us=2.0,
        )
        mlp2 = mlp2.reshape(FF // 4, D)
    else:
        last = flip(grads[2], "wshard", 2)
        first, second, mlp = sum_plainly(*first), sum_plainly(*second), sum_plainly(*mlp)
        grad_in = jnp.stack([first[:, : 3 * D], second[:, : 3 * D]])
        grad_out = jnp.stack([first[:, 3 * D : 4 * D], second[:, 3 * D :]])
        smalls = first[:STRIP, 4 * D :].reshape(STRIP, -1, 128).transpose(1, 0, 2).reshape(-1, 128)
        mlp1 = jnp.concatenate([mlp[0:64], mlp[128:192]], axis=0)
        final_rows, input_grad = contract(final, pictures), contract(dx, pictures)
        mlp2 = jnp.stack([mlp[64:128], mlp[192:256]]).reshape(2, 64, 4, D).transpose(2, 0, 1, 3).reshape(FF // 4, D)

    expert2 = join(join_columns_kernel, (FF, D), grads[2:], [last])
    return (
        final_rows,
        input_grad,
        grad_in,
        grad_out,
        smalls[0:4],
        mlp1,
        mlp2,
        smalls[4 : 4 + experts].T,
        expert1[None],
        expert2[None],
    )


def solution(mesh):
    rows = P(("expert", "wshard"), None)
    dense = (P(None, "wshard", None), P(None, "wshard", None), P(None, "wshard"))
    shards = (P("wshard", None),) * 3
    experts = (P("expert", None, None),) * 2
    return jax.shard_map(
        local,
        mesh=mesh,
        in_specs=(rows, *dense, *shards, *experts, rows, rows),
        out_specs=(rows, rows, *dense, *shards, *experts),
        check_vma=False,
    )
```

```python
import functools

import jax
import jax.numpy as jnp
from jax import lax
from jax.experimental import pallas as pl
from jax.experimental.pallas import tpu as pltpu
from jax.sharding import PartitionSpec as P

D = 512
HEADS = 8
FF = 2048
SEQ = 197
TOP = 2
HEAD_DIM = 64
PAD = 208
STRIP = 32
CHUNK = 512
EPSILON = 1e-06
ROOT_2_PI = 0.7978845608028654
CUBIC = 0.044715

F32 = jnp.float32
BF16 = jnp.bfloat16
VMEM_LIMIT = 40 * 1024 * 1024
LINKED = 8


def dot(a, b, ca=1, cb=0):
    return lax.dot_general(a, b, (((ca,), (cb,)), ((), ())), preferred_element_type=F32)


def unit_rows(rows):
    centred = rows - jnp.mean(rows, axis=-1, keepdims=True)
    scale = lax.rsqrt(jnp.mean(centred * centred, axis=-1, keepdims=True) + EPSILON)
    return centred * scale, scale


def norm_backward(unit, scale, gain, grad):
    scaled = gain * grad
    inner = (
        scaled
        - jnp.mean(scaled, axis=-1, keepdims=True)
        - unit * jnp.mean(scaled * unit, axis=-1, keepdims=True)
    )
    return inner * scale, jnp.sum(grad * unit, axis=0, keepdims=True)


def gelu_parts(h):
    square = h * h
    t = jnp.tanh(ROOT_2_PI * h * (1.0 + CUBIC * square))
    half = 0.5 * (1.0 + t)
    slope = half + 0.5 * h * (1.0 - t * t) * (ROOT_2_PI * (1.0 + 3.0 * CUBIC * square))
    return h * half, slope


def gelu(h):
    return 0.5 * h * (1.0 + jnp.tanh(ROOT_2_PI * h * (1.0 + CUBIC * h * h)))


def start_weight(pos_ref, pieces, held, sems, first):
    copies = []
    for j, piece in enumerate(pieces):
        copy = pltpu.make_async_copy(piece, held.at[pos_ref[0] ^ j], sems.at[first + j])
        copy.start()
        copies.append(copy)
    return copies


def wait_all(copies):
    for copy in copies:
        copy.wait()


def softmax_rows(q, k):
    scores = dot(q, k, 1, 1) * (HEAD_DIM**-0.5)
    column = lax.broadcasted_iota(jnp.int32, scores.shape, 1)
    scores = jnp.where(column < SEQ, scores, -1e30)
    raised = jnp.exp(scores - jnp.max(scores, axis=-1, keepdims=True))
    return raised * (1.0 / jnp.sum(raised, axis=-1, keepdims=True))


def shards_of(pos_ref, send_ref, keep_ref):
    for target, turn in ((send_ref, 1), (keep_ref, 0)):
        for place in range(2):
            yield target, place, pos_ref[0] ^ (turn + 2 * (1 - place))


def own_half(pos_ref, half):
    return 1 - ((pos_ref[1] & 1) ^ half)


def attend_forward_kernel(pos_ref, x_ref, gain_ref, *refs):
    wi, wo = refs[0:4], refs[4:8]
    y_ref, packed_ref, o_ref, wi_held, wo_held, sems = refs[8:]
    wi_copies = start_weight(pos_ref, wi, wi_held, sems, 0)
    wo_copies = start_weight(pos_ref, wo, wo_held, sems, 4)
    rows = x_ref[...].astype(F32)
    unit, _ = unit_rows(rows)
    normed = (unit * gain_ref[...]).astype(BF16)
    wait_all(wi_copies)
    packed_ref[...] = dot(normed, wi_held[...].reshape(D, 3 * D)).astype(BF16)
    lane = lax.broadcasted_iota(jnp.int32, (PAD, 2 * HEAD_DIM), 1)
    for image in range(x_ref.shape[0] // PAD):
        here = pl.ds(image * PAD, PAD)
        for pair in range(HEADS // 2):
            at = pair * 2 * HEAD_DIM
            q = packed_ref[here, at : at + 128]
            k = packed_ref[here, D + at : D + at + 128]
            v = packed_ref[here, 2 * D + at : 2 * D + at + 128]
            total = None
            for side in range(2):
                mine = (lane >= HEAD_DIM) == bool(side)
                chances = softmax_rows(jnp.where(mine, q, jnp.zeros_like(q)), k).astype(BF16)
                part = dot(chances, jnp.where(mine, v, jnp.zeros_like(v)))
                total = part if total is None else total + part
            o_ref[here, at : at + 128] = total.astype(BF16)
    wait_all(wo_copies)
    y_ref[...] = x_ref[...].astype(F32) + dot(o_ref[...], wo_held[...].reshape(D, D))


def attend_backward_kernel(smalls, pos_ref, x_ref, gain_ref, packed_ref, o_ref, dz_ref, *refs):
    wi, wo = refs[0:4], refs[4:8]
    extra = refs[8 : 8 + smalls]
    dx_ref, dgain_ref, send_ref, keep_ref, wi_held, wo_held, dp_ref, dout_ref, do_ref, normed_ref, sems = refs[
        8 + smalls :
    ]
    wo_copies = start_weight(pos_ref, wo, wo_held, sems, 4)
    wi_copies = start_weight(pos_ref, wi, wi_held, sems, 0)
    unit, scale = unit_rows(x_ref[...].astype(F32))
    gain = gain_ref[...]
    normed_ref[...] = (unit * gain).astype(BF16)
    dout_ref[...] = dz_ref[...].astype(BF16)
    wait_all(wo_copies)
    do_ref[...] = dot(dout_ref[...], wo_held[...].reshape(D, D), 1, 1).astype(BF16)
    lane = lax.broadcasted_iota(jnp.int32, (PAD, 2 * HEAD_DIM), 1)
    factor = HEAD_DIM**-0.5
    for image in range(x_ref.shape[0] // PAD):
        here = pl.ds(image * PAD, PAD)
        for pair in range(HEADS // 2):
            at = pair * 2 * HEAD_DIM
            q = packed_ref[here, at : at + 128]
            k = packed_ref[here, D + at : D + at + 128]
            v = packed_ref[here, 2 * D + at : 2 * D + at + 128]
            do = do_ref[here, at : at + 128]
            dq = dk = dv = None
            for side in range(2):
                mine = (lane >= HEAD_DIM) == bool(side)
                own = lambda a: jnp.where(mine, a, jnp.zeros_like(a))
                q_own, k_own, do_own = own(q), own(k), own(do)
                chances = softmax_rows(q_own, k)
                dv_part = dot(chances.astype(BF16), do_own, 0, 0)
                da = dot(do_own, v, 1, 1)
                ds = chances * (da - jnp.sum(da * chances, axis=-1, keepdims=True))
                ds = ds.astype(BF16)
                dq_part = dot(ds, k_own)
                dk_part = dot(ds, q_own, 0, 0)
                dq = dq_part if dq is None else dq + dq_part
                dk = dk_part if dk is None else dk + dk_part
                dv = dv_part if dv is None else dv + dv_part
            dp_ref[here, at : at + 128] = (dq * factor).astype(BF16)
            dp_ref[here, D + at : D + at + 128] = (dk * factor).astype(BF16)
            dp_ref[here, 2 * D + at : 2 * D + at + 128] = dv.astype(BF16)
    wait_all(wi_copies)
    dn = dot(dp_ref[...], wi_held[...].reshape(D, 3 * D), 1, 1)
    unit, scale = unit_rows(x_ref[...].astype(F32))
    dx, dgain = norm_backward(unit, scale, gain, dn)
    dx_ref[...] = dz_ref[...] + dx
    dgain_ref[...] = dgain
    for target, place, shard in shards_of(pos_ref, send_ref, keep_ref):
        columns = pl.ds(pl.multiple_of(shard * 128, 128), 128)
        grad_in = dot(normed_ref[:, columns], dp_ref[...], 0, 0).astype(BF16)
        grad_out = dot(o_ref[:, columns], dout_ref[...], 0, 0).astype(BF16)
        for half in range(2):
            there = own_half(pos_ref, half)
            target[place, there, :, 0 : 3 * D] = grad_in[half * 64 : half * 64 + 64]
            target[place, there, :, 3 * D : 4 * D] = grad_out[half * 64 : half * 64 + 64]
    if smalls:
        small = jnp.concatenate([dgain] + [ref[...] for ref in extra], axis=0)
        small = jnp.concatenate([small, jnp.zeros((-small.shape[0] % STRIP, D), F32)], axis=0)
        for target, place, shard in shards_of(pos_ref, send_ref, keep_ref):
            piece = jnp.zeros((small.shape[0], 128), F32)
            for s in range(4):
                piece = jnp.where(shard == s, small[:, s * 128 : (s + 1) * 128], piece)
            piece = piece.astype(BF16)
            for half in range(2):
                for strip in range(64 // STRIP):
                    for group in range(small.shape[0] // STRIP):
                        at = 4 * D + group * 128
                        target[place, half, strip * STRIP : (strip + 1) * STRIP, at : at + 128] = piece[
                            group * STRIP : (group + 1) * STRIP
                        ]


def feed_forward_kernel(pos_ref, x_ref, gain_ref, *refs):
    w1, w2 = refs[0:4], refs[4:8]
    y_ref, w1_held, w2_held, sems = refs[8:]
    w1_copies = start_weight(pos_ref, w1, w1_held, sems, 0)
    w2_copies = start_weight(pos_ref, w2, w2_held, sems, 4)
    unit, _ = unit_rows(x_ref[...])
    normed = (unit * gain_ref[...]).astype(BF16)
    wait_all(w1_copies)
    total = x_ref[...]
    for j in range(FF // 1024):
        at = slice(j * 1024, (j + 1) * 1024)
        active = gelu(dot(normed, w1_held[:, :, at].reshape(D, 1024))).astype(BF16)
        if j == 0:
            wait_all(w2_copies)
        total = total + dot(active, w2_held[...].reshape(FF, D)[at])
    y_ref[...] = total


def feed_backward_kernel(pos_ref, x_ref, gain_ref, dz_ref, *refs):
    w1, w2 = refs[0:4], refs[4:8]
    dx_ref, dgain_ref, send_ref, keep_ref, w1_held, w2_held, g1_ref, g2_ref, sems = refs[8:]
    w1_copies = start_weight(pos_ref, w1, w1_held, sems, 0)
    w2_copies = start_weight(pos_ref, w2, w2_held, sems, 4)
    unit, scale = unit_rows(x_ref[...])
    gain = gain_ref[...]
    normed = (unit * gain).astype(BF16)
    dout = dz_ref[...].astype(BF16)
    wait_all(w1_copies)
    wait_all(w2_copies)
    dn = None
    for j in range(FF // 1024):
        at = slice(j * 1024, (j + 1) * 1024)
        w1_now = w1_held[:, :, at].reshape(D, 1024)
        w2_now = w2_held[...].reshape(FF, D)[at]
        active, slope = gelu_parts(dot(normed, w1_now))
        dh = (slope * dot(dout, w2_now, 1, 1)).astype(BF16)
        g2_ref[at] = dot(active.astype(BF16), dout, 0, 0).astype(BF16)
        g1_ref[:, at] = dot(normed, dh, 0, 0).astype(BF16)
        part = dot(dh, w1_now, 1, 1)
        dn = part if dn is None else dn + part
    dx, dgain = norm_backward(unit, scale, gain, dn)
    dx_ref[...] = dz_ref[...] + dx
    dgain_ref[...] = dgain
    for target, place, shard in shards_of(pos_ref, send_ref, keep_ref):
        for half in range(2):
            there = own_half(pos_ref, half)
            target[place, there, 0:64] = g1_ref[pl.ds(pl.multiple_of(shard * 128 + half * 64, 64), 64)]
            for part in range(4):
                start = pl.multiple_of(shard * 512 + part * 128 + half * 64, 64)
                target[place, there, 64:128, part * 512 : (part + 1) * 512] = g2_ref[pl.ds(start, 64)]


def routing_kernel(slots, ids_ref, cot_ref, index_ref, blocks_ref):
    experts = blocks_ref.shape[0] // slots
    tokens = ids_ref.shape[1]
    expert = lax.broadcasted_iota(jnp.int32, (experts, tokens), 0)
    named = [ids_ref[k : k + 1, :] == expert for k in range(TOP)]
    matches = jnp.where(named[0] | named[1], 1.0, 0.0).astype(BF16)
    earlier = lax.broadcasted_iota(jnp.int32, (tokens, tokens), 0) < lax.broadcasted_iota(
        jnp.int32, (tokens, tokens), 1
    )
    rank = dot(matches, jnp.where(earlier, 1.0, 0.0).astype(BF16))
    index_ref[...] = jnp.full(index_ref.shape, -1, jnp.int32)
    place = lax.broadcasted_iota(jnp.int32, (blocks_ref.shape[0], tokens), 0)
    chosen = None
    for k in range(TOP):
        slot = jnp.sum(jnp.where(named[k], rank, 0.0), axis=0, keepdims=True).astype(jnp.int32)
        index = ids_ref[k : k + 1, :] * slots + slot
        index_ref[k : k + 1, :] = index
        hit = place == index
        chosen = hit if chosen is None else chosen | hit
    blocks_ref[...] = dot(jnp.where(chosen, 1.0, 0.0).astype(BF16), cot_ref[...]).astype(BF16)


def write_spare(slots, column):
    eye = lax.broadcasted_iota(jnp.int32, (slots, D), 0) == lax.broadcasted_iota(jnp.int32, (slots, D), 1)
    line = jnp.sum(jnp.where(eye, column, 0.0), axis=0, keepdims=True)
    high = line.astype(BF16).astype(F32)
    middle = (line - high).astype(BF16).astype(F32)
    low = line - high - middle
    row = lax.broadcasted_iota(jnp.int32, (8, D), 0)
    return jnp.where(row == 0, high, jnp.where(row == 1, middle, jnp.where(row == 2, low, 0.0)))


def read_spare(tile, slots):
    line = tile[0:1] + tile[1:2] + tile[2:3]
    eye = lax.broadcasted_iota(jnp.int32, (slots, D), 0) == lax.broadcasted_iota(jnp.int32, (slots, D), 1)
    return jnp.sum(jnp.where(eye, line, 0.0), axis=1, keepdims=True)


def small_kernel(pos_ref, *refs):
    out_ref = refs[4]
    for j in range(4):
        start = pl.multiple_of((pos_ref[0] ^ j) * 128, 128)
        out_ref[:, pl.ds(start, 128)] = refs[j][...].astype(F32)


def dispatch_kernel(slots, pos_ref, x_ref, gain_ref, router_ref, ids_ref, index_ref, c_ref, gate_ref, *blocks):
    tokens = x_ref.shape[0]
    each = blocks[0].shape[0] // slots
    experts = len(blocks) * each
    unit, _ = unit_rows(x_ref[...])
    c = (unit * gain_ref[...]).astype(BF16)
    c_ref[...] = c
    logits = dot(router_ref[...].astype(BF16), c, 1, 1)
    expert = lax.broadcasted_iota(jnp.int32, (experts, tokens), 0)
    picked = [
        jnp.sum(jnp.where(ids_ref[k : k + 1, :] == expert, logits, 0.0), axis=0, keepdims=True) for k in range(TOP)
    ]
    gates = [0.5 + 0.5 * jnp.tanh(0.5 * (picked[k] - picked[1 - k])) for k in range(TOP)]
    gate_ref[...] = jnp.concatenate(gates + [jnp.zeros((8 - TOP, tokens), F32)], axis=0)
    for k in range(experts):
        place = lax.broadcasted_iota(jnp.int32, (slots, tokens), 0) + (pos_ref[1] ^ k) * slots
        hits = [place == index_ref[k : k + 1, :] for k in range(TOP)]
        rows = dot(jnp.where(hits[0] | hits[1], 1.0, 0.0).astype(BF16), c)
        weight = sum(jnp.where(hits[k], gates[k], 0.0) for k in range(TOP))
        tile = write_spare(slots, jnp.sum(weight, axis=1, keepdims=True))
        at = k % each * slots
        blocks[k // each][at : at + slots] = jnp.concatenate([rows[: slots - 8], tile], axis=0).astype(BF16)


def experts_kernel(slots, n, each, pos_ref, w1_ref, w2_ref, *refs):
    g_refs, c_refs, refs = refs[: n * each], refs[n * each : n * each + n], refs[n * each + n :]
    dc_refs, z_refs = refs[:n], refs[n : 2 * n]
    f_ref, dh_ref, dy_ref, gate_ref, y_ref, dc_ref = refs[2 * n :]
    step = pl.program_id(0)
    blocks = [(b, slice(b * slots, (b + 1) * slots)) for b in range(n * each)]

    @pl.when(step == 0)
    def _():
        for b, here in blocks:
            end = (b % each + 1) * slots
            gate = read_spare(c_refs[b // each][end - 16 : end].astype(F32)[8:], slots)
            gate_ref[here] = jnp.broadcast_to(gate, (slots, 128))
            dy_ref[here] = (gate * g_refs[b][0].astype(F32)).astype(BF16)

    c = c_refs[0][...] if n == 1 else jnp.concatenate([ref[...] for ref in c_refs], axis=0)
    active, slope = gelu_parts(dot(c, w1_ref[...]))
    active = active.astype(BF16)
    f_ref[...] = active
    dh = (slope * dot(dy_ref[...], w2_ref[...], 1, 1)).astype(BF16)
    dh_ref[...] = dh
    y = dot(active, w2_ref[...])
    dc = dot(dh, w1_ref[...], 1, 1)

    @pl.when(step == 0)
    def _():
        y_ref[...] = y
        dc_ref[...] = dc

    @pl.when(step > 0)
    def _():
        y_ref[...] += y
        dc_ref[...] += dc

    @pl.when(step == pl.num_programs(0) - 1)
    def _():
        for b, here in blocks:
            there = slice(b % each * slots, (b % each + 1) * slots)
            rounded = y_ref[here].astype(BF16).astype(F32)
            dgate = jnp.sum(g_refs[b][0].astype(F32) * rounded, axis=1, keepdims=True)
            z_refs[b // each][there] = (gate_ref[here, 0:1] * rounded).astype(BF16)
            rows = jnp.concatenate([dc_ref[here][: slots - 8], write_spare(slots, dgate)], axis=0)
            dc_refs[b // each][there] = rows.astype(BF16)


def expert_grads_kernel(n, pos_ref, *refs):
    m = len(refs) - 2 - 3 * n
    c_refs = refs[:m]
    f_refs, dh_refs, dy_refs = refs[m : m + n], refs[m + n : m + 2 * n], refs[m + 2 * n : m + 3 * n]
    send_ref, keep_ref = refs[m + 3 * n :]
    per = m // n
    for target, half in ((send_ref, 1 - (pos_ref[0] & 1)), (keep_ref, pos_ref[0] & 1)):
        at = pl.ds(pl.multiple_of(half * 256, 256), 256)
        total1 = total2 = None
        for i in range(n):
            c = [ref[:, at] for ref in c_refs[i * per : (i + 1) * per]]
            c = c[0] if per == 1 else jnp.concatenate(c, axis=0)
            part1 = dot(c, dh_refs[i][...], 0, 0)
            part2 = dot(f_refs[i][...], dy_refs[i][:, at], 0, 0)
            total1 = part1 if total1 is None else total1 + part1
            total2 = part2 if total2 is None else total2 + part2
        target[0:256] = total1.astype(BF16)
        for block in range(total2.shape[0] // 256):
            rows = slice(block * 256, (block + 1) * 256)
            target[256:512, rows] = total2[rows].astype(BF16)


def cut_kernel(a_ref, b_ref, *outs):
    row = 0
    for out in outs:
        rows = slice(row, row + out.shape[0])
        out[...] = (a_ref[rows].astype(F32) + b_ref[rows].astype(F32)).astype(BF16)
        row += out.shape[0]


def glue_kernel(*refs):
    n, row = (len(refs) - 1) // 2, 0
    for a_ref, b_ref in zip(refs[:n], refs[n : 2 * n]):
        refs[-1][row : row + a_ref.shape[0]] = (a_ref[...].astype(F32) + b_ref[...].astype(F32)).astype(BF16)
        row += a_ref.shape[0]


def join_rows_kernel(pos_ref, own_ref, other_ref, out_ref):
    core = pos_ref[0] & 1
    for mine, ref in ((core, own_ref), (1 - core, other_ref)):
        out_ref[pl.ds(pl.multiple_of(mine * 256, 256), 256)] = ref[...].astype(F32)


def join_columns_kernel(pos_ref, own_ref, other_ref, out_ref):
    core = pos_ref[0] & 1
    for mine, ref in ((core, own_ref), (1 - core, other_ref)):
        at = pl.ds(pl.multiple_of(mine * 256, 256), 256)
        for block in range(FF // 256):
            rows = slice(block * 256, (block + 1) * 256)
            out_ref[rows, at] = ref[:, rows].astype(F32)


def arrange_kernel(pos_ref, *refs):
    for k, ref in enumerate(refs[:-1]):
        refs[-1][pos_ref[1] ^ k] = ref[...]


def one_hot_columns(index_ref, width):
    place = lax.broadcasted_iota(jnp.int32, (index_ref.shape[0], width), 1)
    hit = (place == index_ref[:, 0:1]) | (place == index_ref[:, 1:2])
    return jnp.where(hit, 1.0, 0.0).astype(BF16)


def combine_kernel(
    slots, pos_ref, x_ref, gain_ref, router_ref, ids_ref, index_ref, turned_ref, c_ref, gate_ref, cot_ref, *refs
):
    blocks, (dx_ref, dgain_ref, drouter_ref) = refs[:-3], refs[-3:]
    each = blocks[0].shape[0] // slots
    experts = len(blocks) * each
    tokens = x_ref.shape[0]
    dgates = [jnp.zeros((1, tokens), F32) for _ in range(TOP)]
    gc = None
    for k in range(experts):
        at = k % each * slots
        block = blocks[k // each][at : at + slots]
        start = (pos_ref[1] ^ k) * slots
        place = lax.broadcasted_iota(jnp.int32, (tokens, slots), 1) + start
        hit = (place == turned_ref[:, 0:1]) | (place == turned_ref[:, 1:2])
        part = dot(jnp.where(hit, 1.0, 0.0).astype(BF16), block)
        gc = part if gc is None else gc + part
        place = lax.broadcasted_iota(jnp.int32, (slots, tokens), 0) + start
        column = read_spare(block[slots - 16 :].astype(F32)[8:], slots)
        for j in range(TOP):
            hit = place == index_ref[j : j + 1, :]
            dgates[j] = dgates[j] + jnp.sum(jnp.where(hit, column, 0.0), axis=0, keepdims=True)
    dl = gate_ref[0:1] * gate_ref[1:2] * (dgates[0] - dgates[1])
    expert = lax.broadcasted_iota(jnp.int32, (experts, tokens), 0)
    dlogits = jnp.where(ids_ref[0:1, :] == expert, dl, 0.0) - jnp.where(ids_ref[1:2, :] == expert, dl, 0.0)
    dlogits = dlogits.astype(BF16)
    gc = gc + dot(dlogits, router_ref[...].astype(BF16), 0, 0)
    drouter_ref[...] = dot(dlogits, c_ref[...])
    unit, scale = unit_rows(x_ref[...])
    dx, dgain = norm_backward(unit, scale, gain_ref[...], gc)
    dx_ref[...] = cot_ref[...].astype(F32) + dx
    dgain_ref[...] = dgain


def split_cube_kernel(n, pos_ref, *refs):
    kept, came, out_ref = refs[0:n], refs[n : 2 * n], refs[2 * n]
    for place in range(2):
        for half in range(2):
            x = (pos_ref[1] & 1) ^ (1 - half)
            y = (pos_ref[0] >> 1) ^ (1 - place)
            row = 0
            for keep, new in zip(kept, came):
                total = (keep[place, half].astype(F32) + new[place, half].astype(F32)).astype(BF16)
                for start in range(0, keep.shape[2], 64):
                    for depth in range(2):
                        at = start + depth * STRIP
                        out_ref[depth * 4 + x * 2 + y, row : row + STRIP] = total[at : at + STRIP]
                    row += STRIP


def sum_cube_kernel(a_ref, out_ref):
    total = a_ref[0].astype(F32)
    for k in range(1, a_ref.shape[0]):
        total = total + a_ref[k].astype(F32)
    out_ref[...] = total.astype(BF16)


def sum_kernel(*refs):
    total = refs[0][...].astype(F32)
    for ref in refs[1:-1]:
        total = total + ref[...].astype(F32)
    refs[-1][...] = total.astype(BF16)


def rows_of(pos_ref, k):
    source = pos_ref[1] ^ k
    return pl.ds(pl.multiple_of((source & 1) * 64 + (source >> 1 & 1) * STRIP, STRIP), STRIP)


def finish_mlp_kernel(pos_ref, *refs):
    mlp1_ref, mlp2_ref = refs[4:]
    for k in range(4):
        there = rows_of(pos_ref, k)
        mlp1_ref[there] = refs[k][STRIP : 2 * STRIP].astype(F32)
        for part in range(4):
            mlp2_ref[part, there] = refs[k][2 * STRIP :, part * 512 : (part + 1) * 512].astype(F32)


def finish_attention_kernel(pos_ref, *refs):
    in_ref, out_ref, small_ref = refs[8:]
    for k in range(4):
        there = rows_of(pos_ref, k)
        for layer, ref in ((0, refs[k]), (1, refs[4 + k])):
            in_ref[layer, there] = ref[0:STRIP, 0 : 3 * D].astype(F32)
            out_ref[layer, there] = ref[0:STRIP, 3 * D : 4 * D].astype(F32)
    for group in range(small_ref.shape[0] // STRIP):
        at = 4 * D + group * 128
        small_ref[group * STRIP : (group + 1) * STRIP] = refs[0][:, at : at + 128].astype(F32)


def final_kernel(blocks_ref, x_ref, turned_ref, out_ref):
    out_ref[...] = (x_ref[...] + dot(one_hot_columns(turned_ref, blocks_ref.shape[0]), blocks_ref[...])).astype(BF16)


def spent(us):
    return pl.CostEstimate(flops=int(us * 1.0e9), bytes_accessed=0, transcendentals=0)


def call(kernel, outs, *args, us=1.0, scratch=(), specs=None, room=40, **more):
    return list(
        pl.pallas_call(
        kernel,
        out_shape=[(pltpu.HBM if rest else jax.ShapeDtypeStruct)(shape, kind) for shape, kind, *rest in outs],
        in_specs=specs if specs is not None else [WHOLE] * len(args),
        out_specs=[WHOLE] * len(outs),
        scratch_shapes=list(scratch),
        cost_estimate=spent(us),
        compiler_params=pltpu.CompilerParams(vmem_limit_bytes=room * 1024 * 1024),
        **more,
        )(*args)
    )


WHOLE = pl.BlockSpec(memory_space=pltpu.VMEM)
SCALAR = pl.BlockSpec(memory_space=pltpu.SMEM)
AWAY = pl.BlockSpec(memory_space=pltpu.HBM)


def flip(array, axis, bit):
    return lax.ppermute(array, axis, [(i, i ^ bit) for i in range(lax.axis_size(axis))])


def gather_pieces(piece, across=None):
    across = flip(piece, "wshard", 2) if across is None else across
    return (piece, flip(piece, "wshard", 1), across, flip(across, "wshard", 1))


def after(array, *others):
    return lax.optimization_barrier((array, *others))[0]


def split_cube(pos, bundle):
    came = [flip(send, "wshard", 1) for send, _ in bundle]
    tall = sum(keep.shape[2] for _, keep in bundle)
    wide = bundle[0][0].shape[-1]
    return call(
        functools.partial(split_cube_kernel, len(bundle)),
        [((8, tall // 2, wide), BF16, AWAY)],
        pos,
        *[keep for _, keep in bundle],
        *came,
        specs=[SCALAR] + [WHOLE] * (2 * len(bundle)),
        us=3.0,
    )[0]


def trade_cube(blocks):
    inner = lax.axis_size("wshard")
    groups = [
        [((2 * z + depth) * 2 + x) * inner + y * 2 + core for depth in range(2) for x in range(2) for y in range(2)]
        for z in range(lax.axis_size("expert") // 4)
        for core in range(2)
    ]
    return lax.all_to_all(blocks, ("expert", "wshard"), 0, 0, axis_index_groups=groups, tiled=True)


def sum_cube(blocks):
    return call(sum_cube_kernel, [(blocks.shape[1:], BF16, AWAY)], blocks, us=2.0)[0]


def sum_two(strip, other):
    return call(sum_kernel, [(strip.shape, BF16, AWAY)], strip, other)[0]


def spread(strip):
    return [strip] + [flip(strip, "expert", k) for k in range(1, 4)]


def sum_plainly(send, keep):
    half = (keep.astype(F32) + flip(send, "wshard", 1).astype(F32)).astype(BF16)
    rows = half[1].astype(F32) + flip(half[0], "wshard", 2).astype(F32)
    return lax.psum(jnp.concatenate([rows[1], rows[0]], axis=0), "expert")


def expand(rows, images):
    return jnp.pad(rows.reshape(images, SEQ, -1), ((0, 0), (0, PAD - SEQ), (0, 0))).reshape(images * PAD, -1)


def contract(rows, images):
    return rows.reshape(images, PAD, -1)[:, :SEQ].reshape(images * SEQ, -1)


def local(
    images, attn_in, attn_out, norm_gains, mlp_in, mlp_out, router, expert_in, expert_out, expert_ids, cotangent
):
    owners = lax.axis_size("expert")
    experts = owners * expert_in.shape[0]
    tokens = images.shape[0]
    pictures = tokens // SEQ
    rows = pictures * PAD
    capacity = max(2, 2 * TOP * tokens // experts)
    slots = (capacity + 8 + 15) // 16 * 16
    every = experts * slots
    linked = owners == LINKED
    own = lax.axis_index("expert") if linked else 0
    pos = jnp.stack([lax.axis_index("wshard"), own]).astype(jnp.int32)

    small = jnp.concatenate([norm_gains, router.T], axis=0)
    small = jnp.pad(small, ((0, -small.shape[0] % 16), (0, 0)))
    (small_full,) = call(
        small_kernel, [((small.shape[0], D), F32)], pos, *gather_pieces(small), specs=[SCALAR] + [WHOLE] * 4
    )
    gains = [small_full[i : i + 1] for i in range(4)]
    router_full = small_full[4 : 4 + experts]

    wi0 = flip(attn_in[0], "wshard", 2)
    wo0 = flip(attn_out[0], "wshard", 2)
    w1_across = flip(after(mlp_in, wi0), "wshard", 2)
    w2_across = flip(after(mlp_out, wi0), "wshard", 2)
    wi1 = flip(after(attn_in[1], w1_across), "wshard", 2)
    wo1 = flip(after(attn_out[1], w1_across), "wshard", 2)
    wi = [gather_pieces(attn_in[0], wi0), None]
    wo = [gather_pieces(attn_out[0], wo0), None]
    x0 = expand(images, pictures)

    weight_specs = [AWAY] * 8
    attn_scratch = [pltpu.VMEM((4, D // 4, 3 * D), BF16), pltpu.VMEM((4, D // 4, D), BF16)]
    mlp_scratch = [pltpu.VMEM((4, D // 4, FF), BF16), pltpu.VMEM((4, FF // 4, D), BF16)]
    sems = pltpu.SemaphoreType.DMA((8,))

    def attend(x, layer):
        return call(
            attend_forward_kernel,
            [((rows, D), F32), ((rows, 3 * D), BF16), ((rows, D), BF16)],
            pos, x, gains[2 * layer], *wi[layer], *wo[layer],
            specs=[SCALAR, WHOLE, WHOLE] + weight_specs,
            scratch=attn_scratch + [sems],
            us=7.0,
        )

    def attend_back(x, layer, packed, o, dz, extra):
        wide = 4 * D
        if extra:
            wide += (sum(a.shape[0] for a in extra) + 1 + STRIP - 1) // STRIP * 128
        return call(
            functools.partial(attend_backward_kernel, len(extra)),
            [((rows, D), F32), ((1, D), F32), ((2, 2, 64, wide), BF16, AWAY), ((2, 2, 64, wide), BF16, AWAY)],
            pos, x, gains[2 * layer], packed, o, dz, *wi[layer], *wo[layer], *extra,
            specs=[SCALAR] + [WHOLE] * 5 + weight_specs + [WHOLE] * len(extra),
            scratch=attn_scratch
            + [pltpu.VMEM((rows, 3 * D), BF16)]
            + [pltpu.VMEM((rows, D), BF16)] * 3
            + [sems],
            us=12.5,
            room=58,
        )

    x1, packed1, o1 = attend(x0, 0)
    ids = jnp.pad(after(expert_ids, x1).T.reshape(TOP, pictures, SEQ), ((0, 8 - TOP), (0, 0), (0, PAD - SEQ)), constant_values=-1)
    ids = ids.reshape(8, rows)
    cot = expand(after(cotangent, x1), pictures)

    index, g_out = call(
        functools.partial(routing_kernel, slots), [((8, rows), jnp.int32), ((every, D), BF16)], ids, cot, us=3.4
    )
    turned = index.T
    trade = functools.partial(lax.all_to_all, axis_name="expert", split_axis=0, concat_axis=0, tiled=True)
    g_in = trade(g_out.reshape(experts, slots, D))

    w1 = gather_pieces(mlp_in, after(w1_across, x1))
    w2 = gather_pieces(mlp_out, after(w2_across, x1))
    (x2,) = call(
        feed_forward_kernel, [((rows, D), F32)], pos, x1, gains[1], *w1, *w2,
        specs=[SCALAR, WHOLE, WHOLE] + weight_specs, scratch=mlp_scratch + [sems], us=6.5,
    )
    wi[1] = gather_pieces(attn_in[1], after(wi1, x2))
    wo[1] = gather_pieces(attn_out[1], after(wo1, x2))
    x3, packed2, o2 = attend(x2, 1)
    arrays = experts if linked else max(1, experts // (2 * PAD // slots))
    each = experts // arrays
    c, gate, *c_out = call(
        functools.partial(dispatch_kernel, slots),
        [((rows, D), BF16), ((8, rows), F32)] + [((each * slots, D), BF16, AWAY)] * arrays,
        pos, x3, gains[3], router_full, ids, index,
        specs=[SCALAR] + [WHOLE] * 5,
        us=4.6,
    )

    def swap(blocks, first=0):
        if linked:
            return [flip(block, "expert", k) if k else block for k, block in enumerate(blocks, first)]
        moved = trade(jnp.concatenate(blocks).reshape(experts, slots, D))
        return list(moved.reshape(arrays, each * slots, D))

    c_in = swap(c_out)
    per = 2 if linked else 1
    work = []
    dc_out, z_out, dc_in = [], [], []
    for first in range(0, arrays, per):
        given = c_in[first : first + per]
        if linked and first >= 2 * per:
            given[0], *dc_in[-2 * per : -per] = lax.optimization_barrier((given[0], *dc_in[-2 * per : -per]))
        count = list(range(first * each, (first + per) * each))
        tall = len(count) * slots
        fixed = lambda *shape: pl.BlockSpec(shape, lambda j, pos_ref: (0,) * len(shape))
        source = lambda k: pl.BlockSpec((1, slots, D), lambda j, pos_ref: (pos_ref[1] ^ k, 0, 0))
        across = lambda height: pl.BlockSpec((height, 1024), lambda j, pos_ref: (0, j))
        *made, f, dh, dy = pl.pallas_call(
            functools.partial(experts_kernel, slots, per, each),
            out_shape=[pltpu.HBM((each * slots, D), BF16)] * (2 * per)
            + [pltpu.HBM((tall, FF), BF16)] * 2
            + [pltpu.HBM((tall, D), BF16)],
            grid_spec=pltpu.PrefetchScalarGridSpec(
                num_scalar_prefetch=1,
                grid=(FF // 1024,),
                in_specs=[across(D), pl.BlockSpec((1024, D), lambda j, pos_ref: (j, 0))]
                + [source(k) for k in count]
                + [fixed(each * slots, D)] * per,
                out_specs=[fixed(each * slots, D)] * (2 * per) + [across(tall)] * 2 + [fixed(tall, D)],
                scratch_shapes=[pltpu.VMEM((tall, 128), F32), pltpu.VMEM((tall, D), F32), pltpu.VMEM((tall, D), F32)],
            ),
            cost_estimate=spent(8.0),
            compiler_params=pltpu.CompilerParams(vmem_limit_bytes=VMEM_LIMIT if first else 58 * 1024 * 1024),
        )(pos, expert_in[0], expert_out[0], *[g_in] * len(count), *given)
        dc_out += made[:per]
        z_out += made[per:]
        if linked:
            dc_in += swap(made[:per], first)
        work.append((f, dh, dy))
    if not linked:
        dc_in = swap(dc_out)
    if linked:
        (z_block,) = call(
            arrange_kernel, [((experts, slots, D), BF16, AWAY)], pos, *z_out, specs=[SCALAR] + [WHOLE] * experts, us=2.0
        )
    else:
        z_block = jnp.concatenate(z_out).reshape(experts, slots, D)
    n = len(work)
    whole_rows = lambda a: pl.BlockSpec(a.shape, lambda j: (0, 0))
    chunk = lambda a: pl.BlockSpec((a.shape[0], 1024), lambda j: (0, j))
    fs, dhs, dys = ([w[i] for w in work] for i in range(3))
    if linked:
        dys[0], *dc_in[per : 2 * per] = lax.optimization_barrier((dys[0], *dc_in[per : 2 * per]))
    grad_send, grad_keep = pl.pallas_call(
        functools.partial(expert_grads_kernel, n),
        grid=(FF // 1024,),
        in_specs=[SCALAR]
        + [whole_rows(a) for a in c_in]
        + [chunk(a) for a in fs + dhs]
        + [whole_rows(a) for a in dys],
        out_specs=[pl.BlockSpec((512, 1024), lambda j: (0, j))] * 2,
        out_shape=[pltpu.HBM((512, FF), BF16)] * 2,
        cost_estimate=spent(10.0),
        compiler_params=pltpu.CompilerParams(vmem_limit_bytes=VMEM_LIMIT),
    )(pos, *c_in, *fs, *dhs, *dys)
    x3_late, z_block, grad_send, grad_keep = lax.optimization_barrier((x3, z_block, grad_send, grad_keep))
    g3, gain3, drouter = call(
        functools.partial(combine_kernel, slots),
        [((rows, D), F32), ((1, D), F32), ((experts, D), F32)],
        pos, x3_late, gains[3], router_full, ids, index, turned, c, gate, cot, *dc_in,
        specs=[SCALAR] + [WHOLE] * (9 + arrays),
        us=5.5,
    )
    g3, z_block, grad_send = lax.optimization_barrier((g3, z_block, grad_send))
    z_in = trade(z_block)
    grads = call(
        cut_kernel,
        [((tall, FF), BF16, AWAY) for tall in (128, 128, 256)],
        grad_keep, flip(grad_send, "wshard", 1),
        us=2.0,
    )
    g3 = after(g3, *grads)
    crossed = [flip(piece, "wshard", 2) for piece in grads[:2]]
    g2, gain2, *second = attend_back(x2, 1, packed2, o2, g3, [])
    g1, gain1, *mlp = call(
        feed_backward_kernel,
        [((rows, D), F32), ((1, D), F32)] + [((2, 2, 128, FF), BF16, AWAY)] * 2,
        pos, x1, gains[1], g2, *w1, *w2,
        specs=[SCALAR, WHOLE, WHOLE, WHOLE] + weight_specs,
        scratch=mlp_scratch + [pltpu.VMEM((D, FF), BF16), pltpu.VMEM((FF, D), BF16), sems],
        us=12.5,
        room=58,
    )
    *second, mlp[0], mlp[1], crossed[0], crossed[1] = lax.optimization_barrier(
        (*second, mlp[0], mlp[1], crossed[0], crossed[1])
    )
    if linked:
        bulk = split_cube(pos, [second, mlp])
        g1 = after(g1, z_in, bulk)
        bulk = trade_cube(bulk)
    dx, _, *first = attend_back(x0, 0, packed1, o1, g1, [gain1, gain2, gain3, drouter])
    (final,) = call(final_kernel, [((rows, D), BF16)], z_in.reshape(every, D), x3, turned, us=3.5)

    wide = first[0].shape[-1]

    def join(kernel, shape, pieces, came):
        (half,) = call(glue_kernel, [((256, FF), BF16, AWAY)], *pieces, *came)
        return call(
            kernel, [(shape, F32)], pos, half, flip(half, "wshard", 1), specs=[SCALAR] + [WHOLE] * 2, us=2.0
        )[0]

    expert1 = join(join_rows_kernel, (D, FF), [after(grads[0], dx), grads[1]], crossed)
    if linked:
        tail = split_cube(pos, [(first[0], after(first[1], final))])
        final_rows, input_grad = contract(final, pictures), contract(dx, pictures)
        bulk = sum_cube(after(bulk, tail, final_rows, input_grad))
        deep = flip(bulk, "expert", 4)
        tail = sum_cube(after(trade_cube(after(tail, bulk)), deep, expert1))
        last = flip(after(grads[2], tail), "wshard", 2)
        bulk = spread(sum_two(bulk, deep))
        tail = sum_two(tail, flip(tail, "expert", 4))
        last = after(last, tail, *bulk)
        tail = spread(tail)
        mlp1, mlp2 = call(
            finish_mlp_kernel,
            [((D // 4, FF), F32), ((4, 128, D), F32)],
            pos, *bulk, specs=[SCALAR] + [WHOLE] * 4, us=2.0,
        )
        grad_in, grad_out, smalls = call(
            finish_attention_kernel,
            [((2, D // 4, 3 * D), F32), ((2, D // 4, D), F32), (((wide - 4 * D) // 128 * STRIP, 128), F32)],
            pos, *tail, *bulk, specs=[SCALAR] + [WHOLE] * 8, us=2.0,
        )
        mlp2 = mlp2.reshape(FF // 4, D)
    else:
        last = flip(grads[2], "wshard", 2)
        first, second, mlp = sum_plainly(*first), sum_plainly(*second), sum_plainly(*mlp)
        grad_in = jnp.stack([first[:, : 3 * D], second[:, : 3 * D]])
        grad_out = jnp.stack([first[:, 3 * D : 4 * D], second[:, 3 * D :]])
        smalls = first[:STRIP, 4 * D :].reshape(STRIP, -1, 128).transpose(1, 0, 2).reshape(-1, 128)
        mlp1 = jnp.concatenate([mlp[0:64], mlp[128:192]], axis=0)
        final_rows, input_grad = contract(final, pictures), contract(dx, pictures)
        mlp2 = jnp.stack([mlp[64:128], mlp[192:256]]).reshape(2, 64, 4, D).transpose(2, 0, 1, 3).reshape(FF // 4, D)

    expert2 = join(join_columns_kernel, (FF, D), grads[2:], [last])
    return (
        final_rows,
        input_grad,
        grad_in,
        grad_out,
        smalls[0:4],
        mlp1,
        mlp2,
        smalls[4 : 4 + experts].T,
        expert1[None],
        expert2[None],
    )


def solution(mesh):
    rows = P(("expert", "wshard"), None)
    dense = (P(None, "wshard", None), P(None, "wshard", None), P(None, "wshard"))
    shards = (P("wshard", None),) * 3
    experts = (P("expert", None, None),) * 2
    return jax.shard_map(
        local,
        mesh=mesh,
        in_specs=(rows, *dense, *shards, *experts, rows, rows),
        out_specs=(rows, rows, *dense, *shards, *experts),
        check_vma=False,
    )
```

```python
import functools

import jax
import jax.numpy as jnp
from jax import lax
from jax.experimental import pallas as pl
from jax.experimental.pallas import tpu as pltpu
from jax.sharding import PartitionSpec as P

D = 512
HEADS = 8
FF = 2048
SEQ = 197
TOP = 2
HEAD_DIM = 64
PAD = 208
STRIP = 32
CHUNK = 512
EPSILON = 1e-06
ROOT_2_PI = 0.7978845608028654
CUBIC = 0.044715

F32 = jnp.float32
BF16 = jnp.bfloat16
VMEM_LIMIT = 40 * 1024 * 1024
LINKED = 8


def dot(a, b, ca=1, cb=0):
    return lax.dot_general(a, b, (((ca,), (cb,)), ((), ())), preferred_element_type=F32)


def unit_rows(rows):
    centred = rows - jnp.mean(rows, axis=-1, keepdims=True)
    scale = lax.rsqrt(jnp.mean(centred * centred, axis=-1, keepdims=True) + EPSILON)
    return centred * scale, scale


def norm_backward(unit, scale, gain, grad):
    scaled = gain * grad
    inner = (
        scaled
        - jnp.mean(scaled, axis=-1, keepdims=True)
        - unit * jnp.mean(scaled * unit, axis=-1, keepdims=True)
    )
    return inner * scale, jnp.sum(grad * unit, axis=0, keepdims=True)


def gelu_parts(h):
    square = h * h
    t = jnp.tanh(ROOT_2_PI * h * (1.0 + CUBIC * square))
    half = 0.5 * (1.0 + t)
    slope = half + 0.5 * h * (1.0 - t * t) * (ROOT_2_PI * (1.0 + 3.0 * CUBIC * square))
    return h * half, slope


def gelu(h):
    return 0.5 * h * (1.0 + jnp.tanh(ROOT_2_PI * h * (1.0 + CUBIC * h * h)))


def start_weight(pos_ref, pieces, held, sems, first):
    copies = []
    for j, piece in enumerate(pieces):
        copy = pltpu.make_async_copy(piece, held.at[pos_ref[0] ^ j], sems.at[first + j])
        copy.start()
        copies.append(copy)
    return copies


def wait_all(copies):
    for copy in copies:
        copy.wait()


def softmax_rows(q, k):
    scores = dot(q, k, 1, 1) * (HEAD_DIM**-0.5)
    column = lax.broadcasted_iota(jnp.int32, scores.shape, 1)
    scores = jnp.where(column < SEQ, scores, -1e30)
    raised = jnp.exp(scores - jnp.max(scores, axis=-1, keepdims=True))
    return raised * (1.0 / jnp.sum(raised, axis=-1, keepdims=True))


def shards_of(pos_ref, send_ref, keep_ref):
    for target, turn in ((send_ref, 1), (keep_ref, 0)):
        for place in range(2):
            yield target, place, pos_ref[0] ^ (turn + 2 * (1 - place))


def own_half(pos_ref, half):
    return 1 - ((pos_ref[1] & 1) ^ half)


def attend_forward_kernel(pos_ref, x_ref, gain_ref, *refs):
    wi, wo = refs[0:4], refs[4:8]
    y_ref, packed_ref, o_ref, wi_held, wo_held, sems = refs[8:]
    wi_copies = start_weight(pos_ref, wi, wi_held, sems, 0)
    wo_copies = start_weight(pos_ref, wo, wo_held, sems, 4)
    rows = x_ref[...].astype(F32)
    unit, _ = unit_rows(rows)
    normed = (unit * gain_ref[...]).astype(BF16)
    wait_all(wi_copies)
    packed_ref[...] = dot(normed, wi_held[...].reshape(D, 3 * D)).astype(BF16)
    lane = lax.broadcasted_iota(jnp.int32, (PAD, 2 * HEAD_DIM), 1)
    for image in range(x_ref.shape[0] // PAD):
        here = pl.ds(image * PAD, PAD)
        for pair in range(HEADS // 2):
            at = pair * 2 * HEAD_DIM
            q = packed_ref[here, at : at + 128]
            k = packed_ref[here, D + at : D + at + 128]
            v = packed_ref[here, 2 * D + at : 2 * D + at + 128]
            total = None
            for side in range(2):
                mine = (lane >= HEAD_DIM) == bool(side)
                chances = softmax_rows(jnp.where(mine, q, jnp.zeros_like(q)), k).astype(BF16)
                part = dot(chances, jnp.where(mine, v, jnp.zeros_like(v)))
                total = part if total is None else total + part
            o_ref[here, at : at + 128] = total.astype(BF16)
    wait_all(wo_copies)
    y_ref[...] = x_ref[...].astype(F32) + dot(o_ref[...], wo_held[...].reshape(D, D))


def attend_backward_kernel(smalls, pos_ref, x_ref, gain_ref, packed_ref, o_ref, dz_ref, *refs):
    wi, wo = refs[0:4], refs[4:8]
    extra = refs[8 : 8 + smalls]
    dx_ref, dgain_ref, send_ref, keep_ref, wi_held, wo_held, dp_ref, dout_ref, do_ref, normed_ref, sems = refs[
        8 + smalls :
    ]
    wo_copies = start_weight(pos_ref, wo, wo_held, sems, 4)
    wi_copies = start_weight(pos_ref, wi, wi_held, sems, 0)
    unit, scale = unit_rows(x_ref[...].astype(F32))
    gain = gain_ref[...]
    normed_ref[...] = (unit * gain).astype(BF16)
    dout_ref[...] = dz_ref[...].astype(BF16)
    wait_all(wo_copies)
    do_ref[...] = dot(dout_ref[...], wo_held[...].reshape(D, D), 1, 1).astype(BF16)
    lane = lax.broadcasted_iota(jnp.int32, (PAD, 2 * HEAD_DIM), 1)
    factor = HEAD_DIM**-0.5
    for image in range(x_ref.shape[0] // PAD):
        here = pl.ds(image * PAD, PAD)
        for pair in range(HEADS // 2):
            at = pair * 2 * HEAD_DIM
            q = packed_ref[here, at : at + 128]
            k = packed_ref[here, D + at : D + at + 128]
            v = packed_ref[here, 2 * D + at : 2 * D + at + 128]
            do = do_ref[here, at : at + 128]
            dq = dk = dv = None
            for side in range(2):
                mine = (lane >= HEAD_DIM) == bool(side)
                own = lambda a: jnp.where(mine, a, jnp.zeros_like(a))
                q_own, k_own, do_own = own(q), own(k), own(do)
                chances = softmax_rows(q_own, k)
                dv_part = dot(chances.astype(BF16), do_own, 0, 0)
                da = dot(do_own, v, 1, 1)
                ds = chances * (da - jnp.sum(da * chances, axis=-1, keepdims=True))
                ds = ds.astype(BF16)
                dq_part = dot(ds, k_own)
                dk_part = dot(ds, q_own, 0, 0)
                dq = dq_part if dq is None else dq + dq_part
                dk = dk_part if dk is None else dk + dk_part
                dv = dv_part if dv is None else dv + dv_part
            dp_ref[here, at : at + 128] = (dq * factor).astype(BF16)
            dp_ref[here, D + at : D + at + 128] = (dk * factor).astype(BF16)
            dp_ref[here, 2 * D + at : 2 * D + at + 128] = dv.astype(BF16)
    wait_all(wi_copies)
    dn = dot(dp_ref[...], wi_held[...].reshape(D, 3 * D), 1, 1)
    unit, scale = unit_rows(x_ref[...].astype(F32))
    dx, dgain = norm_backward(unit, scale, gain, dn)
    dx_ref[...] = dz_ref[...] + dx
    dgain_ref[...] = dgain
    for target, place, shard in shards_of(pos_ref, send_ref, keep_ref):
        columns = pl.ds(pl.multiple_of(shard * 128, 128), 128)
        grad_in = dot(normed_ref[:, columns], dp_ref[...], 0, 0).astype(BF16)
        grad_out = dot(o_ref[:, columns], dout_ref[...], 0, 0).astype(BF16)
        for half in range(2):
            there = own_half(pos_ref, half)
            target[place, there, :, 0 : 3 * D] = grad_in[half * 64 : half * 64 + 64]
            target[place, there, :, 3 * D : 4 * D] = grad_out[half * 64 : half * 64 + 64]
    if smalls:
        small = jnp.concatenate([dgain] + [ref[...] for ref in extra], axis=0)
        small = jnp.concatenate([small, jnp.zeros((-small.shape[0] % STRIP, D), F32)], axis=0)
        for target, place, shard in shards_of(pos_ref, send_ref, keep_ref):
            piece = jnp.zeros((small.shape[0], 128), F32)
            for s in range(4):
                piece = jnp.where(shard == s, small[:, s * 128 : (s + 1) * 128], piece)
            piece = piece.astype(BF16)
            for half in range(2):
                for strip in range(64 // STRIP):
                    for group in range(small.shape[0] // STRIP):
                        at = 4 * D + group * 128
                        target[place, half, strip * STRIP : (strip + 1) * STRIP, at : at + 128] = piece[
                            group * STRIP : (group + 1) * STRIP
                        ]


def feed_forward_kernel(pos_ref, x_ref, gain_ref, *refs):
    w1, w2 = refs[0:4], refs[4:8]
    y_ref, w1_held, w2_held, sems = refs[8:]
    w1_copies = start_weight(pos_ref, w1, w1_held, sems, 0)
    w2_copies = start_weight(pos_ref, w2, w2_held, sems, 4)
    unit, _ = unit_rows(x_ref[...])
    normed = (unit * gain_ref[...]).astype(BF16)
    wait_all(w1_copies)
    total = x_ref[...]
    for j in range(FF // 1024):
        at = slice(j * 1024, (j + 1) * 1024)
        active = gelu(dot(normed, w1_held[:, :, at].reshape(D, 1024))).astype(BF16)
        if j == 0:
            wait_all(w2_copies)
        total = total + dot(active, w2_held[...].reshape(FF, D)[at])
    y_ref[...] = total


def feed_backward_kernel(pos_ref, x_ref, gain_ref, dz_ref, *refs):
    w1, w2 = refs[0:4], refs[4:8]
    dx_ref, dgain_ref, send_ref, keep_ref, w1_held, w2_held, g1_ref, g2_ref, sems = refs[8:]
    w1_copies = start_weight(pos_ref, w1, w1_held, sems, 0)
    w2_copies = start_weight(pos_ref, w2, w2_held, sems, 4)
    unit, scale = unit_rows(x_ref[...])
    gain = gain_ref[...]
    normed = (unit * gain).astype(BF16)
    dout = dz_ref[...].astype(BF16)
    wait_all(w1_copies)
    wait_all(w2_copies)
    dn = None
    for j in range(FF // 1024):
        at = slice(j * 1024, (j + 1) * 1024)
        w1_now = w1_held[:, :, at].reshape(D, 1024)
        w2_now = w2_held[...].reshape(FF, D)[at]
        active, slope = gelu_parts(dot(normed, w1_now))
        dh = (slope * dot(dout, w2_now, 1, 1)).astype(BF16)
        g2_ref[at] = dot(active.astype(BF16), dout, 0, 0).astype(BF16)
        g1_ref[:, at] = dot(normed, dh, 0, 0).astype(BF16)
        part = dot(dh, w1_now, 1, 1)
        dn = part if dn is None else dn + part
    dx, dgain = norm_backward(unit, scale, gain, dn)
    dx_ref[...] = dz_ref[...] + dx
    dgain_ref[...] = dgain
    for target, place, shard in shards_of(pos_ref, send_ref, keep_ref):
        for half in range(2):
            there = own_half(pos_ref, half)
            target[place, there, 0:64] = g1_ref[pl.ds(pl.multiple_of(shard * 128 + half * 64, 64), 64)]
            for part in range(4):
                start = pl.multiple_of(shard * 512 + part * 128 + half * 64, 64)
                target[place, there, 64:128, part * 512 : (part + 1) * 512] = g2_ref[pl.ds(start, 64)]


def routing_kernel(slots, ids_ref, cot_ref, index_ref, blocks_ref):
    experts = blocks_ref.shape[0] // slots
    tokens = ids_ref.shape[1]
    expert = lax.broadcasted_iota(jnp.int32, (experts, tokens), 0)
    named = [ids_ref[k : k + 1, :] == expert for k in range(TOP)]
    matches = jnp.where(named[0] | named[1], 1.0, 0.0).astype(BF16)
    earlier = lax.broadcasted_iota(jnp.int32, (tokens, tokens), 0) < lax.broadcasted_iota(
        jnp.int32, (tokens, tokens), 1
    )
    rank = dot(matches, jnp.where(earlier, 1.0, 0.0).astype(BF16))
    index_ref[...] = jnp.full(index_ref.shape, -1, jnp.int32)
    place = lax.broadcasted_iota(jnp.int32, (blocks_ref.shape[0], tokens), 0)
    chosen = None
    for k in range(TOP):
        slot = jnp.sum(jnp.where(named[k], rank, 0.0), axis=0, keepdims=True).astype(jnp.int32)
        index = ids_ref[k : k + 1, :] * slots + slot
        index_ref[k : k + 1, :] = index
        hit = place == index
        chosen = hit if chosen is None else chosen | hit
    blocks_ref[...] = dot(jnp.where(chosen, 1.0, 0.0).astype(BF16), cot_ref[...]).astype(BF16)


def write_spare(slots, column):
    eye = lax.broadcasted_iota(jnp.int32, (slots, D), 0) == lax.broadcasted_iota(jnp.int32, (slots, D), 1)
    line = jnp.sum(jnp.where(eye, column, 0.0), axis=0, keepdims=True)
    high = line.astype(BF16).astype(F32)
    middle = (line - high).astype(BF16).astype(F32)
    low = line - high - middle
    row = lax.broadcasted_iota(jnp.int32, (8, D), 0)
    return jnp.where(row == 0, high, jnp.where(row == 1, middle, jnp.where(row == 2, low, 0.0)))


def read_spare(tile, slots):
    line = tile[0:1] + tile[1:2] + tile[2:3]
    eye = lax.broadcasted_iota(jnp.int32, (slots, D), 0) == lax.broadcasted_iota(jnp.int32, (slots, D), 1)
    return jnp.sum(jnp.where(eye, line, 0.0), axis=1, keepdims=True)


def small_kernel(pos_ref, *refs):
    out_ref = refs[4]
    for j in range(4):
        start = pl.multiple_of((pos_ref[0] ^ j) * 128, 128)
        out_ref[:, pl.ds(start, 128)] = refs[j][...].astype(F32)


def dispatch_kernel(slots, pos_ref, x_ref, gain_ref, router_ref, ids_ref, index_ref, c_ref, gate_ref, *blocks):
    tokens = x_ref.shape[0]
    each = blocks[0].shape[0] // slots
    experts = len(blocks) * each
    unit, _ = unit_rows(x_ref[...])
    c = (unit * gain_ref[...]).astype(BF16)
    c_ref[...] = c
    logits = dot(router_ref[...].astype(BF16), c, 1, 1)
    expert = lax.broadcasted_iota(jnp.int32, (experts, tokens), 0)
    picked = [
        jnp.sum(jnp.where(ids_ref[k : k + 1, :] == expert, logits, 0.0), axis=0, keepdims=True) for k in range(TOP)
    ]
    gates = [0.5 + 0.5 * jnp.tanh(0.5 * (picked[k] - picked[1 - k])) for k in range(TOP)]
    gate_ref[...] = jnp.concatenate(gates + [jnp.zeros((8 - TOP, tokens), F32)], axis=0)
    for k in range(experts):
        place = lax.broadcasted_iota(jnp.int32, (slots, tokens), 0) + (pos_ref[1] ^ k) * slots
        hits = [place == index_ref[k : k + 1, :] for k in range(TOP)]
        rows = dot(jnp.where(hits[0] | hits[1], 1.0, 0.0).astype(BF16), c)
        weight = sum(jnp.where(hits[k], gates[k], 0.0) for k in range(TOP))
        tile = write_spare(slots, jnp.sum(weight, axis=1, keepdims=True))
        at = k % each * slots
        blocks[k // each][at : at + slots] = jnp.concatenate([rows[: slots - 8], tile], axis=0).astype(BF16)


def experts_kernel(slots, n, each, pos_ref, w1_ref, w2_ref, *refs):
    g_refs, c_refs, refs = refs[: n * each], refs[n * each : n * each + n], refs[n * each + n :]
    dc_refs, z_refs = refs[:n], refs[n : 2 * n]
    f_ref, dh_ref, dy_ref, gate_ref, y_ref, dc_ref = refs[2 * n :]
    step = pl.program_id(0)
    blocks = [(b, slice(b * slots, (b + 1) * slots)) for b in range(n * each)]

    @pl.when(step == 0)
    def _():
        for b, here in blocks:
            end = (b % each + 1) * slots
            gate = read_spare(c_refs[b // each][end - 16 : end].astype(F32)[8:], slots)
            gate_ref[here] = jnp.broadcast_to(gate, (slots, 128))
            dy_ref[here] = (gate * g_refs[b][0].astype(F32)).astype(BF16)

    c = c_refs[0][...] if n == 1 else jnp.concatenate([ref[...] for ref in c_refs], axis=0)
    active, slope = gelu_parts(dot(c, w1_ref[...]))
    active = active.astype(BF16)
    f_ref[...] = active
    dh = (slope * dot(dy_ref[...], w2_ref[...], 1, 1)).astype(BF16)
    dh_ref[...] = dh
    y = dot(active, w2_ref[...])
    dc = dot(dh, w1_ref[...], 1, 1)

    @pl.when(step == 0)
    def _():
        y_ref[...] = y
        dc_ref[...] = dc

    @pl.when(step > 0)
    def _():
        y_ref[...] += y
        dc_ref[...] += dc

    @pl.when(step == pl.num_programs(0) - 1)
    def _():
        for b, here in blocks:
            there = slice(b % each * slots, (b % each + 1) * slots)
            rounded = y_ref[here].astype(BF16).astype(F32)
            dgate = jnp.sum(g_refs[b][0].astype(F32) * rounded, axis=1, keepdims=True)
            z_refs[b // each][there] = (gate_ref[here, 0:1] * rounded).astype(BF16)
            rows = jnp.concatenate([dc_ref[here][: slots - 8], write_spare(slots, dgate)], axis=0)
            dc_refs[b // each][there] = rows.astype(BF16)


def expert_grads_kernel(n, pos_ref, *refs):
    m = len(refs) - 2 - 3 * n
    c_refs = refs[:m]
    f_refs, dh_refs, dy_refs = refs[m : m + n], refs[m + n : m + 2 * n], refs[m + 2 * n : m + 3 * n]
    send_ref, keep_ref = refs[m + 3 * n :]
    per = m // n
    for target, half in ((send_ref, 1 - (pos_ref[0] & 1)), (keep_ref, pos_ref[0] & 1)):
        at = pl.ds(pl.multiple_of(half * 256, 256), 256)
        total1 = total2 = None
        for i in range(n):
            c = [ref[:, at] for ref in c_refs[i * per : (i + 1) * per]]
            c = c[0] if per == 1 else jnp.concatenate(c, axis=0)
            part1 = dot(c, dh_refs[i][...], 0, 0)
            part2 = dot(f_refs[i][...], dy_refs[i][:, at], 0, 0)
            total1 = part1 if total1 is None else total1 + part1
            total2 = part2 if total2 is None else total2 + part2
        target[0:256] = total1.astype(BF16)
        for block in range(total2.shape[0] // 256):
            rows = slice(block * 256, (block + 1) * 256)
            target[256:512, rows] = total2[rows].astype(BF16)


def cut_kernel(a_ref, b_ref, *outs):
    row = 0
    for out in outs:
        rows = slice(row, row + out.shape[0])
        out[...] = (a_ref[rows].astype(F32) + b_ref[rows].astype(F32)).astype(BF16)
        row += out.shape[0]


def glue_kernel(*refs):
    n, row = (len(refs) - 1) // 2, 0
    for a_ref, b_ref in zip(refs[:n], refs[n : 2 * n]):
        refs[-1][row : row + a_ref.shape[0]] = (a_ref[...].astype(F32) + b_ref[...].astype(F32)).astype(BF16)
        row += a_ref.shape[0]


def join_rows_kernel(pos_ref, own_ref, other_ref, out_ref):
    core = pos_ref[0] & 1
    for mine, ref in ((core, own_ref), (1 - core, other_ref)):
        out_ref[pl.ds(pl.multiple_of(mine * 256, 256), 256)] = ref[...].astype(F32)


def join_columns_kernel(pos_ref, own_ref, other_ref, out_ref):
    core = pos_ref[0] & 1
    for mine, ref in ((core, own_ref), (1 - core, other_ref)):
        at = pl.ds(pl.multiple_of(mine * 256, 256), 256)
        for block in range(FF // 256):
            rows = slice(block * 256, (block + 1) * 256)
            out_ref[rows, at] = ref[:, rows].astype(F32)


def arrange_kernel(pos_ref, *refs):
    for k, ref in enumerate(refs[:-1]):
        refs[-1][pos_ref[1] ^ k] = ref[...]


def one_hot_columns(index_ref, width):
    place = lax.broadcasted_iota(jnp.int32, (index_ref.shape[0], width), 1)
    hit = (place == index_ref[:, 0:1]) | (place == index_ref[:, 1:2])
    return jnp.where(hit, 1.0, 0.0).astype(BF16)


def combine_kernel(
    slots, pos_ref, x_ref, gain_ref, router_ref, ids_ref, index_ref, turned_ref, c_ref, gate_ref, cot_ref, *refs
):
    blocks, (dx_ref, dgain_ref, drouter_ref) = refs[:-3], refs[-3:]
    each = blocks[0].shape[0] // slots
    experts = len(blocks) * each
    tokens = x_ref.shape[0]
    dgates = [jnp.zeros((1, tokens), F32) for _ in range(TOP)]
    gc = None
    for k in range(experts):
        at = k % each * slots
        block = blocks[k // each][at : at + slots]
        start = (pos_ref[1] ^ k) * slots
        place = lax.broadcasted_iota(jnp.int32, (tokens, slots), 1) + start
        hit = (place == turned_ref[:, 0:1]) | (place == turned_ref[:, 1:2])
        part = dot(jnp.where(hit, 1.0, 0.0).astype(BF16), block)
        gc = part if gc is None else gc + part
        place = lax.broadcasted_iota(jnp.int32, (slots, tokens), 0) + start
        column = read_spare(block[slots - 16 :].astype(F32)[8:], slots)
        for j in range(TOP):
            hit = place == index_ref[j : j + 1, :]
            dgates[j] = dgates[j] + jnp.sum(jnp.where(hit, column, 0.0), axis=0, keepdims=True)
    dl = gate_ref[0:1] * gate_ref[1:2] * (dgates[0] - dgates[1])
    expert = lax.broadcasted_iota(jnp.int32, (experts, tokens), 0)
    dlogits = jnp.where(ids_ref[0:1, :] == expert, dl, 0.0) - jnp.where(ids_ref[1:2, :] == expert, dl, 0.0)
    dlogits = dlogits.astype(BF16)
    gc = gc + dot(dlogits, router_ref[...].astype(BF16), 0, 0)
    drouter_ref[...] = dot(dlogits, c_ref[...])
    unit, scale = unit_rows(x_ref[...])
    dx, dgain = norm_backward(unit, scale, gain_ref[...], gc)
    dx_ref[...] = cot_ref[...].astype(F32) + dx
    dgain_ref[...] = dgain


def split_cube_kernel(n, pos_ref, *refs):
    kept, came, out_ref = refs[0:n], refs[n : 2 * n], refs[2 * n]
    for place in range(2):
        for half in range(2):
            x = (pos_ref[1] & 1) ^ (1 - half)
            y = (pos_ref[0] >> 1) ^ (1 - place)
            row = 0
            for keep, new in zip(kept, came):
                total = (keep[place, half].astype(F32) + new[place, half].astype(F32)).astype(BF16)
                for start in range(0, keep.shape[2], 64):
                    for depth in range(2):
                        at = start + depth * STRIP
                        out_ref[depth * 4 + x * 2 + y, row : row + STRIP] = total[at : at + STRIP]
                    row += STRIP


def sum_cube_kernel(a_ref, out_ref):
    total = a_ref[0].astype(F32)
    for k in range(1, a_ref.shape[0]):
        total = total + a_ref[k].astype(F32)
    out_ref[...] = total.astype(BF16)


def sum_kernel(*refs):
    total = refs[0][...].astype(F32)
    for ref in refs[1:-1]:
        total = total + ref[...].astype(F32)
    refs[-1][...] = total.astype(BF16)


def rows_of(pos_ref, k):
    source = pos_ref[1] ^ k
    return pl.ds(pl.multiple_of((source & 1) * 64 + (source >> 1 & 1) * STRIP, STRIP), STRIP)


def finish_mlp_kernel(pos_ref, *refs):
    mlp1_ref, mlp2_ref = refs[4:]
    for k in range(4):
        there = rows_of(pos_ref, k)
        mlp1_ref[there] = refs[k][STRIP : 2 * STRIP].astype(F32)
        for part in range(4):
            mlp2_ref[part, there] = refs[k][2 * STRIP :, part * 512 : (part + 1) * 512].astype(F32)


def finish_attention_kernel(pos_ref, *refs):
    in_ref, out_ref, small_ref = refs[8:]
    for k in range(4):
        there = rows_of(pos_ref, k)
        for layer, ref in ((0, refs[k]), (1, refs[4 + k])):
            in_ref[layer, there] = ref[0:STRIP, 0 : 3 * D].astype(F32)
            out_ref[layer, there] = ref[0:STRIP, 3 * D : 4 * D].astype(F32)
    for group in range(small_ref.shape[0] // STRIP):
        at = 4 * D + group * 128
        small_ref[group * STRIP : (group + 1) * STRIP] = refs[0][:, at : at + 128].astype(F32)


def final_kernel(blocks_ref, x_ref, turned_ref, out_ref):
    out_ref[...] = (x_ref[...] + dot(one_hot_columns(turned_ref, blocks_ref.shape[0]), blocks_ref[...])).astype(BF16)


def spent(us):
    return pl.CostEstimate(flops=int(us * 1.0e9), bytes_accessed=0, transcendentals=0)


def call(kernel, outs, *args, us=1.0, scratch=(), specs=None, room=40, **more):
    return list(
        pl.pallas_call(
        kernel,
        out_shape=[(pltpu.HBM if rest else jax.ShapeDtypeStruct)(shape, kind) for shape, kind, *rest in outs],
        in_specs=specs if specs is not None else [WHOLE] * len(args),
        out_specs=[WHOLE] * len(outs),
        scratch_shapes=list(scratch),
        cost_estimate=spent(us),
        compiler_params=pltpu.CompilerParams(vmem_limit_bytes=room * 1024 * 1024),
        **more,
        )(*args)
    )


WHOLE = pl.BlockSpec(memory_space=pltpu.VMEM)
SCALAR = pl.BlockSpec(memory_space=pltpu.SMEM)
AWAY = pl.BlockSpec(memory_space=pltpu.HBM)


def flip(array, axis, bit):
    return lax.ppermute(array, axis, [(i, i ^ bit) for i in range(lax.axis_size(axis))])


def gather_pieces(piece, across=None):
    across = flip(piece, "wshard", 2) if across is None else across
    return (piece, flip(piece, "wshard", 1), across, flip(across, "wshard", 1))


def after(array, *others):
    return lax.optimization_barrier((array, *others))[0]


def split_cube(pos, bundle):
    came = [flip(send, "wshard", 1) for send, _ in bundle]
    tall = sum(keep.shape[2] for _, keep in bundle)
    wide = bundle[0][0].shape[-1]
    return call(
        functools.partial(split_cube_kernel, len(bundle)),
        [((8, tall // 2, wide), BF16, AWAY)],
        pos,
        *[keep for _, keep in bundle],
        *came,
        specs=[SCALAR] + [WHOLE] * (2 * len(bundle)),
        us=3.0,
    )[0]


def trade_cube(blocks):
    inner = lax.axis_size("wshard")
    groups = [
        [((2 * z + depth) * 2 + x) * inner + y * 2 + core for depth in range(2) for x in range(2) for y in range(2)]
        for z in range(lax.axis_size("expert") // 4)
        for core in range(2)
    ]
    return lax.all_to_all(blocks, ("expert", "wshard"), 0, 0, axis_index_groups=groups, tiled=True)


def sum_cube(blocks):
    return call(sum_cube_kernel, [(blocks.shape[1:], BF16, AWAY)], blocks, us=2.0)[0]


def sum_two(strip, other):
    return call(sum_kernel, [(strip.shape, BF16, AWAY)], strip, other)[0]


def spread(strip):
    return [strip] + [flip(strip, "expert", k) for k in range(1, 4)]


def sum_plainly(send, keep):
    half = (keep.astype(F32) + flip(send, "wshard", 1).astype(F32)).astype(BF16)
    rows = half[1].astype(F32) + flip(half[0], "wshard", 2).astype(F32)
    return lax.psum(jnp.concatenate([rows[1], rows[0]], axis=0), "expert")


def expand(rows, images):
    return jnp.pad(rows.reshape(images, SEQ, -1), ((0, 0), (0, PAD - SEQ), (0, 0))).reshape(images * PAD, -1)


def contract(rows, images):
    return rows.reshape(images, PAD, -1)[:, :SEQ].reshape(images * SEQ, -1)


def local(
    images, attn_in, attn_out, norm_gains, mlp_in, mlp_out, router, expert_in, expert_out, expert_ids, cotangent
):
    owners = lax.axis_size("expert")
    experts = owners * expert_in.shape[0]
    tokens = images.shape[0]
    pictures = tokens // SEQ
    rows = pictures * PAD
    capacity = max(2, 2 * TOP * tokens // experts)
    slots = (capacity + 8 + 15) // 16 * 16
    every = experts * slots
    linked = owners == LINKED
    own = lax.axis_index("expert") if linked else 0
    pos = jnp.stack([lax.axis_index("wshard"), own]).astype(jnp.int32)

    small = jnp.concatenate([norm_gains, router.T], axis=0)
    small = jnp.pad(small, ((0, -small.shape[0] % 16), (0, 0)))
    (small_full,) = call(
        small_kernel, [((small.shape[0], D), F32)], pos, *gather_pieces(small), specs=[SCALAR] + [WHOLE] * 4
    )
    gains = [small_full[i : i + 1] for i in range(4)]
    router_full = small_full[4 : 4 + experts]

    wi0 = flip(attn_in[0], "wshard", 2)
    wo0 = flip(attn_out[0], "wshard", 2)
    w1_across = flip(after(mlp_in, wi0), "wshard", 2)
    w2_across = flip(after(mlp_out, wi0), "wshard", 2)
    wi1 = flip(after(attn_in[1], w1_across), "wshard", 2)
    wo1 = flip(after(attn_out[1], w1_across), "wshard", 2)
    wi = [gather_pieces(attn_in[0], wi0), None]
    wo = [gather_pieces(attn_out[0], wo0), None]
    x0 = expand(images, pictures)

    weight_specs = [AWAY] * 8
    attn_scratch = [pltpu.VMEM((4, D // 4, 3 * D), BF16), pltpu.VMEM((4, D // 4, D), BF16)]
    mlp_scratch = [pltpu.VMEM((4, D // 4, FF), BF16), pltpu.VMEM((4, FF // 4, D), BF16)]
    sems = pltpu.SemaphoreType.DMA((8,))

    def attend(x, layer):
        return call(
            attend_forward_kernel,
            [((rows, D), F32), ((rows, 3 * D), BF16), ((rows, D), BF16)],
            pos, x, gains[2 * layer], *wi[layer], *wo[layer],
            specs=[SCALAR, WHOLE, WHOLE] + weight_specs,
            scratch=attn_scratch + [sems],
            us=7.0,
        )

    def attend_back(x, layer, packed, o, dz, extra):
        wide = 4 * D
        if extra:
            wide += (sum(a.shape[0] for a in extra) + 1 + STRIP - 1) // STRIP * 128
        return call(
            functools.partial(attend_backward_kernel, len(extra)),
            [((rows, D), F32), ((1, D), F32), ((2, 2, 64, wide), BF16, AWAY), ((2, 2, 64, wide), BF16, AWAY)],
            pos, x, gains[2 * layer], packed, o, dz, *wi[layer], *wo[layer], *extra,
            specs=[SCALAR] + [WHOLE] * 5 + weight_specs + [WHOLE] * len(extra),
            scratch=attn_scratch
            + [pltpu.VMEM((rows, 3 * D), BF16)]
            + [pltpu.VMEM((rows, D), BF16)] * 3
            + [sems],
            us=12.5,
            room=58,
        )

    x1, packed1, o1 = attend(x0, 0)
    ids = jnp.pad(after(expert_ids, x1).T.reshape(TOP, pictures, SEQ), ((0, 8 - TOP), (0, 0), (0, PAD - SEQ)), constant_values=-1)
    ids = ids.reshape(8, rows)
    cot = expand(after(cotangent, x1), pictures)

    index, g_out = call(
        functools.partial(routing_kernel, slots), [((8, rows), jnp.int32), ((every, D), BF16)], ids, cot, us=3.4
    )
    turned = index.T
    trade = functools.partial(lax.all_to_all, axis_name="expert", split_axis=0, concat_axis=0, tiled=True)
    g_in = trade(g_out.reshape(experts, slots, D))

    w1 = gather_pieces(mlp_in, after(w1_across, x1))
    w2 = gather_pieces(mlp_out, after(w2_across, x1))
    (x2,) = call(
        feed_forward_kernel, [((rows, D), F32)], pos, x1, gains[1], *w1, *w2,
        specs=[SCALAR, WHOLE, WHOLE] + weight_specs, scratch=mlp_scratch + [sems], us=6.5,
    )
    wi[1] = gather_pieces(attn_in[1], after(wi1, x2))
    wo[1] = gather_pieces(attn_out[1], after(wo1, x2))
    x3, packed2, o2 = attend(x2, 1)
    arrays = experts if linked else max(1, experts // (2 * PAD // slots))
    each = experts // arrays
    c, gate, *c_out = call(
        functools.partial(dispatch_kernel, slots),
        [((rows, D), BF16), ((8, rows), F32)] + [((each * slots, D), BF16, AWAY)] * arrays,
        pos, x3, gains[3], router_full, ids, index,
        specs=[SCALAR] + [WHOLE] * 5,
        us=4.6,
    )

    def swap(blocks, first=0):
        if linked:
            return [flip(block, "expert", k) if k else block for k, block in enumerate(blocks, first)]
        moved = trade(jnp.concatenate(blocks).reshape(experts, slots, D))
        return list(moved.reshape(arrays, each * slots, D))

    c_in = swap(c_out)
    per = 2 if linked else 1
    work = []
    dc_out, z_out, dc_in = [], [], []
    for first in range(0, arrays, per):
        given = c_in[first : first + per]
        if linked and first >= 2 * per:
            given[0], *dc_in[-2 * per : -per] = lax.optimization_barrier((given[0], *dc_in[-2 * per : -per]))
        count = list(range(first * each, (first + per) * each))
        tall = len(count) * slots
        fixed = lambda *shape: pl.BlockSpec(shape, lambda j, pos_ref: (0,) * len(shape))
        source = lambda k: pl.BlockSpec((1, slots, D), lambda j, pos_ref: (pos_ref[1] ^ k, 0, 0))
        across = lambda height: pl.BlockSpec((height, 1024), lambda j, pos_ref: (0, j))
        *made, f, dh, dy = pl.pallas_call(
            functools.partial(experts_kernel, slots, per, each),
            out_shape=[pltpu.HBM((each * slots, D), BF16)] * (2 * per)
            + [pltpu.HBM((tall, FF), BF16)] * 2
            + [pltpu.HBM((tall, D), BF16)],
            grid_spec=pltpu.PrefetchScalarGridSpec(
                num_scalar_prefetch=1,
                grid=(FF // 1024,),
                in_specs=[across(D), pl.BlockSpec((1024, D), lambda j, pos_ref: (j, 0))]
                + [source(k) for k in count]
                + [fixed(each * slots, D)] * per,
                out_specs=[fixed(each * slots, D)] * (2 * per) + [across(tall)] * 2 + [fixed(tall, D)],
                scratch_shapes=[pltpu.VMEM((tall, 128), F32), pltpu.VMEM((tall, D), F32), pltpu.VMEM((tall, D), F32)],
            ),
            cost_estimate=spent(8.0),
            compiler_params=pltpu.CompilerParams(vmem_limit_bytes=VMEM_LIMIT if first else 58 * 1024 * 1024),
        )(pos, expert_in[0], expert_out[0], *[g_in] * len(count), *given)
        dc_out += made[:per]
        z_out += made[per:]
        if linked:
            dc_in += swap(made[:per], first)
        work.append((f, dh, dy))
    if not linked:
        dc_in = swap(dc_out)
    if linked:
        (z_block,) = call(
            arrange_kernel, [((experts, slots, D), BF16, AWAY)], pos, *z_out, specs=[SCALAR] + [WHOLE] * experts, us=2.0
        )
    else:
        z_block = jnp.concatenate(z_out).reshape(experts, slots, D)
    n = len(work)
    whole_rows = lambda a: pl.BlockSpec(a.shape, lambda j: (0, 0))
    chunk = lambda a: pl.BlockSpec((a.shape[0], 1024), lambda j: (0, j))
    fs, dhs, dys = ([w[i] for w in work] for i in range(3))
    if linked:
        dys[0], *dc_in[per : 2 * per] = lax.optimization_barrier((dys[0], *dc_in[per : 2 * per]))
    grad_send, grad_keep = pl.pallas_call(
        functools.partial(expert_grads_kernel, n),
        grid=(FF // 1024,),
        in_specs=[SCALAR]
        + [whole_rows(a) for a in c_in]
        + [chunk(a) for a in fs + dhs]
        + [whole_rows(a) for a in dys],
        out_specs=[pl.BlockSpec((512, 1024), lambda j: (0, j))] * 2,
        out_shape=[pltpu.HBM((512, FF), BF16)] * 2,
        cost_estimate=spent(10.0),
        compiler_params=pltpu.CompilerParams(vmem_limit_bytes=58 * 1024 * 1024),
    )(pos, *c_in, *fs, *dhs, *dys)
    x3_late, z_block, grad_send, grad_keep = lax.optimization_barrier((x3, z_block, grad_send, grad_keep))
    g3, gain3, drouter = call(
        functools.partial(combine_kernel, slots),
        [((rows, D), F32), ((1, D), F32), ((experts, D), F32)],
        pos, x3_late, gains[3], router_full, ids, index, turned, c, gate, cot, *dc_in,
        specs=[SCALAR] + [WHOLE] * (9 + arrays),
        us=5.5,
    )
    g3, z_block, grad_send = lax.optimization_barrier((g3, z_block, grad_send))
    z_in = trade(z_block)
    grads = call(
        cut_kernel,
        [((tall, FF), BF16, AWAY) for tall in (128, 128, 256)],
        grad_keep, flip(grad_send, "wshard", 1),
        us=2.0,
    )
    g3 = after(g3, *grads)
    crossed = [flip(piece, "wshard", 2) for piece in grads[:2]]
    g2, gain2, *second = attend_back(x2, 1, packed2, o2, g3, [])
    g1, gain1, *mlp = call(
        feed_backward_kernel,
        [((rows, D), F32), ((1, D), F32)] + [((2, 2, 128, FF), BF16, AWAY)] * 2,
        pos, x1, gains[1], g2, *w1, *w2,
        specs=[SCALAR, WHOLE, WHOLE, WHOLE] + weight_specs,
        scratch=mlp_scratch + [pltpu.VMEM((D, FF), BF16), pltpu.VMEM((FF, D), BF16), sems],
        us=12.5,
        room=58,
    )
    *second, mlp[0], mlp[1], crossed[0], crossed[1] = lax.optimization_barrier(
        (*second, mlp[0], mlp[1], crossed[0], crossed[1])
    )
    if linked:
        bulk = split_cube(pos, [second, mlp])
        g1 = after(g1, z_in, bulk)
        bulk = trade_cube(bulk)
    dx, _, *first = attend_back(x0, 0, packed1, o1, g1, [gain1, gain2, gain3, drouter])
    (final,) = call(final_kernel, [((rows, D), BF16)], z_in.reshape(every, D), x3, turned, us=3.5)

    wide = first[0].shape[-1]

    def join(kernel, shape, pieces, came):
        (half,) = call(glue_kernel, [((256, FF), BF16, AWAY)], *pieces, *came)
        return call(
            kernel, [(shape, F32)], pos, half, flip(half, "wshard", 1), specs=[SCALAR] + [WHOLE] * 2, us=2.0
        )[0]

    expert1 = join(join_rows_kernel, (D, FF), [after(grads[0], dx), grads[1]], crossed)
    if linked:
        tail = split_cube(pos, [(first[0], after(first[1], final))])
        final_rows, input_grad = contract(final, pictures), contract(dx, pictures)
        bulk = sum_cube(after(bulk, tail, final_rows, input_grad))
        deep = flip(bulk, "expert", 4)
        tail = sum_cube(after(trade_cube(after(tail, bulk)), deep, expert1))
        last = flip(after(grads[2], tail), "wshard", 2)
        bulk = spread(sum_two(bulk, deep))
        tail = sum_two(tail, flip(tail, "expert", 4))
        last = after(last, tail, *bulk)
        tail = spread(tail)
        mlp1, mlp2 = call(
            finish_mlp_kernel,
            [((D // 4, FF), F32), ((4, 128, D), F32)],
            pos, after(bulk[0], tail[1]), *bulk[1:], specs=[SCALAR] + [WHOLE] * 4, us=2.0,
        )
        expert2 = join(join_columns_kernel, (FF, D), grads[2:], [last])
        tail[0] = after(tail[0], expert2)
        grad_in, grad_out, smalls = call(
            finish_attention_kernel,
            [((2, D // 4, 3 * D), F32), ((2, D // 4, D), F32), (((wide - 4 * D) // 128 * STRIP, 128), F32)],
            pos, *tail, *bulk, specs=[SCALAR] + [WHOLE] * 8, us=2.0,
        )
        mlp2 = mlp2.reshape(FF // 4, D)
    else:
        last = flip(grads[2], "wshard", 2)
        expert2 = join(join_columns_kernel, (FF, D), grads[2:], [last])
        first, second, mlp = sum_plainly(*first), sum_plainly(*second), sum_plainly(*mlp)
        grad_in = jnp.stack([first[:, : 3 * D], second[:, : 3 * D]])
        grad_out = jnp.stack([first[:, 3 * D : 4 * D], second[:, 3 * D :]])
        smalls = first[:STRIP, 4 * D :].reshape(STRIP, -1, 128).transpose(1, 0, 2).reshape(-1, 128)
        mlp1 = jnp.concatenate([mlp[0:64], mlp[128:192]], axis=0)
        final_rows, input_grad = contract(final, pictures), contract(dx, pictures)
        mlp2 = jnp.stack([mlp[64:128], mlp[192:256]]).reshape(2, 64, 4, D).transpose(2, 0, 1, 3).reshape(FF // 4, D)

    return (
        final_rows,
        input_grad,
        grad_in,
        grad_out,
        smalls[0:4],
        mlp1,
        mlp2,
        smalls[4 : 4 + experts].T,
        expert1[None],
        expert2[None],
    )


def solution(mesh):
    rows = P(("expert", "wshard"), None)
    dense = (P(None, "wshard", None), P(None, "wshard", None), P(None, "wshard"))
    shards = (P("wshard", None),) * 3
    experts = (P("expert", None, None),) * 2
    return jax.shard_map(
        local,
        mesh=mesh,
        in_specs=(rows, *dense, *shards, *experts, rows, rows),
        out_specs=(rows, rows, *dense, *shards, *experts),
        check_vma=False,
    )
```
